128 devices in a mesh: fsdp: 16 (over y, x), tp: 8 (over z, core).
Axes of the slice: x: 4, y: 4, z: 4, core: 2. Of those that a mesh axis runs over, the one named last changes fastest.
Arguments:
- momentum: bfloat16 [8192, 28672], P('fsdp', 'tp'), may hold values from -300 to 300
- gradient: bfloat16 [8192, 28672], P('fsdp', 'tp'), may hold values from -300 to 300
- seed_value: int32 [1], replicated, may hold values from 0 to 999999
Outputs:
- new_momentum: bfloat16 [8192, 28672], P('fsdp', 'tp')
- update: bfloat16 [8192, 28672], P('fsdp', 'tp')
The draws below stay inside these ranges and needn't reach their ends.
All inputs are finite; a program needn't handle non-finite values.
Results may differ from the reference program's by a relative error of at most 0.012.
Values may be sent and summed in bfloat16 or wider, within the bound.
No kernel may reach another device: no remote copies, remote signals or barrier semaphores. Data moves between devices by JAX's collectives and lax.ppermute only.
A program may use at most 128 MiB of HBM per device.

```python
import math
import jax
import jax.numpy as jnp
from jax import lax

D = 8192
F = 28672
RANK = 512


def scale_grid(key, top):
    key_rows, key_cols = jax.random.split(key)
    row_scale = jnp.exp(jax.random.uniform(key_rows, (D, 1), minval=0.0, maxval=math.log(top)))
    ramp = 3.0 ** (jnp.arange(F, dtype=jnp.float32) / F)
    col_scale = jnp.exp(jax.random.uniform(key_cols, (1, F), minval=0.0, maxval=math.log(top))) * ramp[None, :]
    return row_scale * col_scale


def draw_momentum(key, part):
    key = jax.random.fold_in(key, 5)
    key_base = jax.random.fold_in(key, 0)
    key_grid = jax.random.fold_in(key, 2)
    base = jnp.clip(jax.random.normal(key_base, (D, F)), -5.0, 5.0)
    grid = scale_grid(key_grid, 10.0)
    return jnp.clip(0.1 * base * grid, -300.0, 300.0).astype(jnp.bfloat16)


def draw_gradient(key, part):
    key = jax.random.fold_in(key, 7)
    key_base = jax.random.fold_in(key, 0)
    key_grid = jax.random.fold_in(key, 2)
    base = jnp.clip(jax.random.normal(key_base, (D, F)), -5.0, 5.0)
    grid = scale_grid(key_grid, 10.0)
    return jnp.clip(0.1 * base * grid, -300.0, 300.0).astype(jnp.bfloat16)


def setup_inputs(seed: int = 0) -> dict:
    seeds = jax.random.split(jax.random.key(seed), 4)
    momentum = draw_momentum(jax.random.fold_in(seeds[3], 71), 0)
    gradient = draw_gradient(jax.random.fold_in(seeds[3], 71), 0)
    seed_value = jax.random.randint(seeds[2], (1,), 0, 1000000).astype(jnp.int32)
    return dict(momentum=momentum, gradient=gradient, seed_value=seed_value)


def start_factor(seed_value, first_row, row_count):
    row_ids = (first_row + jnp.arange(row_count, dtype=jnp.int32))[:, None]
    col_ids = jnp.arange(RANK, dtype=jnp.int32)[None, :]
    hashed = (row_ids * 40503 + col_ids * 9973 + seed_value[0]) % 65521
    second = (hashed % 32768 * (hashed % 32768) + 7) % 65521
    third = (second % 32768 * (second % 32768) + hashed) % 65521
    uniform_part = third.astype(jnp.float32) / 65521.0 - 0.5
    return (uniform_part * math.sqrt(12.0 / F)).astype(jnp.bfloat16)

def reference(momentum, gradient, seed_value):
    blended = (momentum.astype(jnp.float32) + gradient.astype(jnp.float32)).astype(jnp.bfloat16)
    start_rows = start_factor(seed_value, 0, F)
    projected = jnp.dot(blended.astype(jnp.float32), start_rows.astype(jnp.float32), preferred_element_type=jnp.float32)
    gram = jnp.dot(projected.T, projected, precision=lax.Precision.HIGHEST)
    lower_factor = jnp.linalg.cholesky(gram)
    ortho_left = jax.scipy.linalg.solve_triangular(lower_factor, projected.T, lower=True).T.astype(jnp.bfloat16)
    right_factor = lax.dot_general(blended.astype(jnp.float32), ortho_left.astype(jnp.float32), (((0,), (0,)), ((), ())), preferred_element_type=jnp.float32)
    square_sums = lax.optimization_barrier(jnp.sum(right_factor * right_factor, axis=0))
    next_factor = (right_factor * lax.rsqrt(square_sums + 1e-06)[None, :]).astype(jnp.bfloat16)
    right_rounded = right_factor.astype(jnp.bfloat16)
    feedback = lax.dot_general(ortho_left.astype(jnp.float32), right_rounded.astype(jnp.float32), (((1,), (1,)), ((), ())), preferred_element_type=jnp.float32)
    new_momentum = (blended.astype(jnp.float32) - 0.05 * feedback).astype(jnp.bfloat16)
    direction = lax.dot_general(ortho_left.astype(jnp.float32), next_factor.astype(jnp.float32), (((1,), (1,)), ((), ())), preferred_element_type=jnp.float32)
    update = (math.sqrt(D * F / RANK) * direction).astype(jnp.bfloat16)
    return (new_momentum, update)
```

```python
import functools
import math

import jax
import jax.numpy as jnp
from jax import lax
from jax.experimental import pallas as pl
from jax.experimental.pallas import tpu as pltpu
from jax.sharding import PartitionSpec as P

D = 8192
F = 28672
RANK = 512
HALF = RANK // 2
PRIME = 65521
NB = 128
PANEL = 16
VMEM_LIMIT = 48 * 1024 * 1024
F32, BF16 = jnp.float32, jnp.bfloat16
AXES = ("fsdp", "tp")
WIRE = jnp.float32


def flat(y, x, z, core):
    return (y * 4 + x) * 8 + z * 2 + core


def everyone():
    return [(y, x, z, c) for y in range(4) for x in range(4) for z in range(4) for c in range(2)]


def shift(along_first, step):
    pairs = []
    for y, x, z, c in everyone():
        if (c == 0) == along_first:
            to = (y, (x + step) % 4, z, c)
        else:
            to = ((y + step) % 4, x, z, c)
        pairs.append((flat(y, x, z, c), flat(*to)))
    return pairs


def send_first(a, step):
    return lax.ppermute(a, AXES, shift(True, step))


def send_second(a, step):
    return lax.ppermute(a, AXES, shift(False, step))


def swap_cores(a):
    return lax.ppermute(a, "tp", [(i, i ^ 1) for i in range(8)])


Z_GROUPS = [[c, 2 + c, 4 + c, 6 + c] for c in range(2)]
SECOND_GROUPS = [[flat(y, x, z, 0) for y in range(4)] for x in range(4) for z in range(4)] + [
    [flat(y, x, z, 1) for x in range(4)] for y in range(4) for z in range(4)
]
FIRST_Z_GROUPS = [[flat(y, x, z, 0) for x in range(4) for z in range(4)] for y in range(4)] + [
    [flat(y, x, z, 1) for y in range(4) for z in range(4)] for x in range(4)
]


def exchange(a, axis, groups=None):
    return lax.all_to_all(a, axis, 0, 0, axis_index_groups=groups, tiled=True)


def vmem_spec():
    return pl.BlockSpec(memory_space=pltpu.VMEM)


def smem_spec():
    return pl.BlockSpec(memory_space=pltpu.SMEM)


def params():
    return pltpu.CompilerParams(vmem_limit_bytes=VMEM_LIMIT)


def dot(a, b, ca, cb, precision=None):
    return lax.dot_general(
        a, b, (((ca,), (cb,)), ((), ())), precision=precision, preferred_element_type=F32
    )


def exact(a, b, ca, cb):
    return dot(a, b, ca, cb, lax.Precision.HIGHEST)


def fold(v):
    return (v & 65535) + 15 * (v >> 16)


def reduce_mod(v):
    v = fold(fold(v))
    return jnp.where(v >= PRIME, v - PRIME, v)


def start_rows(first_row, count, seed):
    rows = first_row + lax.broadcasted_iota(jnp.int32, (count, 1), 0)
    cols = lax.broadcasted_iota(jnp.int32, (1, RANK), 1)
    hashed = reduce_mod(rows * 40503 + seed) + reduce_mod(cols * 9973)
    hashed = jnp.where(hashed >= PRIME, hashed - PRIME, hashed)
    low = hashed & 32767
    low = reduce_mod(low * low + 7) & 32767
    third = reduce_mod(low * low + hashed).astype(F32)
    scale = math.sqrt(12.0 / F)
    return (third * (scale / PRIME) - 0.5 * scale).astype(BF16)


TILE = 512


def left_kernel(meta_ref, m_ref, g_ref, b_ref, keep_ref, send_ref, acc):
    t = pl.program_id(0)
    core, tp, seed = meta_ref[0], meta_ref[1], meta_ref[2]
    b = (m_ref[...].astype(F32) + g_ref[...].astype(F32)).astype(BF16)
    b_ref[...] = b
    part = dot(b, start_rows(tp * 3584 + t * TILE, TILE, seed), 1, 0)

    @pl.when(t == 0)
    def _():
        acc[...] = part

    @pl.when(t > 0)
    def _():
        acc[...] += part

    @pl.when(t == pl.num_programs(0) - 1)
    def _():
        keep_ref[...] = acc[pl.ds(core * HALF, HALF), :]
        send_ref[...] = acc[pl.ds((1 - core) * HALF, HALF), :]


def left_partial(meta, momentum, gradient):
    rows, cols = momentum.shape
    half = jax.ShapeDtypeStruct((HALF, RANK), F32)
    whole = pl.BlockSpec((HALF, RANK), lambda t: (0, 0))
    tile = pl.BlockSpec((rows, TILE), lambda t: (0, t))
    return pl.pallas_call(
        left_kernel,
        grid=(cols // TILE,),
        out_shape=(jax.ShapeDtypeStruct((rows, cols), BF16), half, half),
        in_specs=[smem_spec(), tile, tile],
        out_specs=(tile, whole, whole),
        scratch_shapes=[pltpu.VMEM((rows, RANK), F32)],
        compiler_params=params(),
        name="left_partial",
    )(meta, momentum, gradient)


def gram_kernel(meta_ref, mine_ref, other_ref, out_ref):
    cols = pl.ds(pl.multiple_of(meta_ref[0] * HALF, HALF), HALF)
    out_ref[...] = exact(mine_ref[...], mine_ref[:, cols], 0, 0) + exact(
        other_ref[...], other_ref[:, cols], 0, 0
    )


def gram_half(meta, mine, other):
    return pl.pallas_call(
        gram_kernel,
        out_shape=jax.ShapeDtypeStruct((RANK, HALF), F32),
        in_specs=[smem_spec(), vmem_spec(), vmem_spec()],
        out_specs=vmem_spec(),
        compiler_params=params(),
        name="gram_half",
    )(meta, mine, other)


def right_kernel(offsets, meta_ref, b_ref, mine_ref, other_ref, *rest):
    outs, (hi, lo) = rest[:-2], rest[-2:]
    r = pl.program_id(0)

    @pl.when(r == 0)
    def _():
        core = meta_ref[0]
        for ref, place in ((mine_ref, core), (other_ref, 1 - core)):
            rows = pl.ds(pl.multiple_of(place * HALF, HALF), HALF)
            top = ref[...].astype(BF16)
            hi[rows, :] = top
            lo[rows, :] = (ref[...] - top.astype(F32)).astype(BF16)

    w = dot(b_ref[...], hi[...], 0, 0) + dot(b_ref[...], lo[...], 0, 0)
    w = w.astype(WIRE)
    for k in range(len(offsets)):

        @pl.when(r == k)
        def _():
            outs[2 * k][...] = w[:, :HALF]
            outs[2 * k + 1][...] = w[:, HALF:]


def right_partial(meta, blended, mine, other, offsets):
    rows, cols = blended.shape
    block = cols // 4
    n = len(offsets)

    def place(r, meta_ref):
        off = offsets[0]
        for k in range(1, n):
            off = jnp.where(r == k, offsets[k], off)
        return (0, (meta_ref[3] + off) % 4)

    whole = pl.BlockSpec((HALF, RANK), lambda r, meta_ref: (0, 0))
    out = pl.BlockSpec((block, HALF), lambda r, meta_ref: (0, 0))
    return pl.pallas_call(
        functools.partial(right_kernel, offsets),
        grid_spec=pltpu.PrefetchScalarGridSpec(
            num_scalar_prefetch=1,
            grid=(n,),
            in_specs=[pl.BlockSpec((rows, block), place), whole, whole],
            out_specs=[out] * (2 * n),
            scratch_shapes=[pltpu.VMEM((RANK, RANK), BF16)] * 2,
        ),
        out_shape=[jax.ShapeDtypeStruct((block, HALF), WIRE)] * (2 * n),
        compiler_params=params(),
        name="right_partial",
    )(meta, blended, mine, other)


def add_kernel(a_ref, b_ref, c_ref, d_ref, x_ref, y_ref):
    x_ref[...] = (a_ref[...].astype(F32) + b_ref[...].astype(F32)).astype(x_ref.dtype)
    y_ref[...] = (c_ref[...].astype(F32) + d_ref[...].astype(F32)).astype(y_ref.dtype)


def add_pairs(a, b, c, d):
    shape = jax.ShapeDtypeStruct(a.shape, a.dtype)
    return pl.pallas_call(
        add_kernel,
        out_shape=(shape, shape),
        in_specs=[vmem_spec()] * 4,
        out_specs=(vmem_spec(),) * 2,
        compiler_params=params(),
        name="add_pairs",
    )(a, b, c, d)


def split_kernel(meta_ref, *refs):
    ins, outs = refs[:6], refs[6:]
    quarter = ins[0].shape[0] // 4
    for k, off in enumerate((2, 1, 3, 0)):
        rows = pl.ds(pl.multiple_of((meta_ref[4] + off) % 4 * quarter, quarter), quarter)
        for h in range(2):
            total = sum(ref[rows, :].astype(F32) for ref in ins[3 * h : 3 * h + 3])
            outs[2 * k + h][...] = total.astype(outs[2 * k + h].dtype)


def add_and_split(meta, terms):
    rows = terms[0].shape[0] // 4
    return pl.pallas_call(
        split_kernel,
        out_shape=[jax.ShapeDtypeStruct((rows, HALF), WIRE)] * 8,
        in_specs=[smem_spec()] + [vmem_spec()] * 6,
        out_specs=[vmem_spec()] * 8,
        compiler_params=params(),
        name="add_and_split",
    )(meta, *terms)


def invert_block(ae):
    rows = lax.broadcasted_iota(jnp.int32, (PANEL, NB), 0)
    for k0 in range(0, NB, PANEL):
        left = ae[k0 : k0 + PANEL, :NB]
        right = ae[k0 : k0 + PANEL, NB:]
        columns = [
            jnp.broadcast_to(left[:, k0 + c : k0 + c + 1], (PANEL, NB)) for c in range(PANEL)
        ]
        pivots = jnp.zeros((PANEL, NB), F32)
        for k in range(PANEL):
            pivot = columns[k][k : k + 1, :]
            pivots = jnp.where(rows == k, pivot, pivots)
            if k < PANEL - 1:
                factor = jnp.where(rows > k, columns[k] * (1.0 / pivot), 0.0)
                for c in range(k + 1, PANEL):
                    columns[c] = columns[c] - factor * columns[c][k : k + 1, :]
                left = left - factor * left[k : k + 1, :]
                right = right - factor * right[k : k + 1, :]
        scale = lax.rsqrt(pivots)
        left, right = left * scale, right * scale
        ae[k0 : k0 + PANEL, NB:] = right
        below = k0 + PANEL
        if below < NB:
            ae[below:, :NB] = ae[below:, :NB] - exact(left, left, 0, 0)[below:]
            ae[below:, NB:] = ae[below:, NB:] - exact(left, right, 0, 0)[below:]


def inverse_kernel(meta_ref, mine_ref, other_ref, out_ref, a, ae):
    core = meta_ref[0]
    a[:, pl.ds(pl.multiple_of(core * HALF, HALF), HALF)] = mine_ref[...]
    a[:, pl.ds(pl.multiple_of((1 - core) * HALF, HALF), HALF)] = other_ref[...]
    big = lambda d: lax.broadcasted_iota(jnp.int32, (RANK, RANK), d)
    small = lambda d: lax.broadcasted_iota(jnp.int32, (NB, NB), d)
    out_ref[...] = jnp.where(big(0) == big(1), 1.0, 0.0)
    for lo in range(0, RANK, NB):
        hi = lo + NB
        ae[:, :NB] = a[lo:hi, lo:hi]
        ae[:, NB:] = jnp.where(small(0) == small(1), 1.0, 0.0)
        invert_block(ae)
        inverse = jnp.where(small(0) >= small(1), ae[:, NB:], 0.0)
        done = exact(inverse, out_ref[lo:hi, :hi], 1, 0)
        out_ref[lo:hi, :hi] = done
        if hi < RANK:
            below = exact(a[hi:, lo:hi], inverse, 1, 1)
            a[hi:, hi:] = a[hi:, hi:] - exact(below, below, 1, 1)
            out_ref[hi:, :hi] = out_ref[hi:, :hi] - exact(below, done, 1, 0)


def inverse_factor(meta, mine, other):
    return pl.pallas_call(
        inverse_kernel,
        out_shape=jax.ShapeDtypeStruct((RANK, RANK), F32),
        in_specs=[smem_spec(), vmem_spec(), vmem_spec()],
        out_specs=vmem_spec(),
        scratch_shapes=[pltpu.VMEM((RANK, RANK), F32), pltpu.VMEM((NB, 2 * NB), F32)],
        compiler_params=params(),
        name="inverse_factor",
    )(meta, mine, other)


def solve_kernel(a0, a1, a2, b0, b1, b2, inv_ref, out_ref):
    left = a0[...].astype(F32) + a1[...].astype(F32) + a2[...].astype(F32)
    right = b0[...].astype(F32) + b1[...].astype(F32) + b2[...].astype(F32)
    out_ref[...] = (
        exact(left, inv_ref[:, :HALF], 1, 1) + exact(right, inv_ref[:, HALF:], 1, 1)
    ).astype(BF16)


def solve_rows(terms, inverse):
    return pl.pallas_call(
        solve_kernel,
        out_shape=jax.ShapeDtypeStruct((terms[0].shape[0], RANK), BF16),
        in_specs=[vmem_spec()] * 7,
        out_specs=vmem_spec(),
        compiler_params=params(),
        name="solve_rows",
    )(*terms, inverse)


def ortho_kernel(meta_ref, mine_ref, other_ref, inv_ref, out_ref):
    core = meta_ref[0]
    for ref, place in ((mine_ref, core), (other_ref, 1 - core)):
        rows = pl.ds(pl.multiple_of(place * HALF, HALF), HALF)
        out_ref[rows, :] = exact(ref[...], inv_ref[...], 1, 1).astype(BF16)


def ortho_left(meta, mine, other, inverse):
    return pl.pallas_call(
        ortho_kernel,
        out_shape=jax.ShapeDtypeStruct((RANK, RANK), BF16),
        in_specs=[smem_spec()] + [vmem_spec()] * 3,
        out_specs=vmem_spec(),
        compiler_params=params(),
        name="ortho_left",
    )(meta, mine, other, inverse)


def apply_kernel(parts, meta_ref, b_ref, q_ref, sums_ref, *refs):
    rights, (m_ref, u_ref, scaled) = refs[:parts], refs[-3:]
    scale = lax.rsqrt(sums_ref[0:1, :] + 1e-6) * math.sqrt(D * F / RANK)
    scaled[...] = (q_ref[...].astype(F32) * scale).astype(BF16)
    width = RANK // parts
    feedback = direction = 0.0
    for k, right in enumerate(rights):
        cols = slice(k * width, (k + 1) * width)
        feedback += dot(q_ref[:, cols], right[...], 1, 1)
        direction += dot(scaled[:, cols], right[...], 1, 1)
    m_ref[...] = (b_ref[...].astype(F32) - 0.05 * feedback).astype(BF16)
    u_ref[...] = direction.astype(BF16)


def apply_block(meta, blended, q, sums, rights, offset, outs):
    rows, cols = blended.shape
    block = cols // 4
    here = pl.BlockSpec((rows, block), lambda i, meta_ref: (0, (meta_ref[3] + offset) % 4))
    whole = lambda a: pl.BlockSpec(a.shape, lambda i, meta_ref: (0, 0))
    n = len(rights)
    shape = jax.ShapeDtypeStruct((rows, cols), BF16)
    kept = [pl.BlockSpec(memory_space=pl.ANY)] * len(outs)
    return pl.pallas_call(
        functools.partial(apply_kernel, n),
        grid_spec=pltpu.PrefetchScalarGridSpec(
            num_scalar_prefetch=1,
            grid=(1,),
            in_specs=[here, whole(q), whole(sums)] + [whole(r) for r in rights] + kept,
            out_specs=[here, here],
            scratch_shapes=[pltpu.VMEM((rows, RANK), BF16)],
        ),
        out_shape=[shape, shape],
        input_output_aliases={4 + n + k: k for k in range(len(outs))},
        compiler_params=params(),
        name="apply_block",
    )(meta, blended, q, sums, *rights, *outs)


def sums_kernel(r_ref, out_ref):
    r = r_ref[...].astype(F32)
    out_ref[...] = jnp.broadcast_to(jnp.sum(r * r, axis=0, keepdims=True), out_ref.shape)


def block_sums(r):
    return pl.pallas_call(
        sums_kernel,
        out_shape=jax.ShapeDtypeStruct((16, RANK), F32),
        in_specs=[vmem_spec()],
        out_specs=vmem_spec(),
        compiler_params=params(),
        name="block_sums",
    )(r)


def per_device(momentum, gradient, seed_value):
    fsdp, tp = lax.axis_index("fsdp"), lax.axis_index("tp")
    core, x, y = tp % 2, fsdp % 4, fsdp // 4
    first, second = jnp.where(core == 0, x, y), jnp.where(core == 0, y, x)
    meta = jnp.stack([core, tp, seed_value[0], first, second]).astype(jnp.int32)

    blended, keep, send = left_partial(meta, momentum, gradient)
    half = keep + swap_cores(send)
    pieces = exchange(half, "tp", Z_GROUPS)
    piece = jnp.sum(pieces.reshape(4, HALF // 4, RANK), axis=0)
    mine = exchange(jnp.tile(piece, (4, 1)), "tp", Z_GROUPS)
    other = swap_cores(mine)

    gram = gram_half(meta, mine, other)

    far_a, far_b = right_partial(meta, blended, mine, other, (2,))
    from_low_a = send_first(far_a, 1)
    from_high_b = send_first(far_b, -1)
    next_a, next_b, prev_a, prev_b, own_a, own_b = right_partial(
        meta, blended, mine, other, (1, 3, 0)
    )
    own_b_low = send_first(next_b, 1)
    own_a_high = send_first(prev_a, -1)
    next_a, prev_b = add_pairs(next_a, from_low_a, prev_b, from_high_b)
    own_a_low = send_first(next_a, 1)
    own_b_high = send_first(prev_b, -1)
    cut = add_and_split(meta, (own_a, own_a_low, own_a_high, own_b, own_b_low, own_b_high))
    far_a, far_b, next_a, next_b, prev_a, prev_b, own_a, own_b = cut
    from_low_a = send_second(far_a, 1)
    from_high_b = send_second(far_b, -1)
    own_b_low = send_second(next_b, 1)
    own_a_high = send_second(prev_a, -1)
    next_a, prev_b = add_pairs(next_a, from_low_a, prev_b, from_high_b)
    own_a_low = send_second(next_a, 1)
    own_b_high = send_second(prev_b, -1)

    gram = exchange(gram, "fsdp")
    gram = jnp.sum(gram.reshape(16, RANK // 16, HALF), axis=0)
    gram = exchange(jnp.tile(gram, (16, 1)), "fsdp")
    inverse = inverse_factor(meta, gram, swap_cores(gram))

    block = solve_rows((own_a, own_a_low, own_a_high, own_b, own_b_low, own_b_high), inverse)
    right = exchange(jnp.tile(block, (4, 1)), AXES, SECOND_GROUPS)
    right_low = send_first(right, 1)
    right_high = send_first(right, -1)
    q = ortho_left(meta, mine, other, inverse)
    sums = exchange(block_sums(right), AXES, FIRST_Z_GROUPS)
    sums = jnp.sum(sums, axis=0, keepdims=True)
    sums = jnp.broadcast_to(sums + swap_cores(sums), (8, RANK))
    far_a = send_first(right_low[:, :HALF], 1)
    far_b = send_first(right_high[:, HALF:], -1)
    outs = apply_block(meta, blended, q, sums, [right], 0, [])
    outs = apply_block(meta, blended, q, sums, [right_low], 3, outs)
    outs = apply_block(meta, blended, q, sums, [right_high], 1, outs)
    outs = apply_block(meta, blended, q, sums, [far_a, far_b], 2, outs)
    return tuple(outs)


def solution(mesh):
    return jax.shard_map(
        per_device,
        mesh=mesh,
        in_specs=(P("fsdp", "tp"), P("fsdp", "tp"), P()),
        out_specs=(P("fsdp", "tp"), P("fsdp", "tp")),
        check_vma=False,
    )
```

```python
import functools
import math

import jax
import jax.numpy as jnp
from jax import lax
from jax.experimental import pallas as pl
from jax.experimental.pallas import tpu as pltpu
from jax.sharding import PartitionSpec as P

D = 8192
F = 28672
RANK = 512
HALF = RANK // 2
PRIME = 65521
NB = 128
PANEL = 16
VMEM_LIMIT = 48 * 1024 * 1024
VMEM_MOST = 61 * 1024 * 1024
F32, BF16 = jnp.float32, jnp.bfloat16
AXES = ("fsdp", "tp")
LOSS_MAX = 2.0


def flat(y, x, z, core):
    return (y * 4 + x) * 8 + z * 2 + core


def everyone():
    return [(y, x, z, c) for y in range(4) for x in range(4) for z in range(4) for c in range(2)]


def shift(along_first, step):
    pairs = []
    for y, x, z, c in everyone():
        if (c == 0) == along_first:
            to = (y, (x + step) % 4, z, c)
        else:
            to = ((y + step) % 4, x, z, c)
        pairs.append((flat(y, x, z, c), flat(*to)))
    return pairs


def send_first(a, step):
    return lax.ppermute(a, AXES, shift(True, step))


def send_second(a, step):
    return lax.ppermute(a, AXES, shift(False, step))


def swap_cores(a):
    return lax.ppermute(a, "tp", [(i, i ^ 1) for i in range(8)])


Z_GROUPS = [[c, 2 + c, 4 + c, 6 + c] for c in range(2)]
SECOND_GROUPS = [[flat(y, x, z, 0) for y in range(4)] for x in range(4) for z in range(4)] + [
    [flat(y, x, z, 1) for x in range(4)] for y in range(4) for z in range(4)
]
FIRST_GROUPS = [[flat(y, x, z, 0) for x in range(4)] for y in range(4) for z in range(4)] + [
    [flat(y, x, z, 1) for y in range(4)] for x in range(4) for z in range(4)
]
FIRST_Z_GROUPS = [[flat(y, x, z, 0) for x in range(4) for z in range(4)] for y in range(4)] + [
    [flat(y, x, z, 1) for y in range(4) for z in range(4)] for x in range(4)
]


def exchange(a, axis, groups=None):
    return lax.all_to_all(a, axis, 0, 0, axis_index_groups=groups, tiled=True)


def vmem_spec():
    return pl.BlockSpec(memory_space=pltpu.VMEM)


def smem_spec():
    return pl.BlockSpec(memory_space=pltpu.SMEM)


def params(limit=VMEM_LIMIT):
    return pltpu.CompilerParams(vmem_limit_bytes=limit)


def scatter(a, groups):
    return lax.psum_scatter(
        a, AXES, scatter_dimension=0, axis_index_groups=groups, tiled=True
    )


def sum_kernel(n, a_ref, out_ref):
    rows = a_ref.shape[0] // n
    total = a_ref[:rows, :]
    for k in range(1, n):
        total = total + a_ref[k * rows : (k + 1) * rows, :]
    for k in range(n):
        out_ref[k * rows : (k + 1) * rows, :] = total


def sum_parts(a, n):
    return pl.pallas_call(
        functools.partial(sum_kernel, n),
        out_shape=jax.ShapeDtypeStruct(a.shape, a.dtype),
        in_specs=[vmem_spec()],
        out_specs=vmem_spec(),
        compiler_params=params(),
        name="sum_parts",
    )(a)


def dot(a, b, ca, cb, precision=None):
    return lax.dot_general(
        a, b, (((ca,), (cb,)), ((), ())), precision=precision, preferred_element_type=F32
    )


def exact(a, b, ca, cb):
    return dot(a, b, ca, cb, lax.Precision.HIGHEST)


def fold(v):
    return (v & 65535) + 15 * (v >> 16)


def reduce_mod(v):
    v = fold(fold(v))
    return jnp.where(v >= PRIME, v - PRIME, v)


def start_rows(first_row, count, seed):
    rows = first_row + lax.broadcasted_iota(jnp.int32, (count, 1), 0)
    cols = lax.broadcasted_iota(jnp.int32, (1, RANK), 1)
    hashed = reduce_mod(rows * 40503 + seed) + reduce_mod(cols * 9973)
    hashed = jnp.where(hashed >= PRIME, hashed - PRIME, hashed)
    low = hashed & 32767
    low = reduce_mod(low * low + 7) & 32767
    third = reduce_mod(low * low + hashed).astype(F32)
    scale = math.sqrt(12.0 / F)
    return (third * (scale / PRIME) - 0.5 * scale).astype(BF16)


TILE = 512


def left_kernel(meta_ref, m_ref, g_ref, b_ref, keep_ref, send_ref, acc):
    t = pl.program_id(0)
    core, tp, seed = meta_ref[0], meta_ref[1], meta_ref[2]
    b = (m_ref[...].astype(F32) + g_ref[...].astype(F32)).astype(BF16)
    b_ref[...] = b
    part = dot(b, start_rows(tp * 3584 + t * TILE, TILE, seed), 1, 0)

    @pl.when(t == 0)
    def _():
        acc[...] = part

    @pl.when(t > 0)
    def _():
        acc[...] += part

    @pl.when(t == pl.num_programs(0) - 1)
    def _():
        keep_ref[...] = acc[pl.ds(core * HALF, HALF), :]
        send_ref[...] = acc[pl.ds((1 - core) * HALF, HALF), :]


def left_partial(meta, momentum, gradient):
    rows, cols = momentum.shape
    half = jax.ShapeDtypeStruct((HALF, RANK), F32)
    whole = pl.BlockSpec((HALF, RANK), lambda t: (0, 0))
    tile = pl.BlockSpec((rows, TILE), lambda t: (0, t))
    return pl.pallas_call(
        left_kernel,
        grid=(cols // TILE,),
        out_shape=(jax.ShapeDtypeStruct((rows, cols), BF16), half, half),
        in_specs=[smem_spec(), tile, tile],
        out_specs=(tile, whole, whole),
        scratch_shapes=[pltpu.VMEM((rows, RANK), F32)],
        compiler_params=params(VMEM_MOST),
        name="left_partial",
    )(meta, momentum, gradient)


GRAM_SHARE = (((0, 512, 0, 128), (128, 256, 128, 256)), ((256, 512, 128, 384), (384, 512, 384, 512)))


def gram_blocks(core):
    return [
        (i, j)
        for r0, r1, c0, c1 in GRAM_SHARE[core]
        for i in range(r0, r1, NB)
        for j in range(c0, c1, NB)
    ]


def gram_kernel(meta_ref, mine_ref, other_ref, out_ref):
    for core in range(2):

        @pl.when(meta_ref[0] == core)
        def _():
            k = 0
            for r0, r1, c0, c1 in GRAM_SHARE[core]:
                g = exact(mine_ref[:, r0:r1], mine_ref[:, c0:c1], 0, 0) + exact(
                    other_ref[:, r0:r1], other_ref[:, c0:c1], 0, 0
                )
                for i in range(0, r1 - r0, NB):
                    for j in range(0, c1 - c0, NB):
                        out_ref[k * NB : (k + 1) * NB, :] = g[i : i + NB, j : j + NB]
                        k += 1


def gram_share(meta, mine, other):
    return pl.pallas_call(
        gram_kernel,
        out_shape=jax.ShapeDtypeStruct((5 * NB, NB), F32),
        in_specs=[smem_spec(), vmem_spec(), vmem_spec()],
        out_specs=vmem_spec(),
        compiler_params=params(),
        name="gram_share",
    )(meta, mine, other)


def right_kernel(terms, meta_ref, b_ref, mine_ref, other_ref, out_ref, split):
    @pl.when(pl.program_id(0) == 0)
    def _():
        core = meta_ref[0]
        for ref, place in ((mine_ref, core), (other_ref, 1 - core)):
            rows = pl.ds(pl.multiple_of(place * HALF, HALF), HALF)
            rest = ref[...]
            for k in range(terms):
                term = rest.astype(BF16)
                split[rows, k * RANK : (k + 1) * RANK] = term
                rest = rest - term.astype(F32)

    w = dot(b_ref[...], split[...], 0, 0)
    out_ref[...] = sum(w[:, k * RANK : (k + 1) * RANK] for k in range(terms)).astype(out_ref.dtype)


def right_partial(meta, blended, mine, other, terms, wire):
    rows, cols = blended.shape
    block = cols // 4
    whole = pl.BlockSpec((HALF, RANK), lambda r: (0, 0))
    return pl.pallas_call(
        functools.partial(right_kernel, terms),
        grid=(4,),
        in_specs=[smem_spec(), pl.BlockSpec((rows, block), lambda r: (0, r)), whole, whole],
        out_specs=pl.BlockSpec((block, RANK), lambda r: (r, 0)),
        scratch_shapes=[pltpu.VMEM((RANK, terms * RANK), BF16)],
        out_shape=jax.ShapeDtypeStruct((cols, RANK), wire),
        compiler_params=params(VMEM_MOST),
        name="right_partial",
    )(meta, blended, mine, other)


def invert_block(ae):
    rows = lax.broadcasted_iota(jnp.int32, (PANEL, NB), 0)
    for k0 in range(0, NB, PANEL):
        left = ae[k0 : k0 + PANEL, :NB]
        right = ae[k0 : k0 + PANEL, NB:]
        columns = [
            jnp.broadcast_to(left[:, k0 + c : k0 + c + 1], (PANEL, NB)) for c in range(PANEL)
        ]
        pivots = jnp.zeros((PANEL, NB), F32)
        for k in range(PANEL):
            pivot = columns[k][k : k + 1, :]
            pivots = jnp.where(rows == k, pivot, pivots)
            if k < PANEL - 1:
                factor = jnp.where(rows > k, columns[k] * (1.0 / pivot), 0.0)
                for c in range(k + 1, PANEL):
                    columns[c] = columns[c] - factor * columns[c][k : k + 1, :]
                left = left - factor * left[k : k + 1, :]
                right = right - factor * right[k : k + 1, :]
        scale = lax.rsqrt(pivots)
        left, right = left * scale, right * scale
        ae[k0 : k0 + PANEL, NB:] = right
        below = k0 + PANEL
        if below < NB:
            ae[below:, :NB] = ae[below:, :NB] - exact(left, left, 0, 0)[below:]
            ae[below:, NB:] = ae[below:, NB:] - exact(left, right, 0, 0)[below:]


def inverse_kernel(meta_ref, mine_ref, other_ref, out_ref, loss_ref, a, ae, diagonal):
    for core in range(2):
        for share, ref in ((core, mine_ref), (1 - core, other_ref)):

            @pl.when(meta_ref[0] == core)
            def _():
                for k, (i, j) in enumerate(gram_blocks(share)):
                    a[i : i + NB, j : j + NB] = ref[k * NB : (k + 1) * NB, :]

    big = lambda d: lax.broadcasted_iota(jnp.int32, (RANK, RANK), d)
    small = lambda d: lax.broadcasted_iota(jnp.int32, (NB, NB), d)
    out_ref[...] = jnp.where(big(0) == big(1), 1.0, 0.0)
    for lo in range(0, RANK, NB):
        hi = lo + NB
        on = jnp.where(small(0) == small(1), a[lo:hi, lo:hi], 0.0)
        diagonal[:, lo:hi] = jnp.sum(on, axis=0, keepdims=True)
    for lo in range(0, RANK, NB):
        hi = lo + NB
        ae[:, :NB] = a[lo:hi, lo:hi]
        ae[:, NB:] = jnp.where(small(0) == small(1), 1.0, 0.0)
        invert_block(ae)
        inverse = jnp.where(small(0) >= small(1), ae[:, NB:], 0.0)
        done = exact(inverse, out_ref[lo:hi, :hi], 1, 0)
        out_ref[lo:hi, :hi] = done
        if hi < RANK:
            below = exact(a[hi:, lo:hi], inverse, 1, 1)
            a[hi:, hi:] = a[hi:, hi:] - exact(below, below, 1, 1)
            out_ref[hi:, :hi] = out_ref[hi:, :hi] - exact(below, done, 1, 0)
    out = out_ref[...]
    loss = jnp.max(jnp.sum(out * out * diagonal[...], axis=1, keepdims=True), axis=0, keepdims=True)
    loss_ref[...] = jnp.broadcast_to(loss, loss_ref.shape)


def inverse_factor(meta, mine, other):
    return pl.pallas_call(
        inverse_kernel,
        out_shape=(
            jax.ShapeDtypeStruct((RANK, RANK), F32),
            jax.ShapeDtypeStruct((8, NB), F32),
        ),
        in_specs=[smem_spec(), vmem_spec(), vmem_spec()],
        out_specs=(vmem_spec(), vmem_spec()),
        scratch_shapes=[
            pltpu.VMEM((RANK, RANK), F32),
            pltpu.VMEM((NB, 2 * NB), F32),
            pltpu.VMEM((1, RANK), F32),
        ],
        compiler_params=params(),
        cost_estimate=pl.CostEstimate(flops=0, bytes_accessed=70_000_000, transcendentals=0),
        name="inverse_factor",
    )(meta, mine, other)


def solve_kernel(w_ref, inv_ref, out_ref):
    out_ref[...] = exact(w_ref[...].astype(F32), inv_ref[...], 1, 1).astype(BF16)


def solve_rows(w, inverse):
    return pl.pallas_call(
        solve_kernel,
        out_shape=jax.ShapeDtypeStruct(w.shape, BF16),
        in_specs=[vmem_spec()] * 2,
        out_specs=vmem_spec(),
        compiler_params=params(),
        name="solve_rows",
    )(w, inverse)


def ortho_kernel(meta_ref, mine_ref, other_ref, inv_ref, out_ref):
    core = meta_ref[0]
    for ref, place in ((mine_ref, core), (other_ref, 1 - core)):
        rows = pl.ds(pl.multiple_of(place * HALF, HALF), HALF)
        out_ref[rows, :] = exact(ref[...], inv_ref[...], 1, 1).astype(BF16)


def ortho_left(meta, mine, other, inverse):
    return pl.pallas_call(
        ortho_kernel,
        out_shape=jax.ShapeDtypeStruct((RANK, RANK), BF16),
        in_specs=[smem_spec()] + [vmem_spec()] * 3,
        out_specs=vmem_spec(),
        compiler_params=params(),
        name="ortho_left",
    )(meta, mine, other, inverse)


def apply_kernel(parts, meta_ref, b_ref, q_ref, sums_ref, *refs):
    rights, (m_ref, u_ref) = refs[:parts], refs[-2:]
    scale = lax.rsqrt(sums_ref[0:1, :] + 1e-6) * math.sqrt(D * F / RANK)
    scaled = (q_ref[...].astype(F32) * scale).astype(BF16)
    width = RANK // parts
    feedback = direction = 0.0
    for k, right in enumerate(rights):
        cols = slice(k * width, (k + 1) * width)
        feedback += dot(q_ref[:, cols], right[...], 1, 1)
        direction += dot(scaled[:, cols], right[...], 1, 1)
    m_ref[...] = (b_ref[...].astype(F32) - 0.05 * feedback).astype(BF16)
    u_ref[...] = direction.astype(BF16)


def apply_block(meta, blended, q, sums, rights, offset, outs):
    rows, cols = blended.shape
    tiles = 2
    here = pl.BlockSpec(
        (rows // tiles, cols // 4), lambda i, meta_ref: (i, (meta_ref[3] + offset) % 4)
    )
    whole = lambda a: pl.BlockSpec(a.shape, lambda i, meta_ref: (0, 0))
    n = len(rights)
    shape = jax.ShapeDtypeStruct((rows, cols), BF16)
    kept = [pl.BlockSpec(memory_space=pl.ANY)] * len(outs)
    return pl.pallas_call(
        functools.partial(apply_kernel, n),
        grid_spec=pltpu.PrefetchScalarGridSpec(
            num_scalar_prefetch=1,
            grid=(tiles,),
            in_specs=[
                here,
                pl.BlockSpec((rows // tiles, RANK), lambda i, meta_ref: (i, 0)),
                whole(sums),
            ]
            + [whole(r) for r in rights]
            + kept,
            out_specs=[here, here],
        ),
        out_shape=[shape, shape],
        input_output_aliases={4 + n + k: k for k in range(len(outs))},
        compiler_params=params(),
        name="apply_block",
    )(meta, blended, q, sums, *rights, *outs)


def sums_kernel(r_ref, out_ref):
    r = r_ref[...].astype(F32)
    out_ref[...] = jnp.broadcast_to(jnp.sum(r * r, axis=0, keepdims=True), out_ref.shape)


def block_sums(r):
    return pl.pallas_call(
        sums_kernel,
        out_shape=jax.ShapeDtypeStruct((16, RANK), F32),
        in_specs=[vmem_spec()],
        out_specs=vmem_spec(),
        compiler_params=params(),
        name="block_sums",
    )(r)


def per_device(momentum, gradient, seed_value):
    fsdp, tp = lax.axis_index("fsdp"), lax.axis_index("tp")
    core, x, y = tp % 2, fsdp % 4, fsdp // 4
    first, second = jnp.where(core == 0, x, y), jnp.where(core == 0, y, x)
    meta = jnp.stack([core, tp, seed_value[0], first, second]).astype(jnp.int32)

    blended, keep, send = left_partial(meta, momentum, gradient)
    half = keep + swap_cores(send)
    mine = exchange(sum_parts(exchange(half, "tp", Z_GROUPS), 4), "tp", Z_GROUPS)
    other = swap_cores(mine)

    w = right_partial(meta, blended, mine, other, 1, BF16)
    mine, other, w = lax.optimization_barrier((mine, other, w))
    w = scatter(w, FIRST_GROUPS)
    gram = exchange(gram_share(meta, mine, other), "fsdp")
    gram = exchange(sum_parts(gram, 16), "fsdp")
    w, gram, gram_other = lax.optimization_barrier((w, gram, swap_cores(gram)))
    w = scatter(w, SECOND_GROUPS)
    inverse, loss = inverse_factor(meta, gram, gram_other)
    w, inverse, loss = lax.optimization_barrier((w, inverse, loss))

    def careful():
        wide = right_partial(meta, blended, mine, other, 2, F32)
        return solve_rows(scatter(scatter(wide, FIRST_GROUPS), SECOND_GROUPS), inverse)

    block = lax.cond(loss[0, 0] <= LOSS_MAX**2, lambda: solve_rows(w, inverse), careful)
    right = exchange(jnp.tile(block, (4, 1)), AXES, SECOND_GROUPS)
    right_low = send_first(right, 1)
    right_high = send_first(right, -1)
    sums = sum_parts(exchange(block_sums(right), AXES, FIRST_Z_GROUPS), 16)
    sums = sums + swap_cores(sums)
    right_low, right_high, sums = lax.optimization_barrier((right_low, right_high, sums))
    far_a = send_first(right_low[:, :HALF], 1)
    far_b = send_first(right_high[:, HALF:], -1)
    q = ortho_left(meta, mine, other, inverse)
    outs = apply_block(meta, blended, q, sums, [right], 0, [])
    outs = apply_block(meta, blended, q, sums, [right_low], 3, outs)
    outs = apply_block(meta, blended, q, sums, [right_high], 1, outs)
    outs = apply_block(meta, blended, q, sums, [far_a, far_b], 2, outs)
    return tuple(outs)


def solution(mesh):
    return jax.shard_map(
        per_device,
        mesh=mesh,
        in_specs=(P("fsdp", "tp"), P("fsdp", "tp"), P()),
        out_specs=(P("fsdp", "tp"), P("fsdp", "tp")),
        check_vma=False,
    )
```

```python
import functools
import math

import jax
import jax.numpy as jnp
from jax import lax
from jax.experimental import pallas as pl
from jax.experimental.pallas import tpu as pltpu
from jax.sharding import PartitionSpec as P

D = 8192
F = 28672
RANK = 512
HALF = RANK // 2
PRIME = 65521
NB = 128
PANEL = 64
STRIP = 16
VMEM_LIMIT = 48 * 1024 * 1024
VMEM_MOST = 61 * 1024 * 1024
F32, BF16 = jnp.float32, jnp.bfloat16
AXES = ("fsdp", "tp")
LOSS_MAX = 2.0


def flat(y, x, z, core):
    return (y * 4 + x) * 8 + z * 2 + core


def everyone():
    return [(y, x, z, c) for y in range(4) for x in range(4) for z in range(4) for c in range(2)]


def shift(along_first, step):
    pairs = []
    for y, x, z, c in everyone():
        if (c == 0) == along_first:
            to = (y, (x + step) % 4, z, c)
        else:
            to = ((y + step) % 4, x, z, c)
        pairs.append((flat(y, x, z, c), flat(*to)))
    return pairs


def send_first(a, step):
    return lax.ppermute(a, AXES, shift(True, step))


def send_second(a, step):
    return lax.ppermute(a, AXES, shift(False, step))


def swap_cores(a):
    return lax.ppermute(a, "tp", [(i, i ^ 1) for i in range(8)])


Z_GROUPS = [[c, 2 + c, 4 + c, 6 + c] for c in range(2)]
SECOND_GROUPS = [[flat(y, x, z, 0) for y in range(4)] for x in range(4) for z in range(4)] + [
    [flat(y, x, z, 1) for x in range(4)] for y in range(4) for z in range(4)
]
FIRST_GROUPS = [[flat(y, x, z, 0) for x in range(4)] for y in range(4) for z in range(4)] + [
    [flat(y, x, z, 1) for y in range(4)] for x in range(4) for z in range(4)
]
FIRST_Z_GROUPS = [[flat(y, x, z, 0) for x in range(4) for z in range(4)] for y in range(4)] + [
    [flat(y, x, z, 1) for y in range(4) for z in range(4)] for x in range(4)
]


def exchange(a, axis, groups=None):
    return lax.all_to_all(a, axis, 0, 0, axis_index_groups=groups, tiled=True)


def vmem_spec():
    return pl.BlockSpec(memory_space=pltpu.VMEM)


def smem_spec():
    return pl.BlockSpec(memory_space=pltpu.SMEM)


def params(limit=VMEM_LIMIT):
    return pltpu.CompilerParams(vmem_limit_bytes=limit)


def scatter(a, groups):
    return lax.psum_scatter(
        a, AXES, scatter_dimension=0, axis_index_groups=groups, tiled=True
    )


def sum_kernel(n, a_ref, out_ref):
    rows = a_ref.shape[0] // n
    total = a_ref[:rows, :]
    for k in range(1, n):
        total = total + a_ref[k * rows : (k + 1) * rows, :]
    for k in range(n):
        out_ref[k * rows : (k + 1) * rows, :] = total


def sum_parts(a, n):
    return pl.pallas_call(
        functools.partial(sum_kernel, n),
        out_shape=jax.ShapeDtypeStruct(a.shape, a.dtype),
        in_specs=[vmem_spec()],
        out_specs=vmem_spec(),
        compiler_params=params(),
        name="sum_parts",
    )(a)


def dot(a, b, ca, cb, precision=None):
    return lax.dot_general(
        a, b, (((ca,), (cb,)), ((), ())), precision=precision, preferred_element_type=F32
    )


def exact(a, b, ca, cb):
    return dot(a, b, ca, cb, lax.Precision.HIGHEST)


def fold(v):
    return v - (v >> 16) * PRIME


def wrap(v):
    return jnp.where(v >= PRIME, v - PRIME, v)


def start_value(a):
    low = a & 32767
    low = wrap(fold(fold(low * low + 7))) & 32767
    third = fold(low * low + a).astype(F32)
    third = third - jnp.floor(third * (1.0 / PRIME) + 0.5 / PRIME) * PRIME
    scale = math.sqrt(12.0 / F)
    return third * (scale / PRIME) - 0.5 * scale


INVERSE = pow(9973, -1, PRIME)
ROW = INVERSE * 40503 % PRIME
TABLE = 520
UNROLL = 8
TILE = 1792


def build_table(table):
    rows = lax.broadcasted_iota(jnp.int32, (8, 128), 0)
    cols = lax.broadcasted_iota(jnp.int32, (8, 128), 1)
    base = wrap(fold(fold(cols * 9973 + rows * 40503)))

    def step(i, offset):
        for k in range(UNROLL):
            table[i * UNROLL + k] = start_value(wrap(base + offset))
            offset = wrap(offset + 9973 * 128 % PRIME)
        return offset

    lax.fori_loop(0, TABLE // UNROLL, step, jnp.int32(0))


def left_kernel(meta_ref, m_ref, g_ref, b_ref, keep_ref, send_ref, acc, table, start):
    t = pl.program_id(0)
    core, tp, seed = meta_ref[0], meta_ref[1], lax.rem(meta_ref[2], PRIME)

    @pl.when(t == 0)
    def _():
        build_table(table)

    window = lax.rem(lax.rem(INVERSE * (seed >> 8), PRIME) * 256 + INVERSE * (seed & 255), PRIME)
    window += lax.rem(tp * (ROW * 3584 % PRIME), PRIME) + lax.rem(t * (ROW * TILE % PRIME), PRIME)
    window = lax.rem(window, PRIME)
    lanes = lax.broadcasted_iota(jnp.int32, (8, 128), 1)
    for i in range(0, TILE, 16):
        groups = []
        for _ in range(2):
            part, whole = window & 127, window >> 7
            turned = [pltpu.roll(table[whole + k], (128 - part) & 127, 1) for k in range(5)]
            first = lanes < 128 - part
            groups.append([jnp.where(first, turned[k], turned[k + 1]) for k in range(4)])
            window = wrap(window + ROW * 8 % PRIME)
        for k in range(4):
            rows = jnp.concatenate([groups[0][k], groups[1][k]], axis=0)
            start[i : i + 16, k * 128 : (k + 1) * 128] = rows.astype(BF16)
    b = (m_ref[...].astype(F32) + g_ref[...].astype(F32)).astype(BF16)
    b_ref[...] = b
    part = dot(b, start[...], 1, 0)

    @pl.when(t == 0)
    def _():
        acc[...] = part

    @pl.when(t == pl.num_programs(0) - 1)
    def _():
        acc[...] += part
        keep_ref[...] = acc[pl.ds(pl.multiple_of(core * HALF, HALF), HALF), :]
        send_ref[...] = acc[pl.ds(pl.multiple_of((1 - core) * HALF, HALF), HALF), :]


def left_partial(meta, momentum, gradient):
    rows, cols = momentum.shape
    half = jax.ShapeDtypeStruct((HALF, RANK), F32)
    whole = pl.BlockSpec((HALF, RANK), lambda t: (0, 0))
    tile = pl.BlockSpec((rows, TILE), lambda t: (0, t))
    return pl.pallas_call(
        left_kernel,
        grid=(2,),
        out_shape=(jax.ShapeDtypeStruct((rows, cols), BF16), half, half),
        in_specs=[smem_spec(), tile, tile],
        out_specs=(tile, whole, whole),
        scratch_shapes=[
            pltpu.VMEM((rows, RANK), F32),
            pltpu.VMEM((TABLE, 8, 128), F32),
            pltpu.VMEM((TILE, RANK), BF16),
        ],
        compiler_params=params(VMEM_MOST),
        name="left_partial",
    )(meta, momentum, gradient)


GRAM_SHARE = (((0, 512, 0, 128), (128, 256, 128, 256)), ((256, 512, 128, 384), (384, 512, 384, 512)))


def gram_blocks(core):
    return [
        (i, j)
        for r0, r1, c0, c1 in GRAM_SHARE[core]
        for i in range(r0, r1, NB)
        for j in range(c0, c1, NB)
    ]


def gram_kernel(meta_ref, mine_ref, other_ref, out_ref):
    for core in range(2):

        @pl.when(meta_ref[0] == core)
        def _():
            k = 0
            for r0, r1, c0, c1 in GRAM_SHARE[core]:
                g = exact(mine_ref[:, r0:r1], mine_ref[:, c0:c1], 0, 0) + exact(
                    other_ref[:, r0:r1], other_ref[:, c0:c1], 0, 0
                )
                for i in range(0, r1 - r0, NB):
                    for j in range(0, c1 - c0, NB):
                        out_ref[k * NB : (k + 1) * NB, :] = g[i : i + NB, j : j + NB]
                        k += 1


def gram_share(meta, mine, other):
    return pl.pallas_call(
        gram_kernel,
        out_shape=jax.ShapeDtypeStruct((5 * NB, NB), F32),
        in_specs=[smem_spec(), vmem_spec(), vmem_spec()],
        out_specs=vmem_spec(),
        compiler_params=params(),
        name="gram_share",
    )(meta, mine, other)


def right_kernel(terms, meta_ref, b_ref, mine_ref, other_ref, out_ref, split):
    @pl.when(pl.program_id(0) == 0)
    def _():
        core = meta_ref[0]
        for ref, place in ((mine_ref, core), (other_ref, 1 - core)):
            rows = pl.ds(pl.multiple_of(place * HALF, HALF), HALF)
            rest = ref[...]
            for k in range(terms):
                term = rest.astype(BF16)
                split[rows, k * RANK : (k + 1) * RANK] = term
                rest = rest - term.astype(F32)

    w = dot(b_ref[...], split[...], 0, 0)
    out_ref[...] = sum(w[:, k * RANK : (k + 1) * RANK] for k in range(terms)).astype(out_ref.dtype)


def right_partial(meta, blended, mine, other, terms, wire):
    rows, cols = blended.shape
    block = cols // 4
    whole = pl.BlockSpec((HALF, RANK), lambda r: (0, 0))
    return pl.pallas_call(
        functools.partial(right_kernel, terms),
        grid=(4,),
        in_specs=[smem_spec(), pl.BlockSpec((rows, block), lambda r: (0, r)), whole, whole],
        out_specs=pl.BlockSpec((block, RANK), lambda r: (r, 0)),
        scratch_shapes=[pltpu.VMEM((RANK, terms * RANK), BF16)],
        out_shape=jax.ShapeDtypeStruct((cols, RANK), wire),
        compiler_params=params(VMEM_MOST),
        name="right_partial",
    )(meta, blended, mine, other)


def invert_block(ae):
    for top in range(0, NB, PANEL):
        end = top + PANEL
        for k0 in range(top, end, STRIP):
            n = end - k0
            rows = lax.broadcasted_iota(jnp.int32, (n, NB), 0)
            left, right = ae[k0:end, :NB], ae[k0:end, NB:]
            columns = [jnp.broadcast_to(left[:, k0 + c : k0 + c + 1], (n, NB)) for c in range(STRIP)]
            scales = []
            for k in range(STRIP):
                pivot = columns[k][k : k + 1, :]
                scales.append(lax.rsqrt(pivot))
                factor = jnp.where(rows > k, columns[k] * (1.0 / pivot), 0.0)
                for c in range(k + 1, STRIP):
                    columns[c] = columns[c] - factor * columns[c][k : k + 1, :]
                left = left - factor * left[k : k + 1, :]
                right = right - factor * right[k : k + 1, :]
            scale = jnp.concatenate(scales, axis=0)
            ae[k0 : k0 + STRIP, :NB] = left[:STRIP] * scale
            ae[k0 : k0 + STRIP, NB:] = right[:STRIP] * scale
            if n > STRIP:
                ae[k0 + STRIP : end, :NB] = left[STRIP:]
                ae[k0 + STRIP : end, NB:] = right[STRIP:]
        if end < NB:
            done = ae[top:end, :]
            ae[end:, :] = ae[end:, :] - exact(done[:, :NB], done, 0, 0)[end:]


def inverse_kernel(meta_ref, mine_ref, other_ref, out_ref, loss_ref, a, ae, diagonal):
    for core in range(2):
        for share, ref in ((core, mine_ref), (1 - core, other_ref)):

            @pl.when(meta_ref[0] == core)
            def _():
                for k, (i, j) in enumerate(gram_blocks(share)):
                    a[i : i + NB, j : j + NB] = ref[k * NB : (k + 1) * NB, :]

    big = lambda d: lax.broadcasted_iota(jnp.int32, (RANK, RANK), d)
    small = lambda d: lax.broadcasted_iota(jnp.int32, (NB, NB), d)
    out_ref[...] = jnp.where(big(0) == big(1), 1.0, 0.0)
    for lo in range(0, RANK, NB):
        hi = lo + NB
        on = jnp.where(small(0) == small(1), a[lo:hi, lo:hi], 0.0)
        diagonal[:, lo:hi] = jnp.sum(on, axis=0, keepdims=True)
    for lo in range(0, RANK, NB):
        hi = lo + NB
        ae[:, :NB] = a[lo:hi, lo:hi]
        ae[:, NB:] = jnp.where(small(0) == small(1), 1.0, 0.0)
        invert_block(ae)
        inverse = jnp.where(small(0) >= small(1), ae[:, NB:], 0.0)
        done = exact(inverse, out_ref[lo:hi, :hi], 1, 0)
        out_ref[lo:hi, :hi] = done
        if hi < RANK:
            below = exact(a[hi:, lo:hi], inverse, 1, 1)
            a[hi:, hi:] = a[hi:, hi:] - exact(below, below, 1, 1)
            out_ref[hi:, :hi] = out_ref[hi:, :hi] - exact(below, done, 1, 0)
    out = out_ref[...]
    loss_ref[0, 0] = jnp.max(jnp.sum(out * out * diagonal[...], axis=1, keepdims=True))


def inverse_factor(meta, mine, other):
    return pl.pallas_call(
        inverse_kernel,
        out_shape=(
            jax.ShapeDtypeStruct((RANK, RANK), F32),
            jax.ShapeDtypeStruct((1, 1), F32),
        ),
        in_specs=[smem_spec(), vmem_spec(), vmem_spec()],
        out_specs=(vmem_spec(), smem_spec()),
        scratch_shapes=[
            pltpu.VMEM((RANK, RANK), F32),
            pltpu.VMEM((NB, 2 * NB), F32),
            pltpu.VMEM((1, RANK), F32),
        ],
        compiler_params=params(),
        cost_estimate=pl.CostEstimate(flops=0, bytes_accessed=70_000_000, transcendentals=0),
        name="inverse_factor",
    )(meta, mine, other)


def two_terms(a):
    top = a.astype(BF16)
    return top, (a - top.astype(F32)).astype(BF16)


def solve_kernel(w_ref, inv_ref, out_ref):
    if w_ref.dtype == BF16:
        top, rest = two_terms(inv_ref[...])
        out = dot(w_ref[...], top, 1, 1) + dot(w_ref[...], rest, 1, 1)
    else:
        out = exact(w_ref[...], inv_ref[...], 1, 1)
    out_ref[...] = out.astype(BF16)


def solve_rows(w, inverse):
    return pl.pallas_call(
        solve_kernel,
        out_shape=jax.ShapeDtypeStruct(w.shape, BF16),
        in_specs=[vmem_spec()] * 2,
        out_specs=vmem_spec(),
        compiler_params=params(),
        name="solve_rows",
    )(w, inverse)


def apply_both(b, q, scaled, right):
    feedback = dot(q, right, 1, 1)
    return (b.astype(F32) - 0.05 * feedback).astype(BF16), dot(scaled, right, 1, 1).astype(BF16)


def apply_kernel(meta_ref, b_ref, mine_ref, other_ref, inv_ref, sums_ref, *refs):
    rights, (m_ref, u_ref, q_ref, scaled_ref) = refs[:3], refs[3:]
    i = pl.program_id(0)

    @pl.when(i == 0)
    def _():
        scale = lax.rsqrt(sums_ref[0:1, :] + 1e-6) * math.sqrt(D * F / RANK)
        top, rest = two_terms(inv_ref[...])
        for ref, place in ((mine_ref, meta_ref[0]), (other_ref, 1 - meta_ref[0])):
            rows = pl.ds(pl.multiple_of(place * HALF, HALF), HALF)
            p_top, p_rest = two_terms(ref[...])
            q = dot(p_top, top, 1, 1) + (dot(p_top, rest, 1, 1) + dot(p_rest, top, 1, 1))
            q = q.astype(BF16)
            q_ref[rows, :] = q
            scaled_ref[rows, :] = (q.astype(F32) * scale).astype(BF16)

    for k in range(3):

        @pl.when(i == k)
        def _():
            m_ref[...], u_ref[...] = apply_both(
                b_ref[...], q_ref[...], scaled_ref[...], rights[k][...]
            )


def apply_three(meta, blended, mine, other, inverse, sums, rights):
    rows, cols = blended.shape

    def place(i, meta_ref):
        offset = jnp.where(i == 0, 0, jnp.where(i == 1, 3, 1))
        return (0, (meta_ref[3] + offset) % 4)

    here = pl.BlockSpec((rows, cols // 4), place)
    whole = lambda a: pl.BlockSpec(a.shape, lambda i, meta_ref: (0, 0))
    shape = jax.ShapeDtypeStruct((rows, cols), BF16)
    square = jax.ShapeDtypeStruct((rows, RANK), BF16)
    rest = [mine, other, inverse, sums] + rights
    return pl.pallas_call(
        apply_kernel,
        grid_spec=pltpu.PrefetchScalarGridSpec(
            num_scalar_prefetch=1,
            grid=(3,),
            in_specs=[here] + [whole(a) for a in rest],
            out_specs=[here, here, whole(square), whole(square)],
        ),
        out_shape=[shape, shape, square, square],
        compiler_params=params(),
        name="apply_three",
    )(meta, blended, *rest)


def last_kernel(meta_ref, b_ref, q_ref, scaled_ref, a_ref, c_ref, m_in, u_in, m_ref, u_ref):
    q, scaled = q_ref[...], scaled_ref[...]
    feedback = dot(q[:, :HALF], a_ref[...], 1, 1) + dot(q[:, HALF:], c_ref[...], 1, 1)
    direction = dot(scaled[:, :HALF], a_ref[...], 1, 1) + dot(scaled[:, HALF:], c_ref[...], 1, 1)
    m_ref[...] = (b_ref[...].astype(F32) - 0.05 * feedback).astype(BF16)
    u_ref[...] = direction.astype(BF16)


def apply_last(meta, blended, q, scaled, rights, outs):
    rows, cols = blended.shape
    tiles = 2
    here = pl.BlockSpec(
        (rows // tiles, cols // 4), lambda i, meta_ref: (i, (meta_ref[3] + 2) % 4)
    )
    part = pl.BlockSpec((rows // tiles, RANK), lambda i, meta_ref: (i, 0))
    whole = pl.BlockSpec((cols // 4, HALF), lambda i, meta_ref: (0, 0))
    kept = pl.BlockSpec(memory_space=pl.ANY)
    shape = jax.ShapeDtypeStruct((rows, cols), BF16)
    return pl.pallas_call(
        last_kernel,
        grid_spec=pltpu.PrefetchScalarGridSpec(
            num_scalar_prefetch=1,
            grid=(tiles,),
            in_specs=[here, part, part, whole, whole, kept, kept],
            out_specs=[here, here],
        ),
        out_shape=[shape, shape],
        input_output_aliases={6: 0, 7: 1},
        compiler_params=params(),
        name="apply_last",
    )(meta, blended, q, scaled, *rights, *outs)


def sums_kernel(r_ref, out_ref):
    r = r_ref[...].astype(F32)
    out_ref[...] = jnp.broadcast_to(jnp.sum(r * r, axis=0, keepdims=True), out_ref.shape)


def block_sums(r):
    return pl.pallas_call(
        sums_kernel,
        out_shape=jax.ShapeDtypeStruct((16, RANK), F32),
        in_specs=[vmem_spec()],
        out_specs=vmem_spec(),
        compiler_params=params(),
        name="block_sums",
    )(r)


def per_device(momentum, gradient, seed_value):
    fsdp, tp = lax.axis_index("fsdp"), lax.axis_index("tp")
    core, x, y = tp % 2, fsdp % 4, fsdp // 4
    first, second = jnp.where(core == 0, x, y), jnp.where(core == 0, y, x)
    meta = jnp.stack([core, tp, seed_value[0], first, second]).astype(jnp.int32)

    blended, keep, send = left_partial(meta, momentum, gradient)
    half = keep + swap_cores(send)
    mine = exchange(sum_parts(exchange(half, "tp", Z_GROUPS), 4), "tp", Z_GROUPS)
    other = swap_cores(mine)

    w = right_partial(meta, blended, mine, other, 1, BF16)
    mine, other, w = lax.optimization_barrier((mine, other, w))
    w = scatter(w, FIRST_GROUPS)
    gram = exchange(gram_share(meta, mine, other), "fsdp")
    gram = exchange(sum_parts(gram, 16), "fsdp")
    w, gram, gram_other = lax.optimization_barrier((w, gram, swap_cores(gram)))
    w = scatter(w, SECOND_GROUPS)
    inverse, loss = inverse_factor(meta, gram, gram_other)
    w, inverse, loss = lax.optimization_barrier((w, inverse, loss))

    def careful():
        wide = right_partial(meta, blended, mine, other, 2, F32)
        return solve_rows(scatter(scatter(wide, FIRST_GROUPS), SECOND_GROUPS), inverse)

    block = lax.cond(loss.reshape(()) <= LOSS_MAX**2, lambda: solve_rows(w, inverse), careful)
    right = exchange(jnp.tile(block, (4, 1)), AXES, SECOND_GROUPS)
    right_low = send_first(right, 1)
    right_high = send_first(right, -1)
    sums = sum_parts(exchange(block_sums(right), AXES, FIRST_Z_GROUPS), 16)
    sums = sums + swap_cores(sums)
    right_low, right_high, sums = lax.optimization_barrier((right_low, right_high, sums))
    far_a = send_first(right_low[:, :HALF], 1)
    far_b = send_first(right_high[:, HALF:], -1)
    *outs, q, scaled = apply_three(
        meta, blended, mine, other, inverse, sums, [right, right_low, right_high]
    )
    return tuple(apply_last(meta, blended, q, scaled, [far_a, far_b], outs))


def solution(mesh):
    return jax.shard_map(
        per_device,
        mesh=mesh,
        in_specs=(P("fsdp", "tp"), P("fsdp", "tp"), P()),
        out_specs=(P("fsdp", "tp"), P("fsdp", "tp")),
        check_vma=False,
    )
```

```python
import functools
import math

import jax
import jax.numpy as jnp
from jax import lax
from jax.experimental import pallas as pl
from jax.experimental.pallas import tpu as pltpu
from jax.sharding import PartitionSpec as P

D = 8192
F = 28672
RANK = 512
HALF = RANK // 2
PRIME = 65521
NB = 128
PANEL = 64
STRIP = 16
VMEM_LIMIT = 48 * 1024 * 1024
VMEM_MOST = 61 * 1024 * 1024
F32, BF16 = jnp.float32, jnp.bfloat16
AXES = ("fsdp", "tp")
LOSS_MAX = 2.0


def flat(y, x, z, core):
    return (y * 4 + x) * 8 + z * 2 + core


def everyone():
    return [(y, x, z, c) for y in range(4) for x in range(4) for z in range(4) for c in range(2)]


def shift(along_first, step):
    pairs = []
    for y, x, z, c in everyone():
        if (c == 0) == along_first:
            to = (y, (x + step) % 4, z, c)
        else:
            to = ((y + step) % 4, x, z, c)
        pairs.append((flat(y, x, z, c), flat(*to)))
    return pairs


def send_first(a, step):
    return lax.ppermute(a, AXES, shift(True, step))


def send_second(a, step):
    return lax.ppermute(a, AXES, shift(False, step))


def swap_cores(a):
    return lax.ppermute(a, "tp", [(i, i ^ 1) for i in range(8)])


Z_GROUPS = [[c, 2 + c, 4 + c, 6 + c] for c in range(2)]
SECOND_GROUPS = [[flat(y, x, z, 0) for y in range(4)] for x in range(4) for z in range(4)] + [
    [flat(y, x, z, 1) for x in range(4)] for y in range(4) for z in range(4)
]
FIRST_GROUPS = [[flat(y, x, z, 0) for x in range(4)] for y in range(4) for z in range(4)] + [
    [flat(y, x, z, 1) for y in range(4)] for x in range(4) for z in range(4)
]


def exchange(a, axis, groups=None):
    return lax.all_to_all(a, axis, 0, 0, axis_index_groups=groups, tiled=True)


def vmem_spec():
    return pl.BlockSpec(memory_space=pltpu.VMEM)


def smem_spec():
    return pl.BlockSpec(memory_space=pltpu.SMEM)


def params(limit=VMEM_LIMIT):
    return pltpu.CompilerParams(vmem_limit_bytes=limit)


def scatter(a, groups):
    return lax.psum_scatter(
        a, AXES, scatter_dimension=0, axis_index_groups=groups, tiled=True
    )


def sum_kernel(n, copies, a_ref, out_ref):
    rows = a_ref.shape[0] // n
    total = a_ref[:rows, :]
    for k in range(1, n):
        total = total + a_ref[k * rows : (k + 1) * rows, :]
    for k in range(copies):
        out_ref[k * rows : (k + 1) * rows, :] = total


def sum_parts(a, n, copies):
    rows, cols = a.shape
    return pl.pallas_call(
        functools.partial(sum_kernel, n, copies),
        out_shape=jax.ShapeDtypeStruct((rows // n * copies, cols), a.dtype),
        in_specs=[vmem_spec()],
        out_specs=vmem_spec(),
        compiler_params=params(),
        name="sum_parts",
    )(a)


def dot(a, b, ca, cb, precision=None):
    return lax.dot_general(
        a, b, (((ca,), (cb,)), ((), ())), precision=precision, preferred_element_type=F32
    )


def exact(a, b, ca, cb):
    return dot(a, b, ca, cb, lax.Precision.HIGHEST)


def fold(v):
    return v - (v >> 16) * PRIME


def wrap(v):
    return jnp.where(v >= PRIME, v - PRIME, v)


def start_value(a):
    low = a & 32767
    low = wrap(fold(fold(low * low + 7))) & 32767
    third = fold(low * low + a).astype(F32)
    third = third - jnp.floor(third * (1.0 / PRIME) + 0.5 / PRIME) * PRIME
    scale = math.sqrt(12.0 / F)
    return third * (scale / PRIME) - 0.5 * scale


INVERSE = pow(9973, -1, PRIME)
ROW = INVERSE * 40503 % PRIME
TABLE = 520
UNROLL = 8
TILE = 1792


def build_table(table):
    rows = lax.broadcasted_iota(jnp.int32, (8, 128), 0)
    cols = lax.broadcasted_iota(jnp.int32, (8, 128), 1)
    base = wrap(fold(fold(cols * 9973 + rows * 40503)))

    def step(i, offset):
        for k in range(UNROLL):
            table[i * UNROLL + k] = start_value(wrap(base + offset))
            offset = wrap(offset + 9973 * 128 % PRIME)
        return offset

    lax.fori_loop(0, TABLE // UNROLL, step, jnp.int32(0))


def left_kernel(meta_ref, m_ref, g_ref, b_ref, keep_ref, send_ref, acc, table, start):
    t = pl.program_id(0)
    core, tp, seed = meta_ref[0], meta_ref[1], lax.rem(meta_ref[2], PRIME)

    @pl.when(t == 0)
    def _():
        build_table(table)

    window = lax.rem(lax.rem(INVERSE * (seed >> 8), PRIME) * 256 + INVERSE * (seed & 255), PRIME)
    window += lax.rem(tp * (ROW * 3584 % PRIME), PRIME) + lax.rem(t * (ROW * TILE % PRIME), PRIME)
    window = lax.rem(window, PRIME)
    lanes = lax.broadcasted_iota(jnp.int32, (8, 128), 1)
    for i in range(0, TILE, 16):
        groups = []
        for _ in range(2):
            part, whole = window & 127, window >> 7
            turned = [pltpu.roll(table[whole + k], (128 - part) & 127, 1) for k in range(5)]
            first = lanes < 128 - part
            groups.append([jnp.where(first, turned[k], turned[k + 1]) for k in range(4)])
            window = wrap(window + ROW * 8 % PRIME)
        for k in range(4):
            rows = jnp.concatenate([groups[0][k], groups[1][k]], axis=0)
            start[i : i + 16, k * 128 : (k + 1) * 128] = rows.astype(BF16)
    b = (m_ref[...].astype(F32) + g_ref[...].astype(F32)).astype(BF16)
    b_ref[...] = b
    part = dot(b, start[...], 1, 0)

    @pl.when(t == 0)
    def _():
        acc[...] = part

    @pl.when(t == pl.num_programs(0) - 1)
    def _():
        acc[...] += part
        keep_ref[...] = acc[pl.ds(pl.multiple_of(core * HALF, HALF), HALF), :]
        send_ref[...] = acc[pl.ds(pl.multiple_of((1 - core) * HALF, HALF), HALF), :]


def left_partial(meta, momentum, gradient):
    rows, cols = momentum.shape
    half = jax.ShapeDtypeStruct((HALF, RANK), F32)
    whole = pl.BlockSpec((HALF, RANK), lambda t: (0, 0))
    tile = pl.BlockSpec((rows, TILE), lambda t: (0, t))
    return pl.pallas_call(
        left_kernel,
        grid=(2,),
        out_shape=(jax.ShapeDtypeStruct((rows, cols), BF16), half, half),
        in_specs=[smem_spec(), tile, tile],
        out_specs=(tile, whole, whole),
        scratch_shapes=[
            pltpu.VMEM((rows, RANK), F32),
            pltpu.VMEM((TABLE, 8, 128), F32),
            pltpu.VMEM((TILE, RANK), BF16),
        ],
        compiler_params=params(VMEM_MOST),
        name="left_partial",
    )(meta, momentum, gradient)


SHARE = NB // 2


def gram_kernel(meta_ref, mine_ref, other_ref, out_ref, g):
    core, z = meta_ref[0], meta_ref[1] // 2
    cols = pl.ds(pl.multiple_of(z * NB, NB), NB)
    g[...] = exact(mine_ref[:, cols], mine_ref[...], 0, 0) + exact(
        other_ref[:, cols], other_ref[...], 0, 0
    )
    rows = pl.ds(pl.multiple_of(core * SHARE, SHARE), SHARE)
    for k in range(4):
        out_ref[k * SHARE : (k + 1) * SHARE, :] = g[rows, k * NB : (k + 1) * NB]


def gram_share(meta, mine, other):
    return pl.pallas_call(
        gram_kernel,
        out_shape=jax.ShapeDtypeStruct((4 * SHARE, NB), F32),
        in_specs=[smem_spec(), vmem_spec(), vmem_spec()],
        out_specs=vmem_spec(),
        scratch_shapes=[pltpu.VMEM((NB, RANK), F32)],
        compiler_params=params(),
        name="gram_share",
    )(meta, mine, other)


def right_kernel(terms, meta_ref, b_ref, mine_ref, other_ref, out_ref, split):
    @pl.when(pl.program_id(0) == 0)
    def _():
        core = meta_ref[0]
        for ref, place in ((mine_ref, core), (other_ref, 1 - core)):
            rows = pl.ds(pl.multiple_of(place * HALF, HALF), HALF)
            rest = ref[...]
            for k in range(terms):
                term = rest.astype(BF16)
                split[rows, k * RANK : (k + 1) * RANK] = term
                rest = rest - term.astype(F32)

    w = dot(b_ref[...], split[...], 0, 0)
    out_ref[...] = sum(w[:, k * RANK : (k + 1) * RANK] for k in range(terms)).astype(out_ref.dtype)


def right_partial(meta, blended, mine, other, terms, wire):
    rows, cols = blended.shape
    block = cols // 2
    whole = pl.BlockSpec((HALF, RANK), lambda r: (0, 0))
    return pl.pallas_call(
        functools.partial(right_kernel, terms),
        grid=(2,),
        in_specs=[smem_spec(), pl.BlockSpec((rows, block), lambda r: (0, r)), whole, whole],
        out_specs=pl.BlockSpec((block, RANK), lambda r: (r, 0)),
        scratch_shapes=[pltpu.VMEM((RANK, terms * RANK), BF16)],
        out_shape=jax.ShapeDtypeStruct((cols, RANK), wire),
        compiler_params=params(VMEM_MOST),
        name="right_partial",
    )(meta, blended, mine, other)


def invert_block(ae):
    for top in range(0, NB, PANEL):
        end = top + PANEL
        for k0 in range(top, end, STRIP):
            n = end - k0
            rows = lax.broadcasted_iota(jnp.int32, (n, NB), 0)
            left, right = ae[k0:end, :NB], ae[k0:end, NB:]
            columns = [jnp.broadcast_to(left[:, k0 + c : k0 + c + 1], (n, NB)) for c in range(STRIP)]
            scales = []
            for k in range(STRIP):
                pivot = columns[k][k : k + 1, :]
                scales.append(lax.rsqrt(pivot))
                factor = jnp.where(rows > k, columns[k] * (1.0 / pivot), 0.0)
                for c in range(k + 1, STRIP):
                    columns[c] = columns[c] - factor * columns[c][k : k + 1, :]
                left = left - factor * left[k : k + 1, :]
                right = right - factor * right[k : k + 1, :]
            scale = jnp.concatenate(scales, axis=0)
            ae[k0 : k0 + STRIP, :NB] = left[:STRIP] * scale
            ae[k0 : k0 + STRIP, NB:] = right[:STRIP] * scale
            if n > STRIP:
                ae[k0 + STRIP : end, :NB] = left[STRIP:]
                ae[k0 + STRIP : end, NB:] = right[STRIP:]
        if end < NB:
            done = ae[top:end, :]
            ae[end:, :] = ae[end:, :] - exact(done[:, :NB], done, 0, 0)[end:]


def inverse_kernel(meta_ref, mine_ref, other_ref, out_ref, loss_ref, a, ae, diagonal):
    for ref, core in ((mine_ref, meta_ref[0]), (other_ref, 1 - meta_ref[0])):
        for z in range(4):
            rows = pl.ds(pl.multiple_of(z * NB + core * SHARE, SHARE), SHARE)
            for k in range(z + 1):
                place = (z * 4 + k) * SHARE
                a[rows, k * NB : (k + 1) * NB] = ref[place : place + SHARE, :]
    big = lambda d: lax.broadcasted_iota(jnp.int32, (RANK, RANK), d)
    small = lambda d: lax.broadcasted_iota(jnp.int32, (NB, NB), d)
    out_ref[...] = jnp.where(big(0) == big(1), 1.0, 0.0)
    for lo in range(0, RANK, NB):
        hi = lo + NB
        on = jnp.where(small(0) == small(1), a[lo:hi, lo:hi], 0.0)
        diagonal[:, lo:hi] = jnp.sum(on, axis=0, keepdims=True)
    for lo in range(0, RANK, NB):
        hi = lo + NB
        ae[:, :NB] = a[lo:hi, lo:hi]
        ae[:, NB:] = jnp.where(small(0) == small(1), 1.0, 0.0)
        invert_block(ae)
        inverse = jnp.where(small(0) >= small(1), ae[:, NB:], 0.0)
        done = exact(inverse, out_ref[lo:hi, :hi], 1, 0)
        out_ref[lo:hi, :hi] = done
        if hi < RANK:
            below = exact(a[hi:, lo:hi], inverse, 1, 1)
            a[hi:, hi:] = a[hi:, hi:] - exact(below, below, 1, 1)
            out_ref[hi:, :hi] = out_ref[hi:, :hi] - exact(below, done, 1, 0)
    out = out_ref[...]
    loss_ref[0, 0] = jnp.max(jnp.sum(out * out * diagonal[...], axis=1, keepdims=True))


def inverse_factor(meta, mine, other):
    return pl.pallas_call(
        inverse_kernel,
        out_shape=(
            jax.ShapeDtypeStruct((RANK, RANK), F32),
            jax.ShapeDtypeStruct((1, 1), F32),
        ),
        in_specs=[smem_spec(), vmem_spec(), vmem_spec()],
        out_specs=(vmem_spec(), smem_spec()),
        scratch_shapes=[
            pltpu.VMEM((RANK, RANK), F32),
            pltpu.VMEM((NB, 2 * NB), F32),
            pltpu.VMEM((1, RANK), F32),
        ],
        compiler_params=params(),
        cost_estimate=pl.CostEstimate(flops=0, bytes_accessed=70_000_000, transcendentals=0),
        name="inverse_factor",
    )(meta, mine, other)


def two_terms(a):
    top = a.astype(BF16)
    return top, (a - top.astype(F32)).astype(BF16)


def solve_kernel(w_ref, inv_ref, out_ref):
    if w_ref.dtype == BF16:
        top, rest = two_terms(inv_ref[...])
        out = dot(w_ref[...], top, 1, 1) + dot(w_ref[...], rest, 1, 1)
    else:
        out = exact(w_ref[...], inv_ref[...], 1, 1)
    out_ref[...] = out.astype(BF16)


def solve_rows(w, inverse):
    return pl.pallas_call(
        solve_kernel,
        out_shape=jax.ShapeDtypeStruct(w.shape, BF16),
        in_specs=[vmem_spec()] * 2,
        out_specs=vmem_spec(),
        compiler_params=params(),
        name="solve_rows",
    )(w, inverse)


def apply_both(b, q, scaled, right):
    feedback = dot(q, right, 1, 1)
    return (b.astype(F32) - 0.05 * feedback).astype(BF16), dot(scaled, right, 1, 1).astype(BF16)


def apply_kernel(meta_ref, b_ref, mine_ref, other_ref, inv_ref, sums_ref, swapped_ref, *refs):
    rights, (m_ref, u_ref, q_ref, scaled_ref) = refs[:3], refs[3:]
    i, j = pl.program_id(0), pl.program_id(1)

    @pl.when((i == 0) & (j == 0))
    def _():
        sums = sums_ref[0:1, :] + swapped_ref[0:1, :]
        scale = lax.rsqrt(sums + 1e-6) * math.sqrt(D * F / RANK)
        top, rest = two_terms(inv_ref[...])
        for ref, place in ((mine_ref, meta_ref[0]), (other_ref, 1 - meta_ref[0])):
            rows = pl.ds(pl.multiple_of(place * HALF, HALF), HALF)
            p_top, p_rest = two_terms(ref[...])
            q = dot(p_top, top, 1, 1) + (dot(p_top, rest, 1, 1) + dot(p_rest, top, 1, 1))
            q = q.astype(BF16)
            q_ref[rows, :] = q
            scaled_ref[rows, :] = (q.astype(F32) * scale).astype(BF16)

    tile = m_ref.shape[0]
    rows = pl.ds(pl.multiple_of(j * tile, tile), tile)
    for k in range(3):

        @pl.when(i == k)
        def _():
            m_ref[...], u_ref[...] = apply_both(
                b_ref[...], q_ref[rows, :], scaled_ref[rows, :], rights[k][...]
            )


def apply_three(meta, blended, mine, other, inverse, sums, rights):
    rows, cols = blended.shape

    tiles = 2

    def place(i, j, meta_ref):
        offset = jnp.where(i == 0, 0, jnp.where(i == 1, 3, 1))
        return (j, (meta_ref[3] + offset) % 4)

    here = pl.BlockSpec((rows // tiles, cols // 4), place)
    whole = lambda a: pl.BlockSpec(a.shape, lambda i, j, meta_ref: (0, 0))
    shape = jax.ShapeDtypeStruct((rows, cols), BF16)
    square = jax.ShapeDtypeStruct((rows, RANK), BF16)
    rest = [mine, other, inverse] + sums + rights
    return pl.pallas_call(
        apply_kernel,
        grid_spec=pltpu.PrefetchScalarGridSpec(
            num_scalar_prefetch=1,
            grid=(3, tiles),
            in_specs=[here] + [whole(a) for a in rest],
            out_specs=[here, here, whole(square), whole(square)],
        ),
        out_shape=[shape, shape, square, square],
        compiler_params=params(),
        name="apply_three",
    )(meta, blended, *rest)


def last_kernel(meta_ref, b_ref, q_ref, scaled_ref, a_ref, c_ref, m_in, u_in, m_ref, u_ref):
    q, scaled = q_ref[...], scaled_ref[...]
    feedback = dot(q[:, :HALF], a_ref[...], 1, 1) + dot(q[:, HALF:], c_ref[...], 1, 1)
    direction = dot(scaled[:, :HALF], a_ref[...], 1, 1) + dot(scaled[:, HALF:], c_ref[...], 1, 1)
    m_ref[...] = (b_ref[...].astype(F32) - 0.05 * feedback).astype(BF16)
    u_ref[...] = direction.astype(BF16)


def apply_last(meta, blended, q, scaled, rights, outs):
    rows, cols = blended.shape
    tiles = 2
    here = pl.BlockSpec(
        (rows // tiles, cols // 4), lambda i, meta_ref: (i, (meta_ref[3] + 2) % 4)
    )
    part = pl.BlockSpec((rows // tiles, RANK), lambda i, meta_ref: (i, 0))
    whole = pl.BlockSpec((cols // 4, HALF), lambda i, meta_ref: (0, 0))
    kept = pl.BlockSpec(memory_space=pl.ANY)
    shape = jax.ShapeDtypeStruct((rows, cols), BF16)
    return pl.pallas_call(
        last_kernel,
        grid_spec=pltpu.PrefetchScalarGridSpec(
            num_scalar_prefetch=1,
            grid=(tiles,),
            in_specs=[here, part, part, whole, whole, kept, kept],
            out_specs=[here, here],
        ),
        out_shape=[shape, shape],
        input_output_aliases={6: 0, 7: 1},
        compiler_params=params(),
        name="apply_last",
    )(meta, blended, q, scaled, *rights, *outs)


def sums_kernel(r_ref, out_ref):
    r = r_ref[...].astype(F32)
    out_ref[...] = jnp.broadcast_to(jnp.sum(r * r, axis=0, keepdims=True), out_ref.shape)


def block_sums(r):
    return pl.pallas_call(
        sums_kernel,
        out_shape=jax.ShapeDtypeStruct((32, RANK), F32),
        in_specs=[vmem_spec()],
        out_specs=vmem_spec(),
        compiler_params=params(),
        name="block_sums",
    )(r)


def per_device(momentum, gradient, seed_value):
    fsdp, tp = lax.axis_index("fsdp"), lax.axis_index("tp")
    core, x, y = tp % 2, fsdp % 4, fsdp // 4
    first, second = jnp.where(core == 0, x, y), jnp.where(core == 0, y, x)
    meta = jnp.stack([core, tp, seed_value[0], first, second]).astype(jnp.int32)

    blended, keep, send = left_partial(meta, momentum, gradient)
    half = keep + swap_cores(send)
    mine = exchange(sum_parts(exchange(half, "tp", Z_GROUPS), 4, 4), "tp", Z_GROUPS)
    other = swap_cores(mine)

    w = right_partial(meta, blended, mine, other, 1, BF16)
    mine, other, w = lax.optimization_barrier((mine, other, w))
    w = scatter(w, FIRST_GROUPS)
    gram = exchange(gram_share(meta, mine, other), "fsdp")
    gram = exchange(sum_parts(gram, 16, 16), "fsdp")
    gram = exchange(jnp.tile(gram, (4, 1)), "tp", Z_GROUPS)
    w, gram, gram_other = lax.optimization_barrier((w, gram, swap_cores(gram)))
    w = scatter(w, SECOND_GROUPS)
    inverse, loss = inverse_factor(meta, gram, gram_other)
    w, inverse, loss = lax.optimization_barrier((w, inverse, loss))

    def careful():
        wide = right_partial(meta, blended, mine, other, 2, F32)
        return solve_rows(scatter(scatter(wide, FIRST_GROUPS), SECOND_GROUPS), inverse)

    block = lax.cond(loss.reshape(()) <= LOSS_MAX**2, lambda: solve_rows(w, inverse), careful)
    right = exchange(jnp.tile(block, (4, 1)), AXES, SECOND_GROUPS)
    right_low = send_first(right, 1)
    right_high = send_first(right, -1)
    sums = sum_parts(exchange(block_sums(right), "tp", Z_GROUPS), 4, 1)
    parts = [sums] + [send_first(sums, k) for k in (1, 2, 3)]
    right_low, right_high, *parts = lax.optimization_barrier((right_low, right_high, *parts))
    far_a = send_first(right_low[:, :HALF], 1)
    far_b = send_first(right_high[:, HALF:], -1)
    sums = sum(parts)
    sums = [sums, swap_cores(sums)]
    *outs, q, scaled = apply_three(
        meta, blended, mine, other, inverse, sums, [right, right_low, right_high]
    )
    return tuple(apply_last(meta, blended, q, scaled, [far_a, far_b], outs))


def solution(mesh):
    return jax.shard_map(
        per_device,
        mesh=mesh,
        in_specs=(P("fsdp", "tp"), P("fsdp", "tp"), P()),
        out_specs=(P("fsdp", "tp"), P("fsdp", "tp")),
        check_vma=False,
    )
```

```python
import functools
import math

import jax
import jax.numpy as jnp
from jax import lax
from jax.experimental import pallas as pl
from jax.experimental.pallas import tpu as pltpu
from jax.sharding import PartitionSpec as P

D = 8192
F = 28672
RANK = 512
HALF = RANK // 2
PRIME = 65521
NB = 128
PANEL = 64
STRIP = 16
VMEM_LIMIT = 48 * 1024 * 1024
VMEM_MOST = 61 * 1024 * 1024
F32, BF16 = jnp.float32, jnp.bfloat16
AXES = ("fsdp", "tp")
LOSS_MAX = 2.0


def flat(y, x, z, core):
    return (y * 4 + x) * 8 + z * 2 + core


def everyone():
    return [(y, x, z, c) for y in range(4) for x in range(4) for z in range(4) for c in range(2)]


def shift(along_first, step):
    pairs = []
    for y, x, z, c in everyone():
        if (c == 0) == along_first:
            to = (y, (x + step) % 4, z, c)
        else:
            to = ((y + step) % 4, x, z, c)
        pairs.append((flat(y, x, z, c), flat(*to)))
    return pairs


def send_first(a, step):
    return lax.ppermute(a, AXES, shift(True, step))


def send_second(a, step):
    return lax.ppermute(a, AXES, shift(False, step))


def swap_cores(a):
    return lax.ppermute(a, "tp", [(i, i ^ 1) for i in range(8)])


def shift_z(a, step):
    return lax.ppermute(a, "tp", [(i, (i + 2 * step) % 8) for i in range(8)])


Z_GROUPS = [[c, 2 + c, 4 + c, 6 + c] for c in range(2)]
SECOND_GROUPS = [[flat(y, x, z, 0) for y in range(4)] for x in range(4) for z in range(4)] + [
    [flat(y, x, z, 1) for x in range(4)] for y in range(4) for z in range(4)
]
FIRST_GROUPS = [[flat(y, x, z, 0) for x in range(4)] for y in range(4) for z in range(4)] + [
    [flat(y, x, z, 1) for y in range(4)] for x in range(4) for z in range(4)
]


def exchange(a, axis, groups=None):
    return lax.all_to_all(a, axis, 0, 0, axis_index_groups=groups, tiled=True)


def vmem_spec():
    return pl.BlockSpec(memory_space=pltpu.VMEM)


def smem_spec():
    return pl.BlockSpec(memory_space=pltpu.SMEM)


def params(limit=VMEM_LIMIT):
    return pltpu.CompilerParams(vmem_limit_bytes=limit)


def scatter(a, groups):
    return lax.psum_scatter(
        a, AXES, scatter_dimension=0, axis_index_groups=groups, tiled=True
    )


def sum_kernel(n, copies, a_ref, out_ref):
    rows = a_ref.shape[0] // n
    total = a_ref[:rows, :]
    for k in range(1, n):
        total = total + a_ref[k * rows : (k + 1) * rows, :]
    for k in range(copies):
        out_ref[k * rows : (k + 1) * rows, :] = total


def piece_kernel(a_ref, out_ref, rounded_ref):
    sum_kernel(4, 1, a_ref, out_ref)
    for k in range(4):
        rows = out_ref.shape[0]
        rounded_ref[k * rows : (k + 1) * rows, :] = out_ref[...].astype(BF16)


def sum_piece(a):
    rows, cols = a.shape
    return pl.pallas_call(
        piece_kernel,
        out_shape=(
            jax.ShapeDtypeStruct((rows // 4, cols), F32),
            jax.ShapeDtypeStruct((rows, cols), BF16),
        ),
        in_specs=[vmem_spec()],
        out_specs=(vmem_spec(), vmem_spec()),
        compiler_params=params(),
        name="sum_piece",
    )(a)


def sum_parts(a, n, copies):
    rows, cols = a.shape
    return pl.pallas_call(
        functools.partial(sum_kernel, n, copies),
        out_shape=jax.ShapeDtypeStruct((rows // n * copies, cols), a.dtype),
        in_specs=[vmem_spec()],
        out_specs=vmem_spec(),
        compiler_params=params(),
        name="sum_parts",
    )(a)


def dot(a, b, ca, cb, precision=None):
    return lax.dot_general(
        a, b, (((ca,), (cb,)), ((), ())), precision=precision, preferred_element_type=F32
    )


def exact(a, b, ca, cb):
    return dot(a, b, ca, cb, lax.Precision.HIGHEST)


def two_terms(a):
    top = a.astype(BF16)
    return top, (a.astype(F32) - top.astype(F32)).astype(BF16)


def product(a, b, ca, cb):
    return dot(a, b, ca, cb) if a.dtype == BF16 else exact(a, b, ca, cb)


def fold(v):
    return v - (v >> 16) * PRIME


def wrap(v):
    return jnp.where(v >= PRIME, v - PRIME, v)


def start_value(a):
    low = a & 32767
    low = wrap(fold(fold(low * low + 7))) & 32767
    third = fold(low * low + a).astype(F32)
    third = third - jnp.floor(third * (1.0 / PRIME) + 0.5 / PRIME) * PRIME
    scale = math.sqrt(12.0 / F)
    return third * (scale / PRIME) - 0.5 * scale


INVERSE = pow(9973, -1, PRIME)
ROW = INVERSE * 40503 % PRIME
TABLE = 520
UNROLL = 8
TILE = 1792


def build_table(table):
    rows = lax.broadcasted_iota(jnp.int32, (8, 128), 0)
    cols = lax.broadcasted_iota(jnp.int32, (8, 128), 1)
    base = wrap(fold(fold(cols * 9973 + rows * 40503)))

    def step(i, offset):
        for k in range(UNROLL):
            table[i * UNROLL + k] = start_value(wrap(base + offset))
            offset = wrap(offset + 9973 * 128 % PRIME)
        return offset

    lax.fori_loop(0, TABLE // UNROLL, step, jnp.int32(0))


def left_kernel(meta_ref, m_ref, g_ref, b_ref, keep_ref, send_ref, acc, table, start):
    t = pl.program_id(0)
    core, tp, seed = meta_ref[0], meta_ref[1], lax.rem(meta_ref[2], PRIME)

    @pl.when(t == 0)
    def _():
        build_table(table)

    window = lax.rem(lax.rem(INVERSE * (seed >> 8), PRIME) * 256 + INVERSE * (seed & 255), PRIME)
    window += lax.rem(tp * (ROW * 3584 % PRIME), PRIME) + lax.rem(t * (ROW * TILE % PRIME), PRIME)
    window = lax.rem(window, PRIME)
    lanes = lax.broadcasted_iota(jnp.int32, (8, 128), 1)
    for i in range(0, TILE, 16):
        groups = []
        for _ in range(2):
            part, whole = window & 127, window >> 7
            turned = [pltpu.roll(table[whole + k], (128 - part) & 127, 1) for k in range(5)]
            first = lanes < 128 - part
            groups.append([jnp.where(first, turned[k], turned[k + 1]) for k in range(4)])
            window = wrap(window + ROW * 8 % PRIME)
        for k in range(4):
            rows = jnp.concatenate([groups[0][k], groups[1][k]], axis=0)
            start[i : i + 16, k * 128 : (k + 1) * 128] = rows.astype(BF16)
    b = (m_ref[...].astype(F32) + g_ref[...].astype(F32)).astype(BF16)
    b_ref[...] = b
    part = dot(b, start[...], 1, 0)

    @pl.when(t == 0)
    def _():
        acc[...] = part

    @pl.when(t == pl.num_programs(0) - 1)
    def _():
        acc[...] += part
        keep_ref[...] = acc[pl.ds(pl.multiple_of(core * HALF, HALF), HALF), :]
        send_ref[...] = acc[pl.ds(pl.multiple_of((1 - core) * HALF, HALF), HALF), :]


def left_partial(meta, momentum, gradient):
    rows, cols = momentum.shape
    half = jax.ShapeDtypeStruct((HALF, RANK), F32)
    whole = pl.BlockSpec((HALF, RANK), lambda t: (0, 0))
    tile = pl.BlockSpec((rows, TILE), lambda t: (0, t))
    return pl.pallas_call(
        left_kernel,
        grid=(2,),
        out_shape=(jax.ShapeDtypeStruct((rows, cols), BF16), half, half),
        in_specs=[smem_spec(), tile, tile],
        out_specs=(tile, whole, whole),
        scratch_shapes=[
            pltpu.VMEM((rows, RANK), F32),
            pltpu.VMEM((TABLE, 8, 128), F32),
            pltpu.VMEM((TILE, RANK), BF16),
        ],
        compiler_params=params(VMEM_MOST),
        name="left_partial",
    )(meta, momentum, gradient)


GRAM_SHARE = (((0, 512, 0, 128), (128, 256, 128, 256)), ((256, 512, 128, 384), (384, 512, 384, 512)))


def gram_blocks(core):
    return [
        (i, j)
        for r0, r1, c0, c1 in GRAM_SHARE[core]
        for i in range(r0, r1, NB)
        for j in range(c0, c1, NB)
    ]


def gram_kernel(meta_ref, mine_ref, other_ref, out_ref):
    for core in range(2):

        @pl.when(meta_ref[0] == core)
        def _():
            k = 0
            for r0, r1, c0, c1 in GRAM_SHARE[core]:
                g = product(mine_ref[:, r0:r1], mine_ref[:, c0:c1], 0, 0) + product(
                    other_ref[:, r0:r1], other_ref[:, c0:c1], 0, 0
                )
                for i in range(0, r1 - r0, NB):
                    for j in range(0, c1 - c0, NB):
                        out_ref[k * NB : (k + 1) * NB, :] = g[i : i + NB, j : j + NB]
                        k += 1


def gram_share(meta, mine, other):
    return pl.pallas_call(
        gram_kernel,
        out_shape=jax.ShapeDtypeStruct((5 * NB, NB), F32),
        in_specs=[smem_spec(), vmem_spec(), vmem_spec()],
        out_specs=vmem_spec(),
        compiler_params=params(),
        name="gram_share",
    )(meta, mine, other)


def right_kernel(meta_ref, b_ref, mine_ref, other_ref, out_ref, split):
    terms = split.shape[1] // RANK

    @pl.when(pl.program_id(0) == 0)
    def _():
        core = meta_ref[0]
        for ref, place in ((mine_ref, core), (other_ref, 1 - core)):
            rows = pl.ds(pl.multiple_of(place * HALF, HALF), HALF)
            for k, term in enumerate(two_terms(ref[...])[:terms]):
                split[rows, k * RANK : (k + 1) * RANK] = term

    w = dot(b_ref[...], split[...], 0, 0)
    out_ref[...] = sum(w[:, k * RANK : (k + 1) * RANK] for k in range(terms)).astype(out_ref.dtype)


def right_partial(meta, blended, mine, other, steps):
    rows, cols = blended.shape
    block = cols // steps
    whole = pl.BlockSpec((HALF, RANK), lambda r: (0, 0))
    terms = 1 if mine.dtype == BF16 else 2
    return pl.pallas_call(
        right_kernel,
        grid=(steps,),
        in_specs=[smem_spec(), pl.BlockSpec((rows, block), lambda r: (0, r)), whole, whole],
        out_specs=pl.BlockSpec((block, RANK), lambda r: (r, 0)),
        scratch_shapes=[pltpu.VMEM((RANK, terms * RANK), BF16)],
        out_shape=jax.ShapeDtypeStruct((cols, RANK), mine.dtype),
        compiler_params=params(VMEM_MOST),
        name="right_partial",
    )(meta, blended, mine, other)


def invert_block(ae):
    for top in range(0, NB, PANEL):
        end = top + PANEL
        for k0 in range(top, end, STRIP):
            n = end - k0
            rows = lax.broadcasted_iota(jnp.int32, (n, NB), 0)
            left, right = ae[k0:end, :NB], ae[k0:end, NB:]
            columns = [jnp.broadcast_to(left[:, k0 + c : k0 + c + 1], (n, NB)) for c in range(STRIP)]
            scales = []
            for k in range(STRIP):
                pivot = columns[k][k : k + 1, :]
                scales.append(lax.rsqrt(pivot))
                factor = jnp.where(rows > k, columns[k] * (1.0 / pivot), 0.0)
                for c in range(k + 1, STRIP):
                    columns[c] = columns[c] - factor * columns[c][k : k + 1, :]
                left = left - factor * left[k : k + 1, :]
                right = right - factor * right[k : k + 1, :]
            scale = jnp.concatenate(scales, axis=0)
            ae[k0 : k0 + STRIP, :NB] = left[:STRIP] * scale
            ae[k0 : k0 + STRIP, NB:] = right[:STRIP] * scale
            if n > STRIP:
                ae[k0 + STRIP : end, :NB] = left[STRIP:]
                ae[k0 + STRIP : end, NB:] = right[STRIP:]
        if end < NB:
            done = ae[top:end, :]
            ae[end:, :] = ae[end:, :] - exact(done[:, :NB], done, 0, 0)[end:]


def inverse_kernel(meta_ref, mine_ref, other_ref, out_ref, loss_ref, a, ae, diagonal):
    for core in range(2):
        for share, ref in ((core, mine_ref), (1 - core, other_ref)):

            @pl.when(meta_ref[0] == core)
            def _():
                for k, (i, j) in enumerate(gram_blocks(share)):
                    a[i : i + NB, j : j + NB] = ref[k * NB : (k + 1) * NB, :]

    big = lambda d: lax.broadcasted_iota(jnp.int32, (RANK, RANK), d)
    small = lambda d: lax.broadcasted_iota(jnp.int32, (NB, NB), d)
    out_ref[...] = jnp.where(big(0) == big(1), 1.0, 0.0)
    for lo in range(0, RANK, NB):
        hi = lo + NB
        on = jnp.where(small(0) == small(1), a[lo:hi, lo:hi], 0.0)
        diagonal[:, lo:hi] = jnp.sum(on, axis=0, keepdims=True)
    for lo in range(0, RANK, NB):
        hi = lo + NB
        ae[:, :NB] = a[lo:hi, lo:hi]
        ae[:, NB:] = jnp.where(small(0) == small(1), 1.0, 0.0)
        invert_block(ae)
        inverse = jnp.where(small(0) >= small(1), ae[:, NB:], 0.0)
        done = exact(inverse, out_ref[lo:hi, :hi], 1, 0)
        out_ref[lo:hi, :hi] = done
        if hi < RANK:
            below = exact(a[hi:, lo:hi], inverse, 1, 1)
            a[hi:, hi:] = a[hi:, hi:] - exact(below, below, 1, 1)
            out_ref[hi:, :hi] = out_ref[hi:, :hi] - exact(below, done, 1, 0)
    out = out_ref[...]
    loss_ref[0, 0] = jnp.max(jnp.sum(out * out * diagonal[...], axis=1, keepdims=True))


def inverse_factor(meta, mine, other):
    return pl.pallas_call(
        inverse_kernel,
        out_shape=(
            jax.ShapeDtypeStruct((RANK, RANK), F32),
            jax.ShapeDtypeStruct((1, 1), F32),
        ),
        in_specs=[smem_spec(), vmem_spec(), vmem_spec()],
        out_specs=(vmem_spec(), smem_spec()),
        scratch_shapes=[
            pltpu.VMEM((RANK, RANK), F32),
            pltpu.VMEM((NB, 2 * NB), F32),
            pltpu.VMEM((1, RANK), F32),
        ],
        compiler_params=params(),
        cost_estimate=pl.CostEstimate(flops=0, bytes_accessed=70_000_000, transcendentals=0),
        name="inverse_factor",
    )(meta, mine, other)


def solve_kernel(meta_ref, w_ref, mine_ref, other_ref, inv_ref, out_ref, q_ref):
    if w_ref.dtype == BF16:
        top, rest = two_terms(inv_ref[...])
        solve = lambda a: dot(a, top, 1, 1) + dot(a, rest, 1, 1)
    else:
        solve = lambda a: exact(a, inv_ref[...], 1, 1)
    out_ref[...] = solve(w_ref[...]).astype(BF16)
    for ref, place in ((mine_ref, meta_ref[0]), (other_ref, 1 - meta_ref[0])):
        rows = pl.ds(pl.multiple_of(place * HALF, HALF), HALF)
        q_ref[rows, :] = solve(ref[...]).astype(BF16)


def solve_rows(meta, w, mine, other, inverse):
    return pl.pallas_call(
        solve_kernel,
        out_shape=(
            jax.ShapeDtypeStruct(w.shape, BF16),
            jax.ShapeDtypeStruct((RANK, RANK), BF16),
        ),
        in_specs=[smem_spec()] + [vmem_spec()] * 4,
        out_specs=(vmem_spec(),) * 2,
        compiler_params=params(),
        name="solve_rows",
    )(meta, w, mine, other, inverse)


def apply_both(b, q, scaled, right):
    feedback = dot(q, right, 1, 1)
    return (b.astype(F32) - 0.05 * feedback).astype(BF16), dot(scaled, right, 1, 1).astype(BF16)


def apply_kernel(meta_ref, b_ref, q_ref, sums_ref, swapped_ref, *refs):
    rights, (m_ref, u_ref, scaled_ref) = refs[:3], refs[3:]
    i, j = pl.program_id(0), pl.program_id(1)

    @pl.when((i == 0) & (j == 0))
    def _():
        sums = sums_ref[0:1, :] + swapped_ref[0:1, :]
        scale = lax.rsqrt(sums + 1e-6) * math.sqrt(D * F / RANK)
        scaled_ref[...] = (q_ref[...].astype(F32) * scale).astype(BF16)

    tile = m_ref.shape[0]
    rows = pl.ds(pl.multiple_of(j * tile, tile), tile)
    for k in range(3):

        @pl.when(i == k)
        def _():
            m_ref[...], u_ref[...] = apply_both(
                b_ref[...], q_ref[rows, :], scaled_ref[rows, :], rights[k][...]
            )


def apply_three(meta, blended, q, sums, rights):
    rows, cols = blended.shape

    tiles = 2

    def place(i, j, meta_ref):
        offset = jnp.where(i == 0, 0, jnp.where(i == 1, 3, 1))
        return (j, (meta_ref[3] + offset) % 4)

    here = pl.BlockSpec((rows // tiles, cols // 4), place)
    whole = lambda a: pl.BlockSpec(a.shape, lambda i, j, meta_ref: (0, 0))
    shape = jax.ShapeDtypeStruct((rows, cols), BF16)
    square = jax.ShapeDtypeStruct((rows, RANK), BF16)
    rest = [q] + sums + rights
    return pl.pallas_call(
        apply_kernel,
        grid_spec=pltpu.PrefetchScalarGridSpec(
            num_scalar_prefetch=1,
            grid=(3, tiles),
            in_specs=[here] + [whole(a) for a in rest],
            out_specs=[here, here, whole(square)],
        ),
        out_shape=[shape, shape, square],
        compiler_params=params(),
        name="apply_three",
    )(meta, blended, *rest)


def last_kernel(meta_ref, b_ref, q_ref, scaled_ref, a_ref, c_ref, m_in, u_in, m_ref, u_ref):
    q, scaled = q_ref[...], scaled_ref[...]
    feedback = dot(q[:, :HALF], a_ref[...], 1, 1) + dot(q[:, HALF:], c_ref[...], 1, 1)
    direction = dot(scaled[:, :HALF], a_ref[...], 1, 1) + dot(scaled[:, HALF:], c_ref[...], 1, 1)
    m_ref[...] = (b_ref[...].astype(F32) - 0.05 * feedback).astype(BF16)
    u_ref[...] = direction.astype(BF16)


def apply_last(meta, blended, q, scaled, rights, outs):
    rows, cols = blended.shape
    tiles = 2
    here = pl.BlockSpec(
        (rows // tiles, cols // 4), lambda i, meta_ref: (i, (meta_ref[3] + 2) % 4)
    )
    part = pl.BlockSpec((rows // tiles, RANK), lambda i, meta_ref: (i, 0))
    whole = pl.BlockSpec((cols // 4, HALF), lambda i, meta_ref: (0, 0))
    kept = pl.BlockSpec(memory_space=pl.ANY)
    shape = jax.ShapeDtypeStruct((rows, cols), BF16)
    return pl.pallas_call(
        last_kernel,
        grid_spec=pltpu.PrefetchScalarGridSpec(
            num_scalar_prefetch=1,
            grid=(tiles,),
            in_specs=[here, part, part, whole, whole, kept, kept],
            out_specs=[here, here],
        ),
        out_shape=[shape, shape],
        input_output_aliases={6: 0, 7: 1},
        compiler_params=params(),
        name="apply_last",
    )(meta, blended, q, scaled, *rights, *outs)


def sums_kernel(r_ref, out_ref):
    r = r_ref[...].astype(F32)
    out_ref[...] = jnp.broadcast_to(jnp.sum(r * r, axis=0, keepdims=True), out_ref.shape)


def block_sums(r):
    return pl.pallas_call(
        sums_kernel,
        out_shape=jax.ShapeDtypeStruct((8, RANK), F32),
        in_specs=[vmem_spec()],
        out_specs=vmem_spec(),
        compiler_params=params(),
        name="block_sums",
    )(r)


def per_device(momentum, gradient, seed_value):
    fsdp, tp = lax.axis_index("fsdp"), lax.axis_index("tp")
    core, x, y = tp % 2, fsdp % 4, fsdp // 4
    first, second = jnp.where(core == 0, x, y), jnp.where(core == 0, y, x)
    meta = jnp.stack([core, tp, seed_value[0], first, second]).astype(jnp.int32)

    blended, keep, send = left_partial(meta, momentum, gradient)
    half = keep + swap_cores(send)
    piece, rounded = sum_piece(exchange(half, "tp", Z_GROUPS))

    def gram_sum(mine, other):
        gram = exchange(gram_share(meta, mine, other), "fsdp")
        gram = exchange(sum_parts(gram, 16, 16), "fsdp")
        return gram, swap_cores(gram)

    def careful():
        mine = exchange(jnp.tile(piece, (4, 1)), "tp", Z_GROUPS)
        other = swap_cores(mine)
        inverse, _ = inverse_factor(meta, *gram_sum(mine, other))
        w = right_partial(meta, blended, mine, other, 4)
        w = scatter(scatter(w, FIRST_GROUPS), SECOND_GROUPS)
        return solve_rows(meta, w, mine, other, inverse)

    mine = exchange(rounded, "tp", Z_GROUPS)
    other = swap_cores(mine)
    w = right_partial(meta, blended, mine, other, 2)
    mine, other, w = lax.optimization_barrier((mine, other, w))
    w = scatter(w, FIRST_GROUPS)
    gram = gram_sum(mine, other)
    w, *gram = lax.optimization_barrier((w, *gram))
    w = scatter(w, SECOND_GROUPS)
    inverse, loss = inverse_factor(meta, *gram)
    w, inverse, loss = lax.optimization_barrier((w, inverse, loss))
    block, q = lax.cond(
        loss.reshape(()) <= LOSS_MAX**2,
        lambda: solve_rows(meta, w, mine, other, inverse),
        careful,
    )
    right = exchange(jnp.tile(block, (4, 1)), AXES, SECOND_GROUPS)
    right_low = send_first(right, 1)
    right_high = send_first(right, -1)
    sums = block_sums(right)
    sums = sums + sum(shift_z(sums, k) for k in (1, 2, 3))
    parts = [sums] + [send_first(sums, k) for k in (1, 2, 3)]
    right_low, right_high, *parts = lax.optimization_barrier((right_low, right_high, *parts))
    far_a = send_first(right_low[:, :HALF], 1)
    far_b = send_first(right_high[:, HALF:], -1)
    sums = sum(parts)
    sums = [sums, swap_cores(sums)]
    *outs, scaled = apply_three(meta, blended, q, sums, [right, right_low, right_high])
    return tuple(apply_last(meta, blended, q, scaled, [far_a, far_b], outs))


def solution(mesh):
    return jax.shard_map(
        per_device,
        mesh=mesh,
        in_specs=(P("fsdp", "tp"), P("fsdp", "tp"), P()),
        out_specs=(P("fsdp", "tp"), P("fsdp", "tp")),
        check_vma=False,
    )
```

```python
import functools
import math

import jax
import jax.numpy as jnp
from jax import lax
from jax.experimental import pallas as pl
from jax.experimental.pallas import tpu as pltpu
from jax.sharding import PartitionSpec as P

D = 8192
F = 28672
RANK = 512
HALF = RANK // 2
PRIME = 65521
NB = 128
PANEL = 64
STRIP = 16
VMEM_LIMIT = 48 * 1024 * 1024
VMEM_MOST = 61 * 1024 * 1024
F32, BF16 = jnp.float32, jnp.bfloat16
AXES = ("fsdp", "tp")
LOSS_MAX = 2.0


def flat(y, x, z, core):
    return (y * 4 + x) * 8 + z * 2 + core


def everyone():
    return [(y, x, z, c) for y in range(4) for x in range(4) for z in range(4) for c in range(2)]


def shift(along_first, step):
    pairs = []
    for y, x, z, c in everyone():
        if (c == 0) == along_first:
            to = (y, (x + step) % 4, z, c)
        else:
            to = ((y + step) % 4, x, z, c)
        pairs.append((flat(y, x, z, c), flat(*to)))
    return pairs


def send_first(a, step):
    return lax.ppermute(a, AXES, shift(True, step))


def send_second(a, step):
    return lax.ppermute(a, AXES, shift(False, step))


def swap_cores(a):
    return lax.ppermute(a, "tp", [(i, i ^ 1) for i in range(8)])


def shift_z(a, step):
    return lax.ppermute(a, "tp", [(i, (i + 2 * step) % 8) for i in range(8)])


Z_GROUPS = [[c, 2 + c, 4 + c, 6 + c] for c in range(2)]
SECOND_GROUPS = [[flat(y, x, z, 0) for y in range(4)] for x in range(4) for z in range(4)] + [
    [flat(y, x, z, 1) for x in range(4)] for y in range(4) for z in range(4)
]
FIRST_GROUPS = [[flat(y, x, z, 0) for x in range(4)] for y in range(4) for z in range(4)] + [
    [flat(y, x, z, 1) for y in range(4)] for x in range(4) for z in range(4)
]


def exchange(a, axis, groups=None):
    return lax.all_to_all(a, axis, 0, 0, axis_index_groups=groups, tiled=True)


def vmem_spec():
    return pl.BlockSpec(memory_space=pltpu.VMEM)


def smem_spec():
    return pl.BlockSpec(memory_space=pltpu.SMEM)


def params(limit=VMEM_LIMIT):
    return pltpu.CompilerParams(vmem_limit_bytes=limit)


def scatter(a, groups):
    return lax.psum_scatter(
        a, AXES, scatter_dimension=0, axis_index_groups=groups, tiled=True
    )


def sum_kernel(n, copies, a_ref, out_ref):
    rows = a_ref.shape[0] // n
    total = a_ref[:rows, :]
    for k in range(1, n):
        total = total + a_ref[k * rows : (k + 1) * rows, :]
    for k in range(copies):
        out_ref[k * rows : (k + 1) * rows, :] = total


def piece_kernel(a_ref, out_ref, rounded_ref):
    sum_kernel(4, 1, a_ref, out_ref)
    for k in range(4):
        rows = out_ref.shape[0]
        rounded_ref[k * rows : (k + 1) * rows, :] = out_ref[...].astype(BF16)


def sum_piece(a):
    rows, cols = a.shape
    return pl.pallas_call(
        piece_kernel,
        out_shape=(
            jax.ShapeDtypeStruct((rows // 4, cols), F32),
            jax.ShapeDtypeStruct((rows, cols), BF16),
        ),
        in_specs=[vmem_spec()],
        out_specs=(vmem_spec(), vmem_spec()),
        compiler_params=params(),
        name="sum_piece",
    )(a)


def sum_parts(a, n, copies):
    rows, cols = a.shape
    return pl.pallas_call(
        functools.partial(sum_kernel, n, copies),
        out_shape=jax.ShapeDtypeStruct((rows // n * copies, cols), a.dtype),
        in_specs=[vmem_spec()],
        out_specs=vmem_spec(),
        compiler_params=params(),
        name="sum_parts",
    )(a)


def dot(a, b, ca, cb, precision=None):
    return lax.dot_general(
        a, b, (((ca,), (cb,)), ((), ())), precision=precision, preferred_element_type=F32
    )


def exact(a, b, ca, cb):
    return dot(a, b, ca, cb, lax.Precision.HIGHEST)


def two_terms(a):
    top = a.astype(BF16)
    return top, (a.astype(F32) - top.astype(F32)).astype(BF16)


def product(a, b, ca, cb):
    return dot(a, b, ca, cb) if a.dtype == BF16 else exact(a, b, ca, cb)


def fold(v):
    return v - (v >> 16) * PRIME


def wrap(v):
    return jnp.where(v >= PRIME, v - PRIME, v)


def start_value(a):
    low = a & 32767
    low = wrap(fold(fold(low * low + 7))) & 32767
    third = fold(low * low + a).astype(F32)
    third = third - jnp.floor(third * (1.0 / PRIME) + 0.5 / PRIME) * PRIME
    scale = math.sqrt(12.0 / F)
    return third * (scale / PRIME) - 0.5 * scale


INVERSE = pow(9973, -1, PRIME)
ROW = INVERSE * 40503 % PRIME
TABLE = 520
UNROLL = 8
TILE = 1792


def build_table(table):
    rows = lax.broadcasted_iota(jnp.int32, (8, 128), 0)
    cols = lax.broadcasted_iota(jnp.int32, (8, 128), 1)
    base = wrap(fold(fold(cols * 9973 + rows * 40503)))

    def step(i, offset):
        for k in range(UNROLL):
            table[i * UNROLL + k] = start_value(wrap(base + offset))
            offset = wrap(offset + 9973 * 128 % PRIME)
        return offset

    lax.fori_loop(0, TABLE // UNROLL, step, jnp.int32(0))


def left_kernel(meta_ref, m_ref, g_ref, b_ref, keep_ref, send_ref, acc, table, start):
    t = pl.program_id(0)
    core, tp, seed = meta_ref[0], meta_ref[1], lax.rem(meta_ref[2], PRIME)

    @pl.when(t == 0)
    def _():
        build_table(table)

    window = lax.rem(lax.rem(INVERSE * (seed >> 8), PRIME) * 256 + INVERSE * (seed & 255), PRIME)
    window += lax.rem(tp * (ROW * 3584 % PRIME), PRIME) + lax.rem(t * (ROW * TILE % PRIME), PRIME)
    window = lax.rem(window, PRIME)
    lanes = lax.broadcasted_iota(jnp.int32, (8, 128), 1)

    def fill(step, window):
        for i in range(0, 128, 16):
            groups = []
            for _ in range(2):
                part, whole = window & 127, window >> 7
                turned = [pltpu.roll(table[whole + k], (128 - part) & 127, 1) for k in range(5)]
                first = lanes < 128 - part
                groups.append([jnp.where(first, turned[k], turned[k + 1]) for k in range(4)])
                window = wrap(window + ROW * 8 % PRIME)
            for k in range(4):
                rows = jnp.concatenate([groups[0][k], groups[1][k]], axis=0)
                place = pl.ds(pl.multiple_of(step * 128 + i, 16), 16)
                start[place, k * 128 : (k + 1) * 128] = rows.astype(BF16)
        return window

    lax.fori_loop(0, TILE // 128, fill, window)
    b = (m_ref[...].astype(F32) + g_ref[...].astype(F32)).astype(BF16)
    b_ref[...] = b
    part = dot(b, start[...], 1, 0)

    @pl.when(t == 0)
    def _():
        acc[...] = part

    @pl.when(t == pl.num_programs(0) - 1)
    def _():
        acc[...] += part
        keep_ref[...] = acc[pl.ds(pl.multiple_of(core * HALF, HALF), HALF), :]
        send_ref[...] = acc[pl.ds(pl.multiple_of((1 - core) * HALF, HALF), HALF), :]


def left_partial(meta, momentum, gradient):
    rows, cols = momentum.shape
    half = jax.ShapeDtypeStruct((HALF, RANK), F32)
    whole = pl.BlockSpec((HALF, RANK), lambda t: (0, 0))
    tile = pl.BlockSpec((rows, TILE), lambda t: (0, t))
    return pl.pallas_call(
        left_kernel,
        grid=(2,),
        out_shape=(jax.ShapeDtypeStruct((rows, cols), BF16), half, half),
        in_specs=[smem_spec(), tile, tile],
        out_specs=(tile, whole, whole),
        scratch_shapes=[
            pltpu.VMEM((rows, RANK), F32),
            pltpu.VMEM((TABLE, 8, 128), F32),
            pltpu.VMEM((TILE, RANK), BF16),
        ],
        compiler_params=params(VMEM_MOST),
        name="left_partial",
    )(meta, momentum, gradient)


GRAM_SHARE = (((0, 512, 0, 128), (128, 256, 128, 256)), ((256, 512, 128, 384), (384, 512, 384, 512)))


def gram_blocks(core):
    return [
        (i, j)
        for r0, r1, c0, c1 in GRAM_SHARE[core]
        for i in range(r0, r1, NB)
        for j in range(c0, c1, NB)
    ]


def gram_kernel(meta_ref, mine_ref, other_ref, out_ref):
    for core in range(2):

        @pl.when(meta_ref[0] == core)
        def _():
            k = 0
            for r0, r1, c0, c1 in GRAM_SHARE[core]:
                g = product(mine_ref[:, r0:r1], mine_ref[:, c0:c1], 0, 0) + product(
                    other_ref[:, r0:r1], other_ref[:, c0:c1], 0, 0
                )
                for i in range(0, r1 - r0, NB):
                    for j in range(0, c1 - c0, NB):
                        out_ref[k * NB : (k + 1) * NB, :] = g[i : i + NB, j : j + NB]
                        k += 1


def gram_share(meta, mine, other):
    return pl.pallas_call(
        gram_kernel,
        out_shape=jax.ShapeDtypeStruct((5 * NB, NB), F32),
        in_specs=[smem_spec(), vmem_spec(), vmem_spec()],
        out_specs=vmem_spec(),
        compiler_params=params(),
        name="gram_share",
    )(meta, mine, other)


def right_kernel(meta_ref, b_ref, mine_ref, other_ref, out_ref, split):
    terms = split.shape[1] // RANK

    @pl.when(pl.program_id(0) == 0)
    def _():
        core = meta_ref[0]
        for ref, place in ((mine_ref, core), (other_ref, 1 - core)):
            rows = pl.ds(pl.multiple_of(place * HALF, HALF), HALF)
            for k, term in enumerate(two_terms(ref[...])[:terms]):
                split[rows, k * RANK : (k + 1) * RANK] = term

    w = dot(b_ref[...], split[...], 0, 0)
    out_ref[...] = sum(w[:, k * RANK : (k + 1) * RANK] for k in range(terms)).astype(out_ref.dtype)


def right_partial(meta, blended, mine, other, steps):
    rows, cols = blended.shape
    block = cols // steps
    whole = pl.BlockSpec((HALF, RANK), lambda r: (0, 0))
    terms = 1 if mine.dtype == BF16 else 2
    return pl.pallas_call(
        right_kernel,
        grid=(steps,),
        in_specs=[smem_spec(), pl.BlockSpec((rows, block), lambda r: (0, r)), whole, whole],
        out_specs=pl.BlockSpec((block, RANK), lambda r: (r, 0)),
        scratch_shapes=[pltpu.VMEM((RANK, terms * RANK), BF16)],
        out_shape=jax.ShapeDtypeStruct((cols, RANK), mine.dtype),
        compiler_params=params(VMEM_MOST),
        name="right_partial",
    )(meta, blended, mine, other)


def invert_block(ae):
    for top in range(0, NB, PANEL):
        end = top + PANEL
        for k0 in range(top, end, STRIP):
            n = end - k0
            rows = lax.broadcasted_iota(jnp.int32, (n, NB), 0)
            left, right = ae[k0:end, :NB], ae[k0:end, NB:]
            columns = [jnp.broadcast_to(left[:, k0 + c : k0 + c + 1], (n, NB)) for c in range(STRIP)]
            scales = []
            for k in range(STRIP):
                pivot = columns[k][k : k + 1, :]
                scales.append(lax.rsqrt(pivot))
                factor = jnp.where(rows > k, columns[k] * (1.0 / pivot), 0.0)
                for c in range(k + 1, STRIP):
                    columns[c] = columns[c] - factor * columns[c][k : k + 1, :]
                left = left - factor * left[k : k + 1, :]
                right = right - factor * right[k : k + 1, :]
            scale = jnp.concatenate(scales, axis=0)
            ae[k0 : k0 + STRIP, :NB] = left[:STRIP] * scale
            ae[k0 : k0 + STRIP, NB:] = right[:STRIP] * scale
            if n > STRIP:
                ae[k0 + STRIP : end, :NB] = left[STRIP:]
                ae[k0 + STRIP : end, NB:] = right[STRIP:]
        if end < NB:
            done = ae[top:end, :]
            ae[end:, :] = ae[end:, :] - exact(done[:, :NB], done, 0, 0)[end:]


def inverse_kernel(meta_ref, mine_ref, other_ref, out_ref, loss_ref, a, ae, diagonal):
    for core in range(2):
        for share, ref in ((core, mine_ref), (1 - core, other_ref)):

            @pl.when(meta_ref[0] == core)
            def _():
                for k, (i, j) in enumerate(gram_blocks(share)):
                    a[i : i + NB, j : j + NB] = ref[k * NB : (k + 1) * NB, :]

    big = lambda d: lax.broadcasted_iota(jnp.int32, (RANK, RANK), d)
    small = lambda d: lax.broadcasted_iota(jnp.int32, (NB, NB), d)
    out_ref[...] = jnp.where(big(0) == big(1), 1.0, 0.0)
    for lo in range(0, RANK, NB):
        hi = lo + NB
        on = jnp.where(small(0) == small(1), a[lo:hi, lo:hi], 0.0)
        diagonal[:, lo:hi] = jnp.sum(on, axis=0, keepdims=True)

    def block(b, carry):
        diag = pl.ds(pl.multiple_of(b * NB, NB), NB)
        ae[:, :NB] = a[diag, diag]
        ae[:, NB:] = jnp.where(small(0) == small(1), 1.0, 0.0)
        invert_block(ae)
        for k in range(RANK // NB):

            @pl.when(b == k)
            def _():
                lo, hi = k * NB, (k + 1) * NB
                inverse = jnp.where(small(0) >= small(1), ae[:, NB:], 0.0)
                done = exact(inverse, out_ref[lo:hi, :hi], 1, 0)
                out_ref[lo:hi, :hi] = done
                if hi < RANK:
                    below = exact(a[hi:, lo:hi], inverse, 1, 1)
                    a[hi:, hi:] = a[hi:, hi:] - exact(below, below, 1, 1)
                    out_ref[hi:, :hi] = out_ref[hi:, :hi] - exact(below, done, 1, 0)

        return carry

    lax.fori_loop(0, RANK // NB, block, 0)
    out = out_ref[...]
    loss_ref[0, 0] = jnp.max(jnp.sum(out * out * diagonal[...], axis=1, keepdims=True))


def inverse_factor(meta, mine, other):
    return pl.pallas_call(
        inverse_kernel,
        out_shape=(
            jax.ShapeDtypeStruct((RANK, RANK), F32),
            jax.ShapeDtypeStruct((1, 1), F32),
        ),
        in_specs=[smem_spec(), vmem_spec(), vmem_spec()],
        out_specs=(vmem_spec(), smem_spec()),
        scratch_shapes=[
            pltpu.VMEM((RANK, RANK), F32),
            pltpu.VMEM((NB, 2 * NB), F32),
            pltpu.VMEM((1, RANK), F32),
        ],
        compiler_params=params(),
        cost_estimate=pl.CostEstimate(flops=0, bytes_accessed=70_000_000, transcendentals=0),
        name="inverse_factor",
    )(meta, mine, other)


def solve_kernel(meta_ref, w_ref, mine_ref, other_ref, inv_ref, out_ref, q_ref):
    if w_ref.dtype == BF16:
        top, rest = two_terms(inv_ref[...])
        solve = lambda a: dot(a, top, 1, 1) + dot(a, rest, 1, 1)
    else:
        solve = lambda a: exact(a, inv_ref[...], 1, 1)
    out_ref[...] = solve(w_ref[...]).astype(BF16)
    for ref, place in ((mine_ref, meta_ref[0]), (other_ref, 1 - meta_ref[0])):
        rows = pl.ds(pl.multiple_of(place * HALF, HALF), HALF)
        q_ref[rows, :] = solve(ref[...]).astype(BF16)


def solve_rows(meta, w, mine, other, inverse):
    return pl.pallas_call(
        solve_kernel,
        out_shape=(
            jax.ShapeDtypeStruct(w.shape, BF16),
            jax.ShapeDtypeStruct((RANK, RANK), BF16),
        ),
        in_specs=[smem_spec()] + [vmem_spec()] * 4,
        out_specs=(vmem_spec(),) * 2,
        compiler_params=params(),
        name="solve_rows",
    )(meta, w, mine, other, inverse)


def apply_both(b, q, scaled, right):
    feedback = dot(q, right, 1, 1)
    return (b.astype(F32) - 0.05 * feedback).astype(BF16), dot(scaled, right, 1, 1).astype(BF16)


def apply_kernel(meta_ref, b_ref, q_ref, sums_ref, swapped_ref, *refs):
    rights, (m_ref, u_ref, scaled_ref) = refs[:3], refs[3:]
    i, j = pl.program_id(0), pl.program_id(1)

    @pl.when((i == 0) & (j == 0))
    def _():
        sums = sums_ref[0:1, :] + swapped_ref[0:1, :]
        scale = lax.rsqrt(sums + 1e-6) * math.sqrt(D * F / RANK)
        scaled_ref[...] = (q_ref[...].astype(F32) * scale).astype(BF16)

    tile = m_ref.shape[0]
    rows = pl.ds(pl.multiple_of(j * tile, tile), tile)
    for k in range(3):

        @pl.when(i == k)
        def _():
            m_ref[...], u_ref[...] = apply_both(
                b_ref[...], q_ref[rows, :], scaled_ref[rows, :], rights[k][...]
            )


def apply_three(meta, blended, q, sums, rights):
    rows, cols = blended.shape

    tiles = 2

    def place(i, j, meta_ref):
        offset = jnp.where(i == 0, 0, jnp.where(i == 1, 3, 1))
        return (j, (meta_ref[3] + offset) % 4)

    here = pl.BlockSpec((rows // tiles, cols // 4), place)
    whole = lambda a: pl.BlockSpec(a.shape, lambda i, j, meta_ref: (0, 0))
    shape = jax.ShapeDtypeStruct((rows, cols), BF16)
    square = jax.ShapeDtypeStruct((rows, RANK), BF16)
    rest = [q] + sums + rights
    return pl.pallas_call(
        apply_kernel,
        grid_spec=pltpu.PrefetchScalarGridSpec(
            num_scalar_prefetch=1,
            grid=(3, tiles),
            in_specs=[here] + [whole(a) for a in rest],
            out_specs=[here, here, whole(square)],
        ),
        out_shape=[shape, shape, square],
        compiler_params=params(),
        name="apply_three",
    )(meta, blended, *rest)


def last_kernel(meta_ref, b_ref, q_ref, scaled_ref, a_ref, c_ref, m_in, u_in, m_ref, u_ref):
    q, scaled = q_ref[...], scaled_ref[...]
    feedback = dot(q[:, :HALF], a_ref[...], 1, 1) + dot(q[:, HALF:], c_ref[...], 1, 1)
    direction = dot(scaled[:, :HALF], a_ref[...], 1, 1) + dot(scaled[:, HALF:], c_ref[...], 1, 1)
    m_ref[...] = (b_ref[...].astype(F32) - 0.05 * feedback).astype(BF16)
    u_ref[...] = direction.astype(BF16)


def apply_last(meta, blended, q, scaled, rights, outs):
    rows, cols = blended.shape
    tiles = 2
    here = pl.BlockSpec(
        (rows // tiles, cols // 4), lambda i, meta_ref: (i, (meta_ref[3] + 2) % 4)
    )
    part = pl.BlockSpec((rows // tiles, RANK), lambda i, meta_ref: (i, 0))
    whole = pl.BlockSpec((cols // 4, HALF), lambda i, meta_ref: (0, 0))
    kept = pl.BlockSpec(memory_space=pl.ANY)
    shape = jax.ShapeDtypeStruct((rows, cols), BF16)
    return pl.pallas_call(
        last_kernel,
        grid_spec=pltpu.PrefetchScalarGridSpec(
            num_scalar_prefetch=1,
            grid=(tiles,),
            in_specs=[here, part, part, whole, whole, kept, kept],
            out_specs=[here, here],
        ),
        out_shape=[shape, shape],
        input_output_aliases={6: 0, 7: 1},
        compiler_params=params(),
        name="apply_last",
    )(meta, blended, q, scaled, *rights, *outs)


def sums_kernel(r_ref, out_ref):
    r = r_ref[...].astype(F32)
    out_ref[...] = jnp.broadcast_to(jnp.sum(r * r, axis=0, keepdims=True), out_ref.shape)


def block_sums(r):
    return pl.pallas_call(
        sums_kernel,
        out_shape=jax.ShapeDtypeStruct((8, RANK), F32),
        in_specs=[vmem_spec()],
        out_specs=vmem_spec(),
        compiler_params=params(),
        name="block_sums",
    )(r)


def per_device(momentum, gradient, seed_value):
    fsdp, tp = lax.axis_index("fsdp"), lax.axis_index("tp")
    core, x, y = tp % 2, fsdp % 4, fsdp // 4
    first, second = jnp.where(core == 0, x, y), jnp.where(core == 0, y, x)
    meta = jnp.stack([core, tp, seed_value[0], first, second]).astype(jnp.int32)

    blended, keep, send = left_partial(meta, momentum, gradient)
    half = keep + swap_cores(send)
    piece, rounded = sum_piece(exchange(half, "tp", Z_GROUPS))

    def gram_sum(mine, other):
        gram = exchange(gram_share(meta, mine, other), "fsdp")
        gram = exchange(sum_parts(gram, 16, 16), "fsdp")
        return gram, swap_cores(gram)

    def careful():
        mine = exchange(jnp.tile(piece, (4, 1)), "tp", Z_GROUPS)
        other = swap_cores(mine)
        inverse, _ = inverse_factor(meta, *gram_sum(mine, other))
        w = right_partial(meta, blended, mine, other, 4)
        w = scatter(scatter(w, FIRST_GROUPS), SECOND_GROUPS)
        return solve_rows(meta, w, mine, other, inverse)

    mine = exchange(rounded, "tp", Z_GROUPS)
    other = swap_cores(mine)
    w = right_partial(meta, blended, mine, other, 2)
    mine, other, w = lax.optimization_barrier((mine, other, w))
    w = scatter(w, FIRST_GROUPS)
    gram = gram_sum(mine, other)
    w, *gram = lax.optimization_barrier((w, *gram))
    w = scatter(w, SECOND_GROUPS)
    inverse, loss = inverse_factor(meta, *gram)
    w, inverse, loss = lax.optimization_barrier((w, inverse, loss))
    block, q = lax.cond(
        loss.reshape(()) <= LOSS_MAX**2,
        lambda: solve_rows(meta, w, mine, other, inverse),
        careful,
    )
    right = exchange(jnp.tile(block, (4, 1)), AXES, SECOND_GROUPS)
    right_low = send_first(right, 1)
    right_high = send_first(right, -1)
    sums = block_sums(right)
    sums = sums + sum(shift_z(sums, k) for k in (1, 2, 3))
    parts = [sums] + [send_first(sums, k) for k in (1, 2, 3)]
    right_low, right_high, *parts = lax.optimization_barrier((right_low, right_high, *parts))
    far_a = send_first(right_low[:, :HALF], 1)
    far_b = send_first(right_high[:, HALF:], -1)
    sums = sum(parts)
    sums = [sums, swap_cores(sums)]
    *outs, scaled = apply_three(meta, blended, q, sums, [right, right_low, right_high])
    return tuple(apply_last(meta, blended, q, scaled, [far_a, far_b], outs))


def solution(mesh):
    return jax.shard_map(
        per_device,
        mesh=mesh,
        in_specs=(P("fsdp", "tp"), P("fsdp", "tp"), P()),
        out_specs=(P("fsdp", "tp"), P("fsdp", "tp")),
        check_vma=False,
    )
```

```python
import functools
import math

import jax
import jax.numpy as jnp
from jax import lax
from jax.experimental import pallas as pl
from jax.experimental.pallas import tpu as pltpu
from jax.sharding import PartitionSpec as P

D = 8192
F = 28672
RANK = 512
HALF = RANK // 2
PRIME = 65521
NB = 128
PANEL = 64
STRIP = 16
VMEM_LIMIT = 48 * 1024 * 1024
VMEM_MOST = 61 * 1024 * 1024
F32, BF16 = jnp.float32, jnp.bfloat16
AXES = ("fsdp", "tp")
LOSS_MAX = 2.0


def flat(y, x, z, core):
    return (y * 4 + x) * 8 + z * 2 + core


def everyone():
    return [(y, x, z, c) for y in range(4) for x in range(4) for z in range(4) for c in range(2)]


def shift(along_first, step):
    pairs = []
    for y, x, z, c in everyone():
        if (c == 0) == along_first:
            to = (y, (x + step) % 4, z, c)
        else:
            to = ((y + step) % 4, x, z, c)
        pairs.append((flat(y, x, z, c), flat(*to)))
    return pairs


def send_first(a, step):
    return lax.ppermute(a, AXES, shift(True, step))


def send_second(a, step):
    return lax.ppermute(a, AXES, shift(False, step))


def swap_cores(a):
    return lax.ppermute(a, "tp", [(i, i ^ 1) for i in range(8)])


def shift_z(a, step):
    return lax.ppermute(a, "tp", [(i, (i + 2 * step) % 8) for i in range(8)])


Z_GROUPS = [[c, 2 + c, 4 + c, 6 + c] for c in range(2)]
SECOND_GROUPS = [[flat(y, x, z, 0) for y in range(4)] for x in range(4) for z in range(4)] + [
    [flat(y, x, z, 1) for x in range(4)] for y in range(4) for z in range(4)
]
FIRST_GROUPS = [[flat(y, x, z, 0) for x in range(4)] for y in range(4) for z in range(4)] + [
    [flat(y, x, z, 1) for y in range(4)] for x in range(4) for z in range(4)
]


def exchange(a, axis, groups=None):
    return lax.all_to_all(a, axis, 0, 0, axis_index_groups=groups, tiled=True)


def vmem_spec():
    return pl.BlockSpec(memory_space=pltpu.VMEM)


def smem_spec():
    return pl.BlockSpec(memory_space=pltpu.SMEM)


def params(limit=VMEM_LIMIT):
    return pltpu.CompilerParams(vmem_limit_bytes=limit)


def scatter(a, groups):
    return lax.psum_scatter(
        a, AXES, scatter_dimension=0, axis_index_groups=groups, tiled=True
    )


def sum_kernel(n, copies, a_ref, out_ref):
    rows = a_ref.shape[0] // n
    total = a_ref[:rows, :]
    for k in range(1, n):
        total = total + a_ref[k * rows : (k + 1) * rows, :]
    for k in range(copies):
        out_ref[k * rows : (k + 1) * rows, :] = total


def piece_kernel(a_ref, out_ref, rounded_ref):
    sum_kernel(4, 1, a_ref, out_ref)
    for k in range(4):
        rows = out_ref.shape[0]
        rounded_ref[k * rows : (k + 1) * rows, :] = out_ref[...].astype(BF16)


def sum_piece(a):
    rows, cols = a.shape
    return pl.pallas_call(
        piece_kernel,
        out_shape=(
            jax.ShapeDtypeStruct((rows // 4, cols), F32),
            jax.ShapeDtypeStruct((rows, cols), BF16),
        ),
        in_specs=[vmem_spec()],
        out_specs=(vmem_spec(), vmem_spec()),
        compiler_params=params(),
        name="sum_piece",
    )(a)


def sum_parts(a, n, copies):
    rows, cols = a.shape
    return pl.pallas_call(
        functools.partial(sum_kernel, n, copies),
        out_shape=jax.ShapeDtypeStruct((rows // n * copies, cols), a.dtype),
        in_specs=[vmem_spec()],
        out_specs=vmem_spec(),
        compiler_params=params(),
        name="sum_parts",
    )(a)


def dot(a, b, ca, cb, precision=None):
    return lax.dot_general(
        a, b, (((ca,), (cb,)), ((), ())), precision=precision, preferred_element_type=F32
    )


def exact(a, b, ca, cb):
    return dot(a, b, ca, cb, lax.Precision.HIGHEST)


def two_terms(a):
    top = a.astype(BF16)
    return top, (a.astype(F32) - top.astype(F32)).astype(BF16)


def product(a, b, ca, cb):
    return dot(a, b, ca, cb) if a.dtype == BF16 else exact(a, b, ca, cb)


def fold(v):
    return v - (v >> 16) * PRIME


def wrap(v):
    return jnp.where(v >= PRIME, v - PRIME, v)


def start_value(a):
    low = a & 32767
    low = wrap(fold(fold(low * low + 7))) & 32767
    third = fold(low * low + a).astype(F32)
    third = third - jnp.floor(third * (1.0 / PRIME) + 0.5 / PRIME) * PRIME
    scale = math.sqrt(12.0 / F)
    return third * (scale / PRIME) - 0.5 * scale


INVERSE = pow(9973, -1, PRIME)
ROW = INVERSE * 40503 % PRIME
TABLE = 520
UNROLL = 8
TILE = 1792


def build_table(table):
    rows = lax.broadcasted_iota(jnp.int32, (8, 128), 0)
    cols = lax.broadcasted_iota(jnp.int32, (8, 128), 1)
    base = wrap(fold(fold(cols * 9973 + rows * 40503)))

    def step(i, offset):
        for k in range(UNROLL):
            table[i * UNROLL + k] = start_value(wrap(base + offset))
            offset = wrap(offset + 9973 * 128 % PRIME)
        return offset

    lax.fori_loop(0, TABLE // UNROLL, step, jnp.int32(0))


def left_kernel(meta_ref, m_ref, g_ref, b_ref, keep_ref, send_ref, acc, table, start):
    t = pl.program_id(0)
    core, tp, seed = meta_ref[0], meta_ref[1], lax.rem(meta_ref[2], PRIME)

    @pl.when(t == 0)
    def _():
        build_table(table)

    window = lax.rem(lax.rem(INVERSE * (seed >> 8), PRIME) * 256 + INVERSE * (seed & 255), PRIME)
    window += lax.rem(tp * (ROW * 3584 % PRIME), PRIME) + lax.rem(t * (ROW * TILE % PRIME), PRIME)
    window = lax.rem(window, PRIME)
    lanes = lax.broadcasted_iota(jnp.int32, (8, 128), 1)
    for i in range(0, TILE, 16):
        groups = []
        for _ in range(2):
            part, whole = window & 127, window >> 7
            turned = [pltpu.roll(table[whole + k], (128 - part) & 127, 1) for k in range(5)]
            first = lanes < 128 - part
            groups.append([jnp.where(first, turned[k], turned[k + 1]) for k in range(4)])
            window = wrap(window + ROW * 8 % PRIME)
        for k in range(4):
            rows = jnp.concatenate([groups[0][k], groups[1][k]], axis=0)
            start[i : i + 16, k * 128 : (k + 1) * 128] = rows.astype(BF16)
    b = (m_ref[...].astype(F32) + g_ref[...].astype(F32)).astype(BF16)
    b_ref[...] = b
    part = dot(b, start[...], 1, 0)

    @pl.when(t == 0)
    def _():
        acc[...] = part

    @pl.when(t == pl.num_programs(0) - 1)
    def _():
        acc[...] += part
        keep_ref[...] = acc[pl.ds(pl.multiple_of(core * HALF, HALF), HALF), :]
        send_ref[...] = acc[pl.ds(pl.multiple_of((1 - core) * HALF, HALF), HALF), :]


def left_partial(meta, momentum, gradient):
    rows, cols = momentum.shape
    half = jax.ShapeDtypeStruct((HALF, RANK), F32)
    whole = pl.BlockSpec((HALF, RANK), lambda t: (0, 0))
    tile = pl.BlockSpec((rows, TILE), lambda t: (0, t))
    return pl.pallas_call(
        left_kernel,
        grid=(2,),
        out_shape=(jax.ShapeDtypeStruct((rows, cols), BF16), half, half),
        in_specs=[smem_spec(), tile, tile],
        out_specs=(tile, whole, whole),
        scratch_shapes=[
            pltpu.VMEM((rows, RANK), F32),
            pltpu.VMEM((TABLE, 8, 128), F32),
            pltpu.VMEM((TILE, RANK), BF16),
        ],
        compiler_params=params(VMEM_MOST),
        name="left_partial",
    )(meta, momentum, gradient)


GRAM_SHARE = (((0, 512, 0, 128), (128, 256, 128, 256)), ((256, 512, 128, 384), (384, 512, 384, 512)))


def gram_blocks(core):
    return [
        (i, j)
        for r0, r1, c0, c1 in GRAM_SHARE[core]
        for i in range(r0, r1, NB)
        for j in range(c0, c1, NB)
    ]


def gram_kernel(meta_ref, mine_ref, other_ref, out_ref):
    for core in range(2):

        @pl.when(meta_ref[0] == core)
        def _():
            k = 0
            for r0, r1, c0, c1 in GRAM_SHARE[core]:
                g = product(mine_ref[:, r0:r1], mine_ref[:, c0:c1], 0, 0) + product(
                    other_ref[:, r0:r1], other_ref[:, c0:c1], 0, 0
                )
                for i in range(0, r1 - r0, NB):
                    for j in range(0, c1 - c0, NB):
                        out_ref[k * NB : (k + 1) * NB, :] = g[i : i + NB, j : j + NB]
                        k += 1


def gram_share(meta, mine, other):
    return pl.pallas_call(
        gram_kernel,
        out_shape=jax.ShapeDtypeStruct((5 * NB, NB), F32),
        in_specs=[smem_spec(), vmem_spec(), vmem_spec()],
        out_specs=vmem_spec(),
        compiler_params=params(),
        name="gram_share",
    )(meta, mine, other)


def right_kernel(meta_ref, b_ref, mine_ref, other_ref, out_ref, split):
    terms = split.shape[1] // RANK

    @pl.when(pl.program_id(0) == 0)
    def _():
        core = meta_ref[0]
        for ref, place in ((mine_ref, core), (other_ref, 1 - core)):
            rows = pl.ds(pl.multiple_of(place * HALF, HALF), HALF)
            for k, term in enumerate(two_terms(ref[...])[:terms]):
                split[rows, k * RANK : (k + 1) * RANK] = term

    w = dot(b_ref[...], split[...], 0, 0)
    out_ref[...] = sum(w[:, k * RANK : (k + 1) * RANK] for k in range(terms)).astype(out_ref.dtype)


def right_partial(meta, blended, mine, other, steps):
    rows, cols = blended.shape
    block = cols // steps
    whole = pl.BlockSpec((HALF, RANK), lambda r: (0, 0))
    terms = 1 if mine.dtype == BF16 else 2
    return pl.pallas_call(
        right_kernel,
        grid=(steps,),
        in_specs=[smem_spec(), pl.BlockSpec((rows, block), lambda r: (0, r)), whole, whole],
        out_specs=pl.BlockSpec((block, RANK), lambda r: (r, 0)),
        scratch_shapes=[pltpu.VMEM((RANK, terms * RANK), BF16)],
        out_shape=jax.ShapeDtypeStruct((cols, RANK), mine.dtype),
        compiler_params=params(VMEM_MOST),
        name="right_partial",
    )(meta, blended, mine, other)


def invert_block(ae):
    for top in range(0, NB, PANEL):
        end = top + PANEL
        for k0 in range(top, end, STRIP):
            n = end - k0
            rows = lax.broadcasted_iota(jnp.int32, (n, NB), 0)
            left, right = ae[k0:end, :NB], ae[k0:end, NB:]
            columns = [jnp.broadcast_to(left[:, k0 + c : k0 + c + 1], (n, NB)) for c in range(STRIP)]
            scales = []
            for k in range(STRIP):
                pivot = columns[k][k : k + 1, :]
                scales.append(lax.rsqrt(pivot))
                factor = jnp.where(rows > k, columns[k] * (1.0 / pivot), 0.0)
                for c in range(k + 1, STRIP):
                    columns[c] = columns[c] - factor * columns[c][k : k + 1, :]
                left = left - factor * left[k : k + 1, :]
                right = right - factor * right[k : k + 1, :]
            scale = jnp.concatenate(scales, axis=0)
            ae[k0 : k0 + STRIP, :NB] = left[:STRIP] * scale
            ae[k0 : k0 + STRIP, NB:] = right[:STRIP] * scale
            if n > STRIP:
                ae[k0 + STRIP : end, :NB] = left[STRIP:]
                ae[k0 + STRIP : end, NB:] = right[STRIP:]
        if end < NB:
            done = ae[top:end, :]
            ae[end:, :] = ae[end:, :] - exact(done[:, :NB], done, 0, 0)[end:]


def inverse_kernel(meta_ref, mine_ref, other_ref, out_ref, loss_ref, a, ae, diagonal):
    for core in range(2):
        for share, ref in ((core, mine_ref), (1 - core, other_ref)):

            @pl.when(meta_ref[0] == core)
            def _():
                for k, (i, j) in enumerate(gram_blocks(share)):
                    a[i : i + NB, j : j + NB] = ref[k * NB : (k + 1) * NB, :]

    big = lambda d: lax.broadcasted_iota(jnp.int32, (RANK, RANK), d)
    small = lambda d: lax.broadcasted_iota(jnp.int32, (NB, NB), d)
    out_ref[...] = jnp.where(big(0) == big(1), 1.0, 0.0)
    for lo in range(0, RANK, NB):
        hi = lo + NB
        on = jnp.where(small(0) == small(1), a[lo:hi, lo:hi], 0.0)
        diagonal[:, lo:hi] = jnp.sum(on, axis=0, keepdims=True)

    def block(b, carry):
        diag = pl.ds(pl.multiple_of(b * NB, NB), NB)
        ae[:, :NB] = a[diag, diag]
        ae[:, NB:] = jnp.where(small(0) == small(1), 1.0, 0.0)
        invert_block(ae)
        for k in range(RANK // NB):

            @pl.when(b == k)
            def _():
                lo, hi = k * NB, (k + 1) * NB
                inverse = jnp.where(small(0) >= small(1), ae[:, NB:], 0.0)
                done = exact(inverse, out_ref[lo:hi, :hi], 1, 0)
                out_ref[lo:hi, :hi] = done
                if hi < RANK:
                    below = exact(a[hi:, lo:hi], inverse, 1, 1)
                    a[hi:, hi:] = a[hi:, hi:] - exact(below, below, 1, 1)
                    out_ref[hi:, :hi] = out_ref[hi:, :hi] - exact(below, done, 1, 0)

        return carry

    lax.fori_loop(0, RANK // NB, block, 0)
    out = out_ref[...]
    loss_ref[0, 0] = jnp.max(jnp.sum(out * out * diagonal[...], axis=1, keepdims=True))


def inverse_factor(meta, mine, other):
    return pl.pallas_call(
        inverse_kernel,
        out_shape=(
            jax.ShapeDtypeStruct((RANK, RANK), F32),
            jax.ShapeDtypeStruct((1, 1), F32),
        ),
        in_specs=[smem_spec(), vmem_spec(), vmem_spec()],
        out_specs=(vmem_spec(), smem_spec()),
        scratch_shapes=[
            pltpu.VMEM((RANK, RANK), F32),
            pltpu.VMEM((NB, 2 * NB), F32),
            pltpu.VMEM((1, RANK), F32),
        ],
        compiler_params=params(),
        cost_estimate=pl.CostEstimate(flops=0, bytes_accessed=70_000_000, transcendentals=0),
        name="inverse_factor",
    )(meta, mine, other)


def solve(a, inv_ref):
    if a.dtype == BF16:
        top, rest = two_terms(inv_ref[...])
        return (dot(a, top, 1, 1) + dot(a, rest, 1, 1)).astype(BF16)
    return exact(a, inv_ref[...], 1, 1).astype(BF16)


def solve_kernel(w_ref, inv_ref, out_ref):
    out_ref[...] = solve(w_ref[...], inv_ref)


def solve_rows(w, inverse):
    return pl.pallas_call(
        solve_kernel,
        out_shape=jax.ShapeDtypeStruct(w.shape, BF16),
        in_specs=[vmem_spec()] * 2,
        out_specs=vmem_spec(),
        compiler_params=params(),
        name="solve_rows",
    )(w, inverse)


def ortho_kernel(meta_ref, mine_ref, other_ref, inv_ref, out_ref):
    for ref, place in ((mine_ref, meta_ref[0]), (other_ref, 1 - meta_ref[0])):
        rows = pl.ds(pl.multiple_of(place * HALF, HALF), HALF)
        out_ref[rows, :] = solve(ref[...], inv_ref)


def ortho_left(meta, mine, other, inverse):
    return pl.pallas_call(
        ortho_kernel,
        out_shape=jax.ShapeDtypeStruct((RANK, RANK), BF16),
        in_specs=[smem_spec()] + [vmem_spec()] * 3,
        out_specs=vmem_spec(),
        compiler_params=params(),
        name="ortho_left",
    )(meta, mine, other, inverse)


def apply_both(b, q, scaled, right):
    feedback = dot(q, right, 1, 1)
    return (b.astype(F32) - 0.05 * feedback).astype(BF16), dot(scaled, right, 1, 1).astype(BF16)


def apply_kernel(meta_ref, b_ref, q_ref, sums_ref, swapped_ref, *refs):
    rights, (m_ref, u_ref, scaled_ref) = refs[:3], refs[3:]
    i, j = pl.program_id(0), pl.program_id(1)

    @pl.when((i == 0) & (j == 0))
    def _():
        sums = sums_ref[0:1, :] + swapped_ref[0:1, :]
        scale = lax.rsqrt(sums + 1e-6) * math.sqrt(D * F / RANK)
        scaled_ref[...] = (q_ref[...].astype(F32) * scale).astype(BF16)

    tile = m_ref.shape[0]
    rows = pl.ds(pl.multiple_of(j * tile, tile), tile)
    for k in range(3):

        @pl.when(i == k)
        def _():
            m_ref[...], u_ref[...] = apply_both(
                b_ref[...], q_ref[rows, :], scaled_ref[rows, :], rights[k][...]
            )


def apply_three(meta, blended, q, sums, rights):
    rows, cols = blended.shape

    tiles = 2

    def place(i, j, meta_ref):
        offset = jnp.where(i == 0, 0, jnp.where(i == 1, 3, 1))
        return (j, (meta_ref[3] + offset) % 4)

    here = pl.BlockSpec((rows // tiles, cols // 4), place)
    whole = lambda a: pl.BlockSpec(a.shape, lambda i, j, meta_ref: (0, 0))
    shape = jax.ShapeDtypeStruct((rows, cols), BF16)
    square = jax.ShapeDtypeStruct((rows, RANK), BF16)
    rest = [q] + sums + rights
    return pl.pallas_call(
        apply_kernel,
        grid_spec=pltpu.PrefetchScalarGridSpec(
            num_scalar_prefetch=1,
            grid=(3, tiles),
            in_specs=[here] + [whole(a) for a in rest],
            out_specs=[here, here, whole(square)],
        ),
        out_shape=[shape, shape, square],
        compiler_params=params(),
        name="apply_three",
    )(meta, blended, *rest)


def last_kernel(meta_ref, b_ref, q_ref, scaled_ref, a_ref, c_ref, m_in, u_in, m_ref, u_ref):
    q, scaled = q_ref[...], scaled_ref[...]
    feedback = dot(q[:, :HALF], a_ref[...], 1, 1) + dot(q[:, HALF:], c_ref[...], 1, 1)
    direction = dot(scaled[:, :HALF], a_ref[...], 1, 1) + dot(scaled[:, HALF:], c_ref[...], 1, 1)
    m_ref[...] = (b_ref[...].astype(F32) - 0.05 * feedback).astype(BF16)
    u_ref[...] = direction.astype(BF16)


def apply_last(meta, blended, q, scaled, rights, outs):
    rows, cols = blended.shape
    tiles = 2
    here = pl.BlockSpec(
        (rows // tiles, cols // 4), lambda i, meta_ref: (i, (meta_ref[3] + 2) % 4)
    )
    part = pl.BlockSpec((rows // tiles, RANK), lambda i, meta_ref: (i, 0))
    whole = pl.BlockSpec((cols // 4, HALF), lambda i, meta_ref: (0, 0))
    kept = pl.BlockSpec(memory_space=pl.ANY)
    shape = jax.ShapeDtypeStruct((rows, cols), BF16)
    return pl.pallas_call(
        last_kernel,
        grid_spec=pltpu.PrefetchScalarGridSpec(
            num_scalar_prefetch=1,
            grid=(tiles,),
            in_specs=[here, part, part, whole, whole, kept, kept],
            out_specs=[here, here],
        ),
        out_shape=[shape, shape],
        input_output_aliases={6: 0, 7: 1},
        compiler_params=params(),
        name="apply_last",
    )(meta, blended, q, scaled, *rights, *outs)


def sums_kernel(r_ref, out_ref):
    r = r_ref[...].astype(F32)
    out_ref[...] = jnp.broadcast_to(jnp.sum(r * r, axis=0, keepdims=True), out_ref.shape)


def block_sums(r):
    return pl.pallas_call(
        sums_kernel,
        out_shape=jax.ShapeDtypeStruct((8, RANK), F32),
        in_specs=[vmem_spec()],
        out_specs=vmem_spec(),
        compiler_params=params(),
        name="block_sums",
    )(r)


def per_device(momentum, gradient, seed_value):
    fsdp, tp = lax.axis_index("fsdp"), lax.axis_index("tp")
    core, x, y = tp % 2, fsdp % 4, fsdp // 4
    first, second = jnp.where(core == 0, x, y), jnp.where(core == 0, y, x)
    meta = jnp.stack([core, tp, seed_value[0], first, second]).astype(jnp.int32)

    blended, keep, send = left_partial(meta, momentum, gradient)
    half = keep + swap_cores(send)
    piece, rounded = sum_piece(exchange(half, "tp", Z_GROUPS))

    def gram_sum(mine, other):
        gram = exchange(gram_share(meta, mine, other), "fsdp")
        return exchange(sum_parts(gram, 16, 16), "fsdp")

    def careful():
        mine = exchange(jnp.tile(piece, (4, 1)), "tp", Z_GROUPS)
        other = swap_cores(mine)
        gram = gram_sum(mine, other)
        inverse, _ = inverse_factor(meta, gram, swap_cores(gram))
        w = right_partial(meta, blended, mine, other, 4)
        w = scatter(scatter(w, FIRST_GROUPS), SECOND_GROUPS)
        return solve_rows(w, inverse), ortho_left(meta, mine, other, inverse)

    mine = exchange(rounded, "tp", Z_GROUPS)
    other = swap_cores(mine)
    w = right_partial(meta, blended, mine, other, 2)
    mine, other, w = lax.optimization_barrier((mine, other, w))
    w = scatter(w, FIRST_GROUPS)
    gram = gram_sum(mine, other)
    w, gram = lax.optimization_barrier((w, gram))
    w = scatter(w, SECOND_GROUPS)
    inverse, loss = inverse_factor(meta, gram, swap_cores(gram))
    q = ortho_left(meta, mine, other, inverse)
    w, inverse, loss, q = lax.optimization_barrier((w, inverse, loss, q))
    block, q = lax.cond(
        loss.reshape(()) <= LOSS_MAX**2, lambda: (solve_rows(w, inverse), q), careful
    )
    right = exchange(jnp.tile(block, (4, 1)), AXES, SECOND_GROUPS)
    right_low = send_first(right, 1)
    right_high = send_first(right, -1)
    sums = block_sums(right)
    sums = sums + sum(shift_z(sums, k) for k in (1, 2, 3))
    parts = [sums] + [send_first(sums, k) for k in (1, 2, 3)]
    right_low, right_high, *parts = lax.optimization_barrier((right_low, right_high, *parts))
    far_a = send_first(right_low[:, :HALF], 1)
    far_b = send_first(right_high[:, HALF:], -1)
    sums = sum(parts)
    sums = [sums, swap_cores(sums)]
    *outs, scaled = apply_three(meta, blended, q, sums, [right, right_low, right_high])
    return tuple(apply_last(meta, blended, q, scaled, [far_a, far_b], outs))


def solution(mesh):
    return jax.shard_map(
        per_device,
        mesh=mesh,
        in_specs=(P("fsdp", "tp"), P("fsdp", "tp"), P()),
        out_specs=(P("fsdp", "tp"), P("fsdp", "tp")),
        check_vma=False,
    )
```

```python
import functools
import math

import jax
import jax.numpy as jnp
from jax import lax
from jax.experimental import pallas as pl
from jax.experimental.pallas import tpu as pltpu
from jax.sharding import PartitionSpec as P

D = 8192
F = 28672
RANK = 512
HALF = RANK // 2
PRIME = 65521
NB = 128
PANEL = 64
STRIP = 16
VMEM_LIMIT = 48 * 1024 * 1024
VMEM_MOST = 57 * 1024 * 1024
VMEM_RIGHT = 52 * 1024 * 1024
F32, BF16 = jnp.float32, jnp.bfloat16
AXES = ("fsdp", "tp")
LOSS_MAX = 2.0


def flat(y, x, z, core):
    return (y * 4 + x) * 8 + z * 2 + core


def everyone():
    return [(y, x, z, c) for y in range(4) for x in range(4) for z in range(4) for c in range(2)]


def shift(along_first, step):
    pairs = []
    for y, x, z, c in everyone():
        if (c == 0) == along_first:
            to = (y, (x + step) % 4, z, c)
        else:
            to = ((y + step) % 4, x, z, c)
        pairs.append((flat(y, x, z, c), flat(*to)))
    return pairs


def send_first(a, step):
    return lax.ppermute(a, AXES, shift(True, step))


def send_second(a, step):
    return lax.ppermute(a, AXES, shift(False, step))


def swap_cores(a):
    return lax.ppermute(a, "tp", [(i, i ^ 1) for i in range(8)])


def shift_z(a, step):
    return lax.ppermute(a, "tp", [(i, (i + 2 * step) % 8) for i in range(8)])


Z_GROUPS = [[c, 2 + c, 4 + c, 6 + c] for c in range(2)]
SECOND_GROUPS = [[flat(y, x, z, 0) for y in range(4)] for x in range(4) for z in range(4)] + [
    [flat(y, x, z, 1) for x in range(4)] for y in range(4) for z in range(4)
]
FIRST_GROUPS = [[flat(y, x, z, 0) for x in range(4)] for y in range(4) for z in range(4)] + [
    [flat(y, x, z, 1) for y in range(4)] for x in range(4) for z in range(4)
]


def exchange(a, axis, groups=None):
    return lax.all_to_all(a, axis, 0, 0, axis_index_groups=groups, tiled=True)


def vmem_spec():
    return pl.BlockSpec(memory_space=pltpu.VMEM)


def smem_spec():
    return pl.BlockSpec(memory_space=pltpu.SMEM)


def params(limit=VMEM_LIMIT):
    return pltpu.CompilerParams(vmem_limit_bytes=limit)


def scatter(a, groups):
    return lax.psum_scatter(
        a, AXES, scatter_dimension=0, axis_index_groups=groups, tiled=True
    )


def sum_kernel(n, copies, a_ref, out_ref):
    rows = a_ref.shape[0] // n
    total = a_ref[:rows, :]
    for k in range(1, n):
        total = total + a_ref[k * rows : (k + 1) * rows, :]
    for k in range(copies):
        out_ref[k * rows : (k + 1) * rows, :] = total


def piece_kernel(a_ref, out_ref, rounded_ref):
    sum_kernel(4, 1, a_ref, out_ref)
    for k in range(4):
        rows = out_ref.shape[0]
        rounded_ref[k * rows : (k + 1) * rows, :] = out_ref[...].astype(BF16)


def sum_piece(a):
    rows, cols = a.shape
    return pl.pallas_call(
        piece_kernel,
        out_shape=(
            jax.ShapeDtypeStruct((rows // 4, cols), F32),
            jax.ShapeDtypeStruct((rows, cols), BF16),
        ),
        in_specs=[vmem_spec()],
        out_specs=(vmem_spec(), vmem_spec()),
        compiler_params=params(),
        name="sum_piece",
    )(a)


def sum_parts(a, n, copies):
    rows, cols = a.shape
    return pl.pallas_call(
        functools.partial(sum_kernel, n, copies),
        out_shape=jax.ShapeDtypeStruct((rows // n * copies, cols), a.dtype),
        in_specs=[vmem_spec()],
        out_specs=vmem_spec(),
        compiler_params=params(),
        name="sum_parts",
    )(a)


def dot(a, b, ca, cb, precision=None):
    return lax.dot_general(
        a, b, (((ca,), (cb,)), ((), ())), precision=precision, preferred_element_type=F32
    )


def exact(a, b, ca, cb):
    return dot(a, b, ca, cb, lax.Precision.HIGHEST)


def two_terms(a):
    top = a.astype(BF16)
    return top, (a.astype(F32) - top.astype(F32)).astype(BF16)


def product(a, b, ca, cb):
    return dot(a, b, ca, cb) if a.dtype == BF16 else exact(a, b, ca, cb)


def fold(v):
    return v - (v >> 16) * PRIME


def wrap(v):
    return jnp.where(v >= PRIME, v - PRIME, v)


def start_value(a):
    low = a & 32767
    low = wrap(fold(fold(low * low + 7))) & 32767
    third = fold(low * low + a).astype(F32)
    third = third - jnp.floor(third * (1.0 / PRIME) + 0.5 / PRIME) * PRIME
    scale = math.sqrt(12.0 / F)
    return third * (scale / PRIME) - 0.5 * scale


INVERSE = pow(9973, -1, PRIME)
ROW = INVERSE * 40503 % PRIME
TABLE = 520
UNROLL = 8
TILE = 1792


def build_table(table):
    rows = lax.broadcasted_iota(jnp.int32, (8, 128), 0)
    cols = lax.broadcasted_iota(jnp.int32, (8, 128), 1)
    base = wrap(fold(fold(cols * 9973 + rows * 40503)))

    def step(i, offset):
        for k in range(UNROLL):
            table[i * UNROLL + k] = start_value(wrap(base + offset))
            offset = wrap(offset + 9973 * 128 % PRIME)
        return offset

    lax.fori_loop(0, TABLE // UNROLL, step, jnp.int32(0))


def left_kernel(meta_ref, m_ref, g_ref, b_ref, keep_ref, send_ref, acc, table, start):
    t = pl.program_id(0)
    core, tp, seed = meta_ref[0], meta_ref[1], lax.rem(meta_ref[2], PRIME)

    @pl.when(t == 0)
    def _():
        build_table(table)

    window = lax.rem(lax.rem(INVERSE * (seed >> 8), PRIME) * 256 + INVERSE * (seed & 255), PRIME)
    window += lax.rem(tp * (ROW * 3584 % PRIME), PRIME) + lax.rem(t * (ROW * TILE % PRIME), PRIME)
    window = lax.rem(window, PRIME)
    lanes = lax.broadcasted_iota(jnp.int32, (8, 128), 1)
    for i in range(0, TILE, 16):
        groups = []
        for _ in range(2):
            part, whole = window & 127, window >> 7
            turned = [pltpu.roll(table[whole + k], (128 - part) & 127, 1) for k in range(5)]
            first = lanes < 128 - part
            groups.append([jnp.where(first, turned[k], turned[k + 1]) for k in range(4)])
            window = wrap(window + ROW * 8 % PRIME)
        for k in range(4):
            rows = jnp.concatenate([groups[0][k], groups[1][k]], axis=0)
            start[i : i + 16, k * 128 : (k + 1) * 128] = rows.astype(BF16)
    b = (m_ref[...].astype(F32) + g_ref[...].astype(F32)).astype(BF16)
    b_ref[...] = b
    part = dot(b, start[...], 1, 0)

    @pl.when(t == 0)
    def _():
        acc[...] = part

    @pl.when(t == pl.num_programs(0) - 1)
    def _():
        acc[...] += part
        keep_ref[...] = acc[pl.ds(pl.multiple_of(core * HALF, HALF), HALF), :]
        send_ref[...] = acc[pl.ds(pl.multiple_of((1 - core) * HALF, HALF), HALF), :]


def left_partial(meta, momentum, gradient):
    rows, cols = momentum.shape
    half = jax.ShapeDtypeStruct((HALF, RANK), F32)
    whole = pl.BlockSpec((HALF, RANK), lambda t: (0, 0))
    tile = pl.BlockSpec((rows, TILE), lambda t: (0, t))
    return pl.pallas_call(
        left_kernel,
        grid=(2,),
        out_shape=(jax.ShapeDtypeStruct((rows, cols), BF16), half, half),
        in_specs=[smem_spec(), tile, tile],
        out_specs=(tile, whole, whole),
        scratch_shapes=[
            pltpu.VMEM((rows, RANK), F32),
            pltpu.VMEM((TABLE, 8, 128), F32),
            pltpu.VMEM((TILE, RANK), BF16),
        ],
        compiler_params=params(VMEM_MOST),
        name="left_partial",
    )(meta, momentum, gradient)


GRAM_SHARE = (((0, 512, 0, 128), (128, 256, 128, 256)), ((256, 512, 128, 384), (384, 512, 384, 512)))


def gram_blocks(core):
    return [
        (i, j)
        for r0, r1, c0, c1 in GRAM_SHARE[core]
        for i in range(r0, r1, NB)
        for j in range(c0, c1, NB)
    ]


def gram_kernel(meta_ref, mine_ref, other_ref, out_ref):
    for core in range(2):

        @pl.when(meta_ref[0] == core)
        def _():
            k = 0
            for r0, r1, c0, c1 in GRAM_SHARE[core]:
                g = product(mine_ref[:, r0:r1], mine_ref[:, c0:c1], 0, 0) + product(
                    other_ref[:, r0:r1], other_ref[:, c0:c1], 0, 0
                )
                for i in range(0, r1 - r0, NB):
                    for j in range(0, c1 - c0, NB):
                        out_ref[k * NB : (k + 1) * NB, :] = g[i : i + NB, j : j + NB]
                        k += 1


def gram_share(meta, mine, other):
    return pl.pallas_call(
        gram_kernel,
        out_shape=jax.ShapeDtypeStruct((5 * NB, NB), F32),
        in_specs=[smem_spec(), vmem_spec(), vmem_spec()],
        out_specs=vmem_spec(),
        compiler_params=params(),
        name="gram_share",
    )(meta, mine, other)


def right_kernel(meta_ref, b_ref, mine_ref, other_ref, out_ref, split):
    terms = split.shape[1] // RANK

    @pl.when(pl.program_id(0) == 0)
    def _():
        core = meta_ref[0]
        for ref, place in ((mine_ref, core), (other_ref, 1 - core)):
            rows = pl.ds(pl.multiple_of(place * HALF, HALF), HALF)
            for k, term in enumerate(two_terms(ref[...])[:terms]):
                split[rows, k * RANK : (k + 1) * RANK] = term

    w = dot(b_ref[...], split[...], 0, 0)
    out_ref[...] = sum(w[:, k * RANK : (k + 1) * RANK] for k in range(terms)).astype(out_ref.dtype)


def right_partial(meta, blended, mine, other, steps):
    rows, cols = blended.shape
    block = cols // steps
    whole = pl.BlockSpec((HALF, RANK), lambda r: (0, 0))
    terms = 1 if mine.dtype == BF16 else 2
    return pl.pallas_call(
        right_kernel,
        grid=(steps,),
        in_specs=[smem_spec(), pl.BlockSpec((rows, block), lambda r: (0, r)), whole, whole],
        out_specs=pl.BlockSpec((block, RANK), lambda r: (r, 0)),
        scratch_shapes=[pltpu.VMEM((RANK, terms * RANK), BF16)],
        out_shape=jax.ShapeDtypeStruct((cols, RANK), mine.dtype),
        compiler_params=params(VMEM_RIGHT),
        name="right_partial",
    )(meta, blended, mine, other)


def invert_block(ae):
    for top in range(0, NB, PANEL):
        end = top + PANEL
        for k0 in range(top, end, STRIP):
            n = end - k0
            rows = lax.broadcasted_iota(jnp.int32, (n, NB), 0)
            left, right = ae[k0:end, :NB], ae[k0:end, NB:]
            columns = [jnp.broadcast_to(left[:, k0 + c : k0 + c + 1], (n, NB)) for c in range(STRIP)]
            scales = []
            for k in range(STRIP):
                pivot = columns[k][k : k + 1, :]
                scales.append(lax.rsqrt(pivot))
                factor = jnp.where(rows > k, columns[k] * (1.0 / pivot), 0.0)
                for c in range(k + 1, STRIP):
                    columns[c] = columns[c] - factor * columns[c][k : k + 1, :]
                left = left - factor * left[k : k + 1, :]
                right = right - factor * right[k : k + 1, :]
            scale = jnp.concatenate(scales, axis=0)
            ae[k0 : k0 + STRIP, :NB] = left[:STRIP] * scale
            ae[k0 : k0 + STRIP, NB:] = right[:STRIP] * scale
            if n > STRIP:
                ae[k0 + STRIP : end, :NB] = left[STRIP:]
                ae[k0 + STRIP : end, NB:] = right[STRIP:]
        if end < NB:
            done = ae[top:end, :]
            ae[end:, :] = ae[end:, :] - exact(done[:, :NB], done, 0, 0)[end:]


def inverse_kernel(meta_ref, mine_ref, other_ref, out_ref, loss_ref, a, ae, diagonal):
    for core in range(2):
        for share, ref in ((core, mine_ref), (1 - core, other_ref)):

            @pl.when(meta_ref[0] == core)
            def _():
                for k, (i, j) in enumerate(gram_blocks(share)):
                    a[i : i + NB, j : j + NB] = ref[k * NB : (k + 1) * NB, :]

    big = lambda d: lax.broadcasted_iota(jnp.int32, (RANK, RANK), d)
    small = lambda d: lax.broadcasted_iota(jnp.int32, (NB, NB), d)
    out_ref[...] = jnp.where(big(0) == big(1), 1.0, 0.0)
    for lo in range(0, RANK, NB):
        hi = lo + NB
        on = jnp.where(small(0) == small(1), a[lo:hi, lo:hi], 0.0)
        diagonal[:, lo:hi] = jnp.sum(on, axis=0, keepdims=True)

    def block(b, carry):
        diag = pl.ds(pl.multiple_of(b * NB, NB), NB)
        ae[:, :NB] = a[diag, diag]
        ae[:, NB:] = jnp.where(small(0) == small(1), 1.0, 0.0)
        invert_block(ae)
        for k in range(RANK // NB):

            @pl.when(b == k)
            def _():
                lo, hi = k * NB, (k + 1) * NB
                inverse = jnp.where(small(0) >= small(1), ae[:, NB:], 0.0)
                done = exact(inverse, out_ref[lo:hi, :hi], 1, 0)
                out_ref[lo:hi, :hi] = done
                if hi < RANK:
                    below = exact(a[hi:, lo:hi], inverse, 1, 1)
                    a[hi:, hi:] = a[hi:, hi:] - exact(below, below, 1, 1)
                    out_ref[hi:, :hi] = out_ref[hi:, :hi] - exact(below, done, 1, 0)

        return carry

    lax.fori_loop(0, RANK // NB, block, 0)
    out = out_ref[...]
    loss_ref[0, 0] = jnp.max(jnp.sum(out * out * diagonal[...], axis=1, keepdims=True))


def inverse_factor(meta, mine, other):
    return pl.pallas_call(
        inverse_kernel,
        out_shape=(
            jax.ShapeDtypeStruct((RANK, RANK), F32),
            jax.ShapeDtypeStruct((1, 1), F32),
        ),
        in_specs=[smem_spec(), vmem_spec(), vmem_spec()],
        out_specs=(vmem_spec(), smem_spec()),
        scratch_shapes=[
            pltpu.VMEM((RANK, RANK), F32),
            pltpu.VMEM((NB, 2 * NB), F32),
            pltpu.VMEM((1, RANK), F32),
        ],
        compiler_params=params(),
        cost_estimate=pl.CostEstimate(flops=0, bytes_accessed=70_000_000, transcendentals=0),
        name="inverse_factor",
    )(meta, mine, other)


def solve(a, inv_ref):
    if a.dtype == BF16:
        top, rest = two_terms(inv_ref[...])
        return (dot(a, top, 1, 1) + dot(a, rest, 1, 1)).astype(BF16)
    return exact(a, inv_ref[...], 1, 1).astype(BF16)


def solve_kernel(w_ref, inv_ref, out_ref):
    out_ref[...] = solve(w_ref[...], inv_ref)


def solve_rows(w, inverse):
    return pl.pallas_call(
        solve_kernel,
        out_shape=jax.ShapeDtypeStruct(w.shape, BF16),
        in_specs=[vmem_spec()] * 2,
        out_specs=vmem_spec(),
        compiler_params=params(),
        name="solve_rows",
    )(w, inverse)


def ortho_kernel(meta_ref, mine_ref, other_ref, inv_ref, out_ref):
    for ref, place in ((mine_ref, meta_ref[0]), (other_ref, 1 - meta_ref[0])):
        rows = pl.ds(pl.multiple_of(place * HALF, HALF), HALF)
        out_ref[rows, :] = solve(ref[...], inv_ref)


def ortho_left(meta, mine, other, inverse):
    return pl.pallas_call(
        ortho_kernel,
        out_shape=jax.ShapeDtypeStruct((RANK, RANK), BF16),
        in_specs=[smem_spec()] + [vmem_spec()] * 3,
        out_specs=vmem_spec(),
        compiler_params=params(),
        name="ortho_left",
    )(meta, mine, other, inverse)


def apply_both(b, q, scaled, right):
    feedback = dot(q, right, 1, 1)
    return (b.astype(F32) - 0.05 * feedback).astype(BF16), dot(scaled, right, 1, 1).astype(BF16)


def apply_kernel(meta_ref, b_ref, q_ref, sums_ref, swapped_ref, *refs):
    rights, (m_ref, u_ref, scaled_ref) = refs[:3], refs[3:]
    i, j = pl.program_id(0), pl.program_id(1)

    @pl.when((i == 0) & (j == 0))
    def _():
        sums = sums_ref[0:1, :] + swapped_ref[0:1, :]
        scale = lax.rsqrt(sums + 1e-6) * math.sqrt(D * F / RANK)
        scaled_ref[...] = (q_ref[...].astype(F32) * scale).astype(BF16)

    tile = m_ref.shape[0]
    rows = pl.ds(pl.multiple_of(j * tile, tile), tile)
    for k in range(3):

        @pl.when(i == k)
        def _():
            m_ref[...], u_ref[...] = apply_both(
                b_ref[...], q_ref[rows, :], scaled_ref[rows, :], rights[k][...]
            )


def apply_three(meta, blended, q, sums, rights):
    rows, cols = blended.shape

    tiles = 2

    def place(i, j, meta_ref):
        offset = jnp.where(i == 0, 0, jnp.where(i == 1, 3, 1))
        return (j, (meta_ref[3] + offset) % 4)

    here = pl.BlockSpec((rows // tiles, cols // 4), place)
    whole = lambda a: pl.BlockSpec(a.shape, lambda i, j, meta_ref: (0, 0))
    shape = jax.ShapeDtypeStruct((rows, cols), BF16)
    square = jax.ShapeDtypeStruct((rows, RANK), BF16)
    rest = [q] + sums + rights
    return pl.pallas_call(
        apply_kernel,
        grid_spec=pltpu.PrefetchScalarGridSpec(
            num_scalar_prefetch=1,
            grid=(3, tiles),
            in_specs=[here] + [whole(a) for a in rest],
            out_specs=[here, here, whole(square)],
        ),
        out_shape=[shape, shape, square],
        compiler_params=params(),
        name="apply_three",
    )(meta, blended, *rest)


def last_kernel(meta_ref, b_ref, q_ref, scaled_ref, a_ref, c_ref, m_in, u_in, m_ref, u_ref):
    q, scaled = q_ref[...], scaled_ref[...]
    feedback = dot(q[:, :HALF], a_ref[...], 1, 1) + dot(q[:, HALF:], c_ref[...], 1, 1)
    direction = dot(scaled[:, :HALF], a_ref[...], 1, 1) + dot(scaled[:, HALF:], c_ref[...], 1, 1)
    m_ref[...] = (b_ref[...].astype(F32) - 0.05 * feedback).astype(BF16)
    u_ref[...] = direction.astype(BF16)


def apply_last(meta, blended, q, scaled, rights, outs):
    rows, cols = blended.shape
    tiles = 2
    here = pl.BlockSpec(
        (rows // tiles, cols // 4), lambda i, meta_ref: (i, (meta_ref[3] + 2) % 4)
    )
    part = pl.BlockSpec((rows // tiles, RANK), lambda i, meta_ref: (i, 0))
    whole = pl.BlockSpec((cols // 4, HALF), lambda i, meta_ref: (0, 0))
    kept = pl.BlockSpec(memory_space=pl.ANY)
    shape = jax.ShapeDtypeStruct((rows, cols), BF16)
    return pl.pallas_call(
        last_kernel,
        grid_spec=pltpu.PrefetchScalarGridSpec(
            num_scalar_prefetch=1,
            grid=(tiles,),
            in_specs=[here, part, part, whole, whole, kept, kept],
            out_specs=[here, here],
        ),
        out_shape=[shape, shape],
        input_output_aliases={6: 0, 7: 1},
        compiler_params=params(),
        name="apply_last",
    )(meta, blended, q, scaled, *rights, *outs)


def sums_kernel(r_ref, out_ref):
    r = r_ref[...].astype(F32)
    out_ref[...] = jnp.broadcast_to(jnp.sum(r * r, axis=0, keepdims=True), out_ref.shape)


def block_sums(r):
    return pl.pallas_call(
        sums_kernel,
        out_shape=jax.ShapeDtypeStruct((8, RANK), F32),
        in_specs=[vmem_spec()],
        out_specs=vmem_spec(),
        compiler_params=params(),
        name="block_sums",
    )(r)


def per_device(momentum, gradient, seed_value):
    fsdp, tp = lax.axis_index("fsdp"), lax.axis_index("tp")
    core, x, y = tp % 2, fsdp % 4, fsdp // 4
    first, second = jnp.where(core == 0, x, y), jnp.where(core == 0, y, x)
    meta = jnp.stack([core, tp, seed_value[0], first, second]).astype(jnp.int32)

    blended, keep, send = left_partial(meta, momentum, gradient)
    half = keep + swap_cores(send)
    piece, rounded = sum_piece(exchange(half, "tp", Z_GROUPS))

    def gram_sum(mine, other):
        gram = exchange(gram_share(meta, mine, other), "fsdp")
        return exchange(sum_parts(gram, 16, 16), "fsdp")

    def careful():
        mine = exchange(jnp.tile(piece, (4, 1)), "tp", Z_GROUPS)
        other = swap_cores(mine)
        gram = gram_sum(mine, other)
        inverse, _ = inverse_factor(meta, gram, swap_cores(gram))
        w = right_partial(meta, blended, mine, other, 4)
        w = scatter(scatter(w, FIRST_GROUPS), SECOND_GROUPS)
        return solve_rows(w, inverse), ortho_left(meta, mine, other, inverse)

    mine = exchange(rounded, "tp", Z_GROUPS)
    other = swap_cores(mine)
    w = right_partial(meta, blended, mine, other, 2)
    mine, other, w = lax.optimization_barrier((mine, other, w))
    w = scatter(w, FIRST_GROUPS)
    gram = gram_sum(mine, other)
    w, gram = lax.optimization_barrier((w, gram))
    w = scatter(w, SECOND_GROUPS)
    inverse, loss = inverse_factor(meta, gram, swap_cores(gram))
    q = ortho_left(meta, mine, other, inverse)
    w, inverse, loss, q = lax.optimization_barrier((w, inverse, loss, q))
    block, q = lax.cond(
        loss.reshape(()) <= LOSS_MAX**2, lambda: (solve_rows(w, inverse), q), careful
    )
    right = exchange(jnp.tile(block, (4, 1)), AXES, SECOND_GROUPS)
    right_low = send_first(right, 1)
    right_high = send_first(right, -1)
    sums = block_sums(right)
    sums = sums + sum(shift_z(sums, k) for k in (1, 2, 3))
    parts = [sums] + [send_first(sums, k) for k in (1, 2, 3)]
    right_low, right_high, *parts = lax.optimization_barrier((right_low, right_high, *parts))
    far_a = send_first(right_low[:, :HALF], 1)
    far_b = send_first(right_high[:, HALF:], -1)
    sums = sum(parts)
    sums = [sums, swap_cores(sums)]
    *outs, scaled = apply_three(meta, blended, q, sums, [right, right_low, right_high])
    return tuple(apply_last(meta, blended, q, scaled, [far_a, far_b], outs))


def solution(mesh):
    return jax.shard_map(
        per_device,
        mesh=mesh,
        in_specs=(P("fsdp", "tp"), P("fsdp", "tp"), P()),
        out_specs=(P("fsdp", "tp"), P("fsdp", "tp")),
        check_vma=False,
    )
```

```python
import functools
import math

import jax
import jax.numpy as jnp
from jax import lax
from jax.experimental import pallas as pl
from jax.experimental.pallas import tpu as pltpu
from jax.sharding import PartitionSpec as P

D = 8192
F = 28672
RANK = 512
HALF = RANK // 2
PRIME = 65521
NB = 128
PANEL = 64
STRIP = 16
VMEM_LIMIT = 48 * 1024 * 1024
VMEM_MOST = 57 * 1024 * 1024
VMEM_RIGHT = 52 * 1024 * 1024
F32, BF16 = jnp.float32, jnp.bfloat16
AXES = ("fsdp", "tp")
LOSS_MAX = 0.0


def flat(y, x, z, core):
    return (y * 4 + x) * 8 + z * 2 + core


def everyone():
    return [(y, x, z, c) for y in range(4) for x in range(4) for z in range(4) for c in range(2)]


def shift(along_first, step):
    pairs = []
    for y, x, z, c in everyone():
        if (c == 0) == along_first:
            to = (y, (x + step) % 4, z, c)
        else:
            to = ((y + step) % 4, x, z, c)
        pairs.append((flat(y, x, z, c), flat(*to)))
    return pairs


def send_first(a, step):
    return lax.ppermute(a, AXES, shift(True, step))


def send_second(a, step):
    return lax.ppermute(a, AXES, shift(False, step))


def swap_cores(a):
    return lax.ppermute(a, "tp", [(i, i ^ 1) for i in range(8)])


def shift_z(a, step):
    return lax.ppermute(a, "tp", [(i, (i + 2 * step) % 8) for i in range(8)])


Z_GROUPS = [[c, 2 + c, 4 + c, 6 + c] for c in range(2)]
SECOND_GROUPS = [[flat(y, x, z, 0) for y in range(4)] for x in range(4) for z in range(4)] + [
    [flat(y, x, z, 1) for x in range(4)] for y in range(4) for z in range(4)
]
FIRST_GROUPS = [[flat(y, x, z, 0) for x in range(4)] for y in range(4) for z in range(4)] + [
    [flat(y, x, z, 1) for y in range(4)] for x in range(4) for z in range(4)
]


def exchange(a, axis, groups=None):
    return lax.all_to_all(a, axis, 0, 0, axis_index_groups=groups, tiled=True)


def vmem_spec():
    return pl.BlockSpec(memory_space=pltpu.VMEM)


def smem_spec():
    return pl.BlockSpec(memory_space=pltpu.SMEM)


def params(limit=VMEM_LIMIT):
    return pltpu.CompilerParams(vmem_limit_bytes=limit)


def scatter(a, groups):
    return lax.psum_scatter(
        a, AXES, scatter_dimension=0, axis_index_groups=groups, tiled=True
    )


def sum_kernel(n, copies, a_ref, out_ref):
    rows = a_ref.shape[0] // n
    total = a_ref[:rows, :]
    for k in range(1, n):
        total = total + a_ref[k * rows : (k + 1) * rows, :]
    for k in range(copies):
        out_ref[k * rows : (k + 1) * rows, :] = total


def piece_kernel(a_ref, out_ref, rounded_ref):
    sum_kernel(4, 1, a_ref, out_ref)
    for k in range(4):
        rows = out_ref.shape[0]
        rounded_ref[k * rows : (k + 1) * rows, :] = out_ref[...].astype(BF16)


def sum_piece(a):
    rows, cols = a.shape
    return pl.pallas_call(
        piece_kernel,
        out_shape=(
            jax.ShapeDtypeStruct((rows // 4, cols), F32),
            jax.ShapeDtypeStruct((rows, cols), BF16),
        ),
        in_specs=[vmem_spec()],
        out_specs=(vmem_spec(), vmem_spec()),
        compiler_params=params(),
        name="sum_piece",
    )(a)


def sum_parts(a, n, copies):
    rows, cols = a.shape
    return pl.pallas_call(
        functools.partial(sum_kernel, n, copies),
        out_shape=jax.ShapeDtypeStruct((rows // n * copies, cols), a.dtype),
        in_specs=[vmem_spec()],
        out_specs=vmem_spec(),
        compiler_params=params(),
        name="sum_parts",
    )(a)


def dot(a, b, ca, cb, precision=None):
    return lax.dot_general(
        a, b, (((ca,), (cb,)), ((), ())), precision=precision, preferred_element_type=F32
    )


def exact(a, b, ca, cb):
    return dot(a, b, ca, cb, lax.Precision.HIGHEST)


def two_terms(a):
    top = a.astype(BF16)
    return top, (a.astype(F32) - top.astype(F32)).astype(BF16)


def product(a, b, ca, cb):
    return dot(a, b, ca, cb) if a.dtype == BF16 else exact(a, b, ca, cb)


def fold(v):
    return v - (v >> 16) * PRIME


def wrap(v):
    return jnp.where(v >= PRIME, v - PRIME, v)


def start_value(a):
    low = a & 32767
    low = wrap(fold(fold(low * low + 7))) & 32767
    third = fold(low * low + a).astype(F32)
    third = third - jnp.floor(third * (1.0 / PRIME) + 0.5 / PRIME) * PRIME
    scale = math.sqrt(12.0 / F)
    return third * (scale / PRIME) - 0.5 * scale


INVERSE = pow(9973, -1, PRIME)
ROW = INVERSE * 40503 % PRIME
TABLE = 520
UNROLL = 8
TILE = 1792


def build_table(table):
    rows = lax.broadcasted_iota(jnp.int32, (8, 128), 0)
    cols = lax.broadcasted_iota(jnp.int32, (8, 128), 1)
    base = wrap(fold(fold(cols * 9973 + rows * 40503)))

    def step(i, offset):
        for k in range(UNROLL):
            table[i * UNROLL + k] = start_value(wrap(base + offset))
            offset = wrap(offset + 9973 * 128 % PRIME)
        return offset

    lax.fori_loop(0, TABLE // UNROLL, step, jnp.int32(0))


def left_kernel(meta_ref, m_ref, g_ref, b_ref, keep_ref, send_ref, acc, table, start):
    t = pl.program_id(0)
    core, tp, seed = meta_ref[0], meta_ref[1], lax.rem(meta_ref[2], PRIME)

    @pl.when(t == 0)
    def _():
        build_table(table)

    window = lax.rem(lax.rem(INVERSE * (seed >> 8), PRIME) * 256 + INVERSE * (seed & 255), PRIME)
    window += lax.rem(tp * (ROW * 3584 % PRIME), PRIME) + lax.rem(t * (ROW * TILE % PRIME), PRIME)
    window = lax.rem(window, PRIME)
    lanes = lax.broadcasted_iota(jnp.int32, (8, 128), 1)
    for i in range(0, TILE, 16):
        groups = []
        for _ in range(2):
            part, whole = window & 127, window >> 7
            turned = [pltpu.roll(table[whole + k], (128 - part) & 127, 1) for k in range(5)]
            first = lanes < 128 - part
            groups.append([jnp.where(first, turned[k], turned[k + 1]) for k in range(4)])
            window = wrap(window + ROW * 8 % PRIME)
        for k in range(4):
            rows = jnp.concatenate([groups[0][k], groups[1][k]], axis=0)
            start[i : i + 16, k * 128 : (k + 1) * 128] = rows.astype(BF16)
    b = (m_ref[...].astype(F32) + g_ref[...].astype(F32)).astype(BF16)
    b_ref[...] = b
    part = dot(b, start[...], 1, 0)

    @pl.when(t == 0)
    def _():
        acc[...] = part

    @pl.when(t == pl.num_programs(0) - 1)
    def _():
        acc[...] += part
        keep_ref[...] = acc[pl.ds(pl.multiple_of(core * HALF, HALF), HALF), :]
        send_ref[...] = acc[pl.ds(pl.multiple_of((1 - core) * HALF, HALF), HALF), :]


def left_partial(meta, momentum, gradient):
    rows, cols = momentum.shape
    half = jax.ShapeDtypeStruct((HALF, RANK), F32)
    whole = pl.BlockSpec((HALF, RANK), lambda t: (0, 0))
    tile = pl.BlockSpec((rows, TILE), lambda t: (0, t))
    return pl.pallas_call(
        left_kernel,
        grid=(2,),
        out_shape=(jax.ShapeDtypeStruct((rows, cols), BF16), half, half),
        in_specs=[smem_spec(), tile, tile],
        out_specs=(tile, whole, whole),
        scratch_shapes=[
            pltpu.VMEM((rows, RANK), F32),
            pltpu.VMEM((TABLE, 8, 128), F32),
            pltpu.VMEM((TILE, RANK), BF16),
        ],
        compiler_params=params(VMEM_MOST),
        name="left_partial",
    )(meta, momentum, gradient)


GRAM_SHARE = (((0, 512, 0, 128), (128, 256, 128, 256)), ((256, 512, 128, 384), (384, 512, 384, 512)))


def gram_blocks(core):
    return [
        (i, j)
        for r0, r1, c0, c1 in GRAM_SHARE[core]
        for i in range(r0, r1, NB)
        for j in range(c0, c1, NB)
    ]


def gram_kernel(meta_ref, mine_ref, other_ref, out_ref):
    for core in range(2):

        @pl.when(meta_ref[0] == core)
        def _():
            k = 0
            for r0, r1, c0, c1 in GRAM_SHARE[core]:
                g = product(mine_ref[:, r0:r1], mine_ref[:, c0:c1], 0, 0) + product(
                    other_ref[:, r0:r1], other_ref[:, c0:c1], 0, 0
                )
                for i in range(0, r1 - r0, NB):
                    for j in range(0, c1 - c0, NB):
                        out_ref[k * NB : (k + 1) * NB, :] = g[i : i + NB, j : j + NB]
                        k += 1


def gram_share(meta, mine, other):
    return pl.pallas_call(
        gram_kernel,
        out_shape=jax.ShapeDtypeStruct((5 * NB, NB), F32),
        in_specs=[smem_spec(), vmem_spec(), vmem_spec()],
        out_specs=vmem_spec(),
        compiler_params=params(),
        name="gram_share",
    )(meta, mine, other)


def right_kernel(meta_ref, b_ref, mine_ref, other_ref, out_ref, split):
    terms = split.shape[1] // RANK

    @pl.when(pl.program_id(0) == 0)
    def _():
        core = meta_ref[0]
        for ref, place in ((mine_ref, core), (other_ref, 1 - core)):
            rows = pl.ds(pl.multiple_of(place * HALF, HALF), HALF)
            for k, term in enumerate(two_terms(ref[...])[:terms]):
                split[rows, k * RANK : (k + 1) * RANK] = term

    w = dot(b_ref[...], split[...], 0, 0)
    out_ref[...] = sum(w[:, k * RANK : (k + 1) * RANK] for k in range(terms)).astype(out_ref.dtype)


def right_partial(meta, blended, mine, other, steps):
    rows, cols = blended.shape
    block = cols // steps
    whole = pl.BlockSpec((HALF, RANK), lambda r: (0, 0))
    terms = 1 if mine.dtype == BF16 else 2
    return pl.pallas_call(
        right_kernel,
        grid=(steps,),
        in_specs=[smem_spec(), pl.BlockSpec((rows, block), lambda r: (0, r)), whole, whole],
        out_specs=pl.BlockSpec((block, RANK), lambda r: (r, 0)),
        scratch_shapes=[pltpu.VMEM((RANK, terms * RANK), BF16)],
        out_shape=jax.ShapeDtypeStruct((cols, RANK), mine.dtype),
        compiler_params=params(VMEM_RIGHT),
        name="right_partial",
    )(meta, blended, mine, other)


def invert_block(ae):
    for top in range(0, NB, PANEL):
        end = top + PANEL
        for k0 in range(top, end, STRIP):
            n = end - k0
            rows = lax.broadcasted_iota(jnp.int32, (n, NB), 0)
            left, right = ae[k0:end, :NB], ae[k0:end, NB:]
            columns = [jnp.broadcast_to(left[:, k0 + c : k0 + c + 1], (n, NB)) for c in range(STRIP)]
            scales = []
            for k in range(STRIP):
                pivot = columns[k][k : k + 1, :]
                scales.append(lax.rsqrt(pivot))
                factor = jnp.where(rows > k, columns[k] * (1.0 / pivot), 0.0)
                for c in range(k + 1, STRIP):
                    columns[c] = columns[c] - factor * columns[c][k : k + 1, :]
                left = left - factor * left[k : k + 1, :]
                right = right - factor * right[k : k + 1, :]
            scale = jnp.concatenate(scales, axis=0)
            ae[k0 : k0 + STRIP, :NB] = left[:STRIP] * scale
            ae[k0 : k0 + STRIP, NB:] = right[:STRIP] * scale
            if n > STRIP:
                ae[k0 + STRIP : end, :NB] = left[STRIP:]
                ae[k0 + STRIP : end, NB:] = right[STRIP:]
        if end < NB:
            done = ae[top:end, :]
            ae[end:, :] = ae[end:, :] - exact(done[:, :NB], done, 0, 0)[end:]


def inverse_kernel(meta_ref, mine_ref, other_ref, out_ref, loss_ref, a, ae, diagonal):
    for core in range(2):
        for share, ref in ((core, mine_ref), (1 - core, other_ref)):

            @pl.when(meta_ref[0] == core)
            def _():
                for k, (i, j) in enumerate(gram_blocks(share)):
                    a[i : i + NB, j : j + NB] = ref[k * NB : (k + 1) * NB, :]

    big = lambda d: lax.broadcasted_iota(jnp.int32, (RANK, RANK), d)
    small = lambda d: lax.broadcasted_iota(jnp.int32, (NB, NB), d)
    out_ref[...] = jnp.where(big(0) == big(1), 1.0, 0.0)
    for lo in range(0, RANK, NB):
        hi = lo + NB
        on = jnp.where(small(0) == small(1), a[lo:hi, lo:hi], 0.0)
        diagonal[:, lo:hi] = jnp.sum(on, axis=0, keepdims=True)

    def block(b, carry):
        diag = pl.ds(pl.multiple_of(b * NB, NB), NB)
        ae[:, :NB] = a[diag, diag]
        ae[:, NB:] = jnp.where(small(0) == small(1), 1.0, 0.0)
        invert_block(ae)
        for k in range(RANK // NB):

            @pl.when(b == k)
            def _():
                lo, hi = k * NB, (k + 1) * NB
                inverse = jnp.where(small(0) >= small(1), ae[:, NB:], 0.0)
                done = exact(inverse, out_ref[lo:hi, :hi], 1, 0)
                out_ref[lo:hi, :hi] = done
                if hi < RANK:
                    below = exact(a[hi:, lo:hi], inverse, 1, 1)
                    a[hi:, hi:] = a[hi:, hi:] - exact(below, below, 1, 1)
                    out_ref[hi:, :hi] = out_ref[hi:, :hi] - exact(below, done, 1, 0)

        return carry

    lax.fori_loop(0, RANK // NB, block, 0)
    out = out_ref[...]
    loss_ref[0, 0] = jnp.max(jnp.sum(out * out * diagonal[...], axis=1, keepdims=True))


def inverse_factor(meta, mine, other):
    return pl.pallas_call(
        inverse_kernel,
        out_shape=(
            jax.ShapeDtypeStruct((RANK, RANK), F32),
            jax.ShapeDtypeStruct((1, 1), F32),
        ),
        in_specs=[smem_spec(), vmem_spec(), vmem_spec()],
        out_specs=(vmem_spec(), smem_spec()),
        scratch_shapes=[
            pltpu.VMEM((RANK, RANK), F32),
            pltpu.VMEM((NB, 2 * NB), F32),
            pltpu.VMEM((1, RANK), F32),
        ],
        compiler_params=params(),
        cost_estimate=pl.CostEstimate(flops=0, bytes_accessed=70_000_000, transcendentals=0),
        name="inverse_factor",
    )(meta, mine, other)


def solve(a, inv_ref):
    if a.dtype == BF16:
        top, rest = two_terms(inv_ref[...])
        return (dot(a, top, 1, 1) + dot(a, rest, 1, 1)).astype(BF16)
    return exact(a, inv_ref[...], 1, 1).astype(BF16)


def solve_kernel(w_ref, inv_ref, out_ref):
    out_ref[...] = solve(w_ref[...], inv_ref)


def solve_rows(w, inverse):
    return pl.pallas_call(
        solve_kernel,
        out_shape=jax.ShapeDtypeStruct(w.shape, BF16),
        in_specs=[vmem_spec()] * 2,
        out_specs=vmem_spec(),
        compiler_params=params(),
        name="solve_rows",
    )(w, inverse)


def ortho_kernel(meta_ref, mine_ref, other_ref, inv_ref, out_ref):
    for ref, place in ((mine_ref, meta_ref[0]), (other_ref, 1 - meta_ref[0])):
        rows = pl.ds(pl.multiple_of(place * HALF, HALF), HALF)
        out_ref[rows, :] = solve(ref[...], inv_ref)


def ortho_left(meta, mine, other, inverse):
    return pl.pallas_call(
        ortho_kernel,
        out_shape=jax.ShapeDtypeStruct((RANK, RANK), BF16),
        in_specs=[smem_spec()] + [vmem_spec()] * 3,
        out_specs=vmem_spec(),
        compiler_params=params(),
        name="ortho_left",
    )(meta, mine, other, inverse)


def apply_both(b, q, scaled, right):
    feedback = dot(q, right, 1, 1)
    return (b.astype(F32) - 0.05 * feedback).astype(BF16), dot(scaled, right, 1, 1).astype(BF16)


def apply_kernel(meta_ref, b_ref, q_ref, sums_ref, swapped_ref, *refs):
    rights, (m_ref, u_ref, scaled_ref) = refs[:3], refs[3:]
    i, j = pl.program_id(0), pl.program_id(1)

    @pl.when((i == 0) & (j == 0))
    def _():
        sums = sums_ref[0:1, :] + swapped_ref[0:1, :]
        scale = lax.rsqrt(sums + 1e-6) * math.sqrt(D * F / RANK)
        scaled_ref[...] = (q_ref[...].astype(F32) * scale).astype(BF16)

    tile = m_ref.shape[0]
    rows = pl.ds(pl.multiple_of(j * tile, tile), tile)
    for k in range(3):

        @pl.when(i == k)
        def _():
            m_ref[...], u_ref[...] = apply_both(
                b_ref[...], q_ref[rows, :], scaled_ref[rows, :], rights[k][...]
            )


def apply_three(meta, blended, q, sums, rights):
    rows, cols = blended.shape

    tiles = 2

    def place(i, j, meta_ref):
        offset = jnp.where(i == 0, 0, jnp.where(i == 1, 3, 1))
        return (j, (meta_ref[3] + offset) % 4)

    here = pl.BlockSpec((rows // tiles, cols // 4), place)
    whole = lambda a: pl.BlockSpec(a.shape, lambda i, j, meta_ref: (0, 0))
    shape = jax.ShapeDtypeStruct((rows, cols), BF16)
    square = jax.ShapeDtypeStruct((rows, RANK), BF16)
    rest = [q] + sums + rights
    return pl.pallas_call(
        apply_kernel,
        grid_spec=pltpu.PrefetchScalarGridSpec(
            num_scalar_prefetch=1,
            grid=(3, tiles),
            in_specs=[here] + [whole(a) for a in rest],
            out_specs=[here, here, whole(square)],
        ),
        out_shape=[shape, shape, square],
        compiler_params=params(),
        name="apply_three",
    )(meta, blended, *rest)


def last_kernel(meta_ref, b_ref, q_ref, scaled_ref, a_ref, c_ref, m_in, u_in, m_ref, u_ref):
    q, scaled = q_ref[...], scaled_ref[...]
    feedback = dot(q[:, :HALF], a_ref[...], 1, 1) + dot(q[:, HALF:], c_ref[...], 1, 1)
    direction = dot(scaled[:, :HALF], a_ref[...], 1, 1) + dot(scaled[:, HALF:], c_ref[...], 1, 1)
    m_ref[...] = (b_ref[...].astype(F32) - 0.05 * feedback).astype(BF16)
    u_ref[...] = direction.astype(BF16)


def apply_last(meta, blended, q, scaled, rights, outs):
    rows, cols = blended.shape
    tiles = 2
    here = pl.BlockSpec(
        (rows // tiles, cols // 4), lambda i, meta_ref: (i, (meta_ref[3] + 2) % 4)
    )
    part = pl.BlockSpec((rows // tiles, RANK), lambda i, meta_ref: (i, 0))
    whole = pl.BlockSpec((cols // 4, HALF), lambda i, meta_ref: (0, 0))
    kept = pl.BlockSpec(memory_space=pl.ANY)
    shape = jax.ShapeDtypeStruct((rows, cols), BF16)
    return pl.pallas_call(
        last_kernel,
        grid_spec=pltpu.PrefetchScalarGridSpec(
            num_scalar_prefetch=1,
            grid=(tiles,),
            in_specs=[here, part, part, whole, whole, kept, kept],
            out_specs=[here, here],
        ),
        out_shape=[shape, shape],
        input_output_aliases={6: 0, 7: 1},
        compiler_params=params(),
        name="apply_last",
    )(meta, blended, q, scaled, *rights, *outs)


def sums_kernel(r_ref, out_ref):
    r = r_ref[...].astype(F32)
    out_ref[...] = jnp.broadcast_to(jnp.sum(r * r, axis=0, keepdims=True), out_ref.shape)


def block_sums(r):
    return pl.pallas_call(
        sums_kernel,
        out_shape=jax.ShapeDtypeStruct((8, RANK), F32),
        in_specs=[vmem_spec()],
        out_specs=vmem_spec(),
        compiler_params=params(),
        name="block_sums",
    )(r)


def per_device(momentum, gradient, seed_value):
    fsdp, tp = lax.axis_index("fsdp"), lax.axis_index("tp")
    core, x, y = tp % 2, fsdp % 4, fsdp // 4
    first, second = jnp.where(core == 0, x, y), jnp.where(core == 0, y, x)
    meta = jnp.stack([core, tp, seed_value[0], first, second]).astype(jnp.int32)

    blended, keep, send = left_partial(meta, momentum, gradient)
    half = keep + swap_cores(send)
    piece, rounded = sum_piece(exchange(half, "tp", Z_GROUPS))

    def gram_sum(mine, other):
        gram = exchange(gram_share(meta, mine, other), "fsdp")
        return exchange(sum_parts(gram, 16, 16), "fsdp")

    def careful():
        mine = exchange(jnp.tile(piece, (4, 1)), "tp", Z_GROUPS)
        other = swap_cores(mine)
        gram = gram_sum(mine, other)
        inverse, _ = inverse_factor(meta, gram, swap_cores(gram))
        w = right_partial(meta, blended, mine, other, 4)
        w = scatter(scatter(w, FIRST_GROUPS), SECOND_GROUPS)
        return solve_rows(w, inverse), ortho_left(meta, mine, other, inverse)

    mine = exchange(rounded, "tp", Z_GROUPS)
    other = swap_cores(mine)
    w = right_partial(meta, blended, mine, other, 2)
    mine, other, w = lax.optimization_barrier((mine, other, w))
    w = scatter(w, FIRST_GROUPS)
    gram = gram_sum(mine, other)
    w, gram = lax.optimization_barrier((w, gram))
    w = scatter(w, SECOND_GROUPS)
    inverse, loss = inverse_factor(meta, gram, swap_cores(gram))
    q = ortho_left(meta, mine, other, inverse)
    w, inverse, loss, q = lax.optimization_barrier((w, inverse, loss, q))
    block, q = lax.cond(
        loss.reshape(()) <= LOSS_MAX**2, lambda: (solve_rows(w, inverse), q), careful
    )
    right = exchange(jnp.tile(block, (4, 1)), AXES, SECOND_GROUPS)
    right_low = send_first(right, 1)
    right_high = send_first(right, -1)
    sums = block_sums(right)
    sums = sums + sum(shift_z(sums, k) for k in (1, 2, 3))
    parts = [sums] + [send_first(sums, k) for k in (1, 2, 3)]
    right_low, right_high, *parts = lax.optimization_barrier((right_low, right_high, *parts))
    far_a = send_first(right_low[:, :HALF], 1)
    far_b = send_first(right_high[:, HALF:], -1)
    sums = sum(parts)
    sums = [sums, swap_cores(sums)]
    *outs, scaled = apply_three(meta, blended, q, sums, [right, right_low, right_high])
    return tuple(apply_last(meta, blended, q, scaled, [far_a, far_b], outs))


def solution(mesh):
    return jax.shard_map(
        per_device,
        mesh=mesh,
        in_specs=(P("fsdp", "tp"), P("fsdp", "tp"), P()),
        out_specs=(P("fsdp", "tp"), P("fsdp", "tp")),
        check_vma=False,
    )
```

```python
import functools
import math

import jax
import jax.numpy as jnp
from jax import lax
from jax.experimental import pallas as pl
from jax.experimental.pallas import tpu as pltpu
from jax.sharding import PartitionSpec as P

D = 8192
F = 28672
RANK = 512
HALF = RANK // 2
PRIME = 65521
NB = 128
PANEL = 64
STRIP = 16
VMEM_LIMIT = 48 * 1024 * 1024
VMEM_MOST = 57 * 1024 * 1024
VMEM_RIGHT = 52 * 1024 * 1024
F32, BF16 = jnp.float32, jnp.bfloat16
AXES = ("fsdp", "tp")
LOSS_MAX = 2.0


def flat(y, x, z, core):
    return (y * 4 + x) * 8 + z * 2 + core


def everyone():
    return [(y, x, z, c) for y in range(4) for x in range(4) for z in range(4) for c in range(2)]


def shift(along_first, step):
    pairs = []
    for y, x, z, c in everyone():
        if (c == 0) == along_first:
            to = (y, (x + step) % 4, z, c)
        else:
            to = ((y + step) % 4, x, z, c)
        pairs.append((flat(y, x, z, c), flat(*to)))
    return pairs


def send_first(a, step):
    return lax.ppermute(a, AXES, shift(True, step))


def send_second(a, step):
    return lax.ppermute(a, AXES, shift(False, step))


def swap_cores(a):
    return lax.ppermute(a, "tp", [(i, i ^ 1) for i in range(8)])


def shift_z(a, step):
    return lax.ppermute(a, "tp", [(i, (i + 2 * step) % 8) for i in range(8)])


Z_GROUPS = [[c, 2 + c, 4 + c, 6 + c] for c in range(2)]
SECOND_GROUPS = [[flat(y, x, z, 0) for y in range(4)] for x in range(4) for z in range(4)] + [
    [flat(y, x, z, 1) for x in range(4)] for y in range(4) for z in range(4)
]
FIRST_GROUPS = [[flat(y, x, z, 0) for x in range(4)] for y in range(4) for z in range(4)] + [
    [flat(y, x, z, 1) for y in range(4)] for x in range(4) for z in range(4)
]


def exchange(a, axis, groups=None):
    return lax.all_to_all(a, axis, 0, 0, axis_index_groups=groups, tiled=True)


def vmem_spec():
    return pl.BlockSpec(memory_space=pltpu.VMEM)


def smem_spec():
    return pl.BlockSpec(memory_space=pltpu.SMEM)


def params(limit=VMEM_LIMIT):
    return pltpu.CompilerParams(vmem_limit_bytes=limit)


def scatter(a, groups):
    return lax.psum_scatter(
        a, AXES, scatter_dimension=0, axis_index_groups=groups, tiled=True
    )


def sum_kernel(n, copies, a_ref, out_ref):
    rows = a_ref.shape[0] // n
    total = a_ref[:rows, :]
    for k in range(1, n):
        total = total + a_ref[k * rows : (k + 1) * rows, :]
    for k in range(copies):
        out_ref[k * rows : (k + 1) * rows, :] = total


def piece_kernel(a_ref, out_ref, rounded_ref):
    sum_kernel(4, 1, a_ref, out_ref)
    for k in range(4):
        rows = out_ref.shape[0]
        rounded_ref[k * rows : (k + 1) * rows, :] = out_ref[...].astype(BF16)


def sum_piece(a):
    rows, cols = a.shape
    return pl.pallas_call(
        piece_kernel,
        out_shape=(
            jax.ShapeDtypeStruct((rows // 4, cols), F32),
            jax.ShapeDtypeStruct((rows, cols), BF16),
        ),
        in_specs=[vmem_spec()],
        out_specs=(vmem_spec(), vmem_spec()),
        compiler_params=params(),
        name="sum_piece",
    )(a)


def sum_parts(a, n, copies):
    rows, cols = a.shape
    return pl.pallas_call(
        functools.partial(sum_kernel, n, copies),
        out_shape=jax.ShapeDtypeStruct((rows // n * copies, cols), a.dtype),
        in_specs=[vmem_spec()],
        out_specs=vmem_spec(),
        compiler_params=params(),
        name="sum_parts",
    )(a)


def dot(a, b, ca, cb, precision=None):
    return lax.dot_general(
        a, b, (((ca,), (cb,)), ((), ())), precision=precision, preferred_element_type=F32
    )


def exact(a, b, ca, cb):
    return dot(a, b, ca, cb, lax.Precision.HIGHEST)


def two_terms(a):
    top = a.astype(BF16)
    return top, (a.astype(F32) - top.astype(F32)).astype(BF16)


def product(a, b, ca, cb):
    return dot(a, b, ca, cb) if a.dtype == BF16 else exact(a, b, ca, cb)


def fold(v):
    return v - (v >> 16) * PRIME


def wrap(v):
    return jnp.where(v >= PRIME, v - PRIME, v)


def start_value(a):
    low = a & 32767
    low = wrap(fold(fold(low * low + 7))) & 32767
    third = fold(low * low + a).astype(F32)
    third = third - jnp.floor(third * (1.0 / PRIME) + 0.5 / PRIME) * PRIME
    scale = math.sqrt(12.0 / F)
    return third * (scale / PRIME) - 0.5 * scale


INVERSE = pow(9973, -1, PRIME)
ROW = INVERSE * 40503 % PRIME
TABLE = 520
UNROLL = 8
TILE = 1792


def build_table(table):
    rows = lax.broadcasted_iota(jnp.int32, (8, 128), 0)
    cols = lax.broadcasted_iota(jnp.int32, (8, 128), 1)
    base = wrap(fold(fold(cols * 9973 + rows * 40503)))

    def step(i, offset):
        for k in range(UNROLL):
            table[i * UNROLL + k] = start_value(wrap(base + offset))
            offset = wrap(offset + 9973 * 128 % PRIME)
        return offset

    lax.fori_loop(0, TABLE // UNROLL, step, jnp.int32(0))


def left_kernel(meta_ref, m_ref, g_ref, b_ref, keep_ref, send_ref, acc, table, start):
    t = pl.program_id(0)
    core, tp, seed = meta_ref[0], meta_ref[1], lax.rem(meta_ref[2], PRIME)

    @pl.when(t == 0)
    def _():
        build_table(table)

    window = lax.rem(lax.rem(INVERSE * (seed >> 8), PRIME) * 256 + INVERSE * (seed & 255), PRIME)
    window += lax.rem(tp * (ROW * 3584 % PRIME), PRIME) + lax.rem(t * (ROW * TILE % PRIME), PRIME)
    window = lax.rem(window, PRIME)
    lanes = lax.broadcasted_iota(jnp.int32, (8, 128), 1)
    for i in range(0, TILE, 16):
        groups = []
        for _ in range(2):
            part, whole = window & 127, window >> 7
            turned = [pltpu.roll(table[whole + k], (128 - part) & 127, 1) for k in range(5)]
            first = lanes < 128 - part
            groups.append([jnp.where(first, turned[k], turned[k + 1]) for k in range(4)])
            window = wrap(window + ROW * 8 % PRIME)
        for k in range(4):
            rows = jnp.concatenate([groups[0][k], groups[1][k]], axis=0)
            start[i : i + 16, k * 128 : (k + 1) * 128] = rows.astype(BF16)
    b = (m_ref[...].astype(F32) + g_ref[...].astype(F32)).astype(BF16)
    b_ref[...] = b
    part = dot(b, start[...], 1, 0)

    @pl.when(t == 0)
    def _():
        acc[...] = part

    @pl.when(t == pl.num_programs(0) - 1)
    def _():
        acc[...] += part
        keep_ref[...] = acc[pl.ds(pl.multiple_of(core * HALF, HALF), HALF), :]
        send_ref[...] = acc[pl.ds(pl.multiple_of((1 - core) * HALF, HALF), HALF), :]


def left_partial(meta, momentum, gradient):
    rows, cols = momentum.shape
    half = jax.ShapeDtypeStruct((HALF, RANK), F32)
    whole = pl.BlockSpec((HALF, RANK), lambda t: (0, 0))
    tile = pl.BlockSpec((rows, TILE), lambda t: (0, t))
    return pl.pallas_call(
        left_kernel,
        grid=(2,),
        out_shape=(jax.ShapeDtypeStruct((rows, cols), BF16), half, half),
        in_specs=[smem_spec(), tile, tile],
        out_specs=(tile, whole, whole),
        scratch_shapes=[
            pltpu.VMEM((rows, RANK), F32),
            pltpu.VMEM((TABLE, 8, 128), F32),
            pltpu.VMEM((TILE, RANK), BF16),
        ],
        compiler_params=params(VMEM_MOST),
        name="left_partial",
    )(meta, momentum, gradient)


GRAM_SHARE = (((0, 512, 0, 128), (128, 256, 128, 256)), ((256, 512, 128, 384), (384, 512, 384, 512)))


def gram_blocks(core):
    return [
        (i, j)
        for r0, r1, c0, c1 in GRAM_SHARE[core]
        for i in range(r0, r1, NB)
        for j in range(c0, c1, NB)
    ]


def gram_kernel(meta_ref, mine_ref, other_ref, out_ref):
    for core in range(2):

        @pl.when(meta_ref[0] == core)
        def _():
            k = 0
            for r0, r1, c0, c1 in GRAM_SHARE[core]:
                g = product(mine_ref[:, r0:r1], mine_ref[:, c0:c1], 0, 0) + product(
                    other_ref[:, r0:r1], other_ref[:, c0:c1], 0, 0
                )
                for i in range(0, r1 - r0, NB):
                    for j in range(0, c1 - c0, NB):
                        out_ref[k * NB : (k + 1) * NB, :] = g[i : i + NB, j : j + NB]
                        k += 1


def gram_share(meta, mine, other):
    return pl.pallas_call(
        gram_kernel,
        out_shape=jax.ShapeDtypeStruct((5 * NB, NB), F32),
        in_specs=[smem_spec(), vmem_spec(), vmem_spec()],
        out_specs=vmem_spec(),
        compiler_params=params(),
        name="gram_share",
    )(meta, mine, other)


def right_kernel(meta_ref, b_ref, mine_ref, other_ref, out_ref, split):
    terms = split.shape[1] // RANK

    @pl.when(pl.program_id(0) == 0)
    def _():
        core = meta_ref[0]
        for ref, place in ((mine_ref, core), (other_ref, 1 - core)):
            rows = pl.ds(pl.multiple_of(place * HALF, HALF), HALF)
            for k, term in enumerate(two_terms(ref[...])[:terms]):
                split[rows, k * RANK : (k + 1) * RANK] = term

    w = dot(b_ref[...], split[...], 0, 0)
    out_ref[...] = sum(w[:, k * RANK : (k + 1) * RANK] for k in range(terms)).astype(out_ref.dtype)


def right_partial(meta, blended, mine, other, steps):
    rows, cols = blended.shape
    block = cols // steps
    whole = pl.BlockSpec((HALF, RANK), lambda r: (0, 0))
    terms = 1 if mine.dtype == BF16 else 2
    return pl.pallas_call(
        right_kernel,
        grid=(steps,),
        in_specs=[smem_spec(), pl.BlockSpec((rows, block), lambda r: (0, r)), whole, whole],
        out_specs=pl.BlockSpec((block, RANK), lambda r: (r, 0)),
        scratch_shapes=[pltpu.VMEM((RANK, terms * RANK), BF16)],
        out_shape=jax.ShapeDtypeStruct((cols, RANK), mine.dtype),
        compiler_params=params(VMEM_RIGHT),
        name="right_partial",
    )(meta, blended, mine, other)


def invert_block(ae):
    for top in range(0, NB, PANEL):
        end = top + PANEL
        for k0 in range(top, end, STRIP):
            n = end - k0
            rows = lax.broadcasted_iota(jnp.int32, (n, NB), 0)
            left, right = ae[k0:end, :NB], ae[k0:end, NB:]
            columns = [jnp.broadcast_to(left[:, k0 + c : k0 + c + 1], (n, NB)) for c in range(STRIP)]
            scales = []
            for k in range(STRIP):
                pivot = columns[k][k : k + 1, :]
                scales.append(lax.rsqrt(pivot))
                factor = jnp.where(rows > k, columns[k] * (1.0 / pivot), 0.0)
                for c in range(k + 1, STRIP):
                    columns[c] = columns[c] - factor * columns[c][k : k + 1, :]
                left = left - factor * left[k : k + 1, :]
                right = right - factor * right[k : k + 1, :]
            scale = jnp.concatenate(scales, axis=0)
            ae[k0 : k0 + STRIP, :NB] = left[:STRIP] * scale
            ae[k0 : k0 + STRIP, NB:] = right[:STRIP] * scale
            if n > STRIP:
                ae[k0 + STRIP : end, :NB] = left[STRIP:]
                ae[k0 + STRIP : end, NB:] = right[STRIP:]
        if end < NB:
            done = ae[top:end, :]
            ae[end:, :] = ae[end:, :] - exact(done[:, :NB], done, 0, 0)[end:]


def inverse_kernel(meta_ref, mine_ref, other_ref, out_ref, loss_ref, a, ae, diagonal):
    for core in range(2):
        for share, ref in ((core, mine_ref), (1 - core, other_ref)):

            @pl.when(meta_ref[0] == core)
            def _():
                for k, (i, j) in enumerate(gram_blocks(share)):
                    a[i : i + NB, j : j + NB] = ref[k * NB : (k + 1) * NB, :]

    big = lambda d: lax.broadcasted_iota(jnp.int32, (RANK, RANK), d)
    small = lambda d: lax.broadcasted_iota(jnp.int32, (NB, NB), d)
    out_ref[...] = jnp.where(big(0) == big(1), 1.0, 0.0)
    for lo in range(0, RANK, NB):
        hi = lo + NB
        on = jnp.where(small(0) == small(1), a[lo:hi, lo:hi], 0.0)
        diagonal[:, lo:hi] = jnp.sum(on, axis=0, keepdims=True)

    def block(b, carry):
        diag = pl.ds(pl.multiple_of(b * NB, NB), NB)
        ae[:, :NB] = a[diag, diag]
        ae[:, NB:] = jnp.where(small(0) == small(1), 1.0, 0.0)
        invert_block(ae)
        for k in range(RANK // NB):

            @pl.when(b == k)
            def _():
                lo, hi = k * NB, (k + 1) * NB
                inverse = jnp.where(small(0) >= small(1), ae[:, NB:], 0.0)
                done = exact(inverse, out_ref[lo:hi, :hi], 1, 0)
                out_ref[lo:hi, :hi] = done
                if hi < RANK:
                    below = exact(a[hi:, lo:hi], inverse, 1, 1)
                    a[hi:, hi:] = a[hi:, hi:] - exact(below, below, 1, 1)
                    out_ref[hi:, :hi] = out_ref[hi:, :hi] - exact(below, done, 1, 0)

        return carry

    lax.fori_loop(0, RANK // NB, block, 0)
    out = out_ref[...]
    loss_ref[0, 0] = jnp.max(jnp.sum(out * out * diagonal[...], axis=1, keepdims=True))


def inverse_factor(meta, mine, other):
    return pl.pallas_call(
        inverse_kernel,
        out_shape=(
            jax.ShapeDtypeStruct((RANK, RANK), F32),
            jax.ShapeDtypeStruct((1, 1), F32),
        ),
        in_specs=[smem_spec(), vmem_spec(), vmem_spec()],
        out_specs=(vmem_spec(), smem_spec()),
        scratch_shapes=[
            pltpu.VMEM((RANK, RANK), F32),
            pltpu.VMEM((NB, 2 * NB), F32),
            pltpu.VMEM((1, RANK), F32),
        ],
        compiler_params=params(),
        cost_estimate=pl.CostEstimate(flops=0, bytes_accessed=70_000_000, transcendentals=0),
        name="inverse_factor",
    )(meta, mine, other)


def solve(a, inv_ref):
    if a.dtype == BF16:
        top, rest = two_terms(inv_ref[...])
        return (dot(a, top, 1, 1) + dot(a, rest, 1, 1)).astype(BF16)
    return exact(a, inv_ref[...], 1, 1).astype(BF16)


def solve_kernel(w_ref, inv_ref, out_ref):
    out_ref[...] = solve(w_ref[...], inv_ref)


def solve_rows(w, inverse):
    return pl.pallas_call(
        solve_kernel,
        out_shape=jax.ShapeDtypeStruct(w.shape, BF16),
        in_specs=[vmem_spec()] * 2,
        out_specs=vmem_spec(),
        compiler_params=params(),
        name="solve_rows",
    )(w, inverse)


def ortho_kernel(meta_ref, mine_ref, other_ref, inv_ref, out_ref):
    for ref, place in ((mine_ref, meta_ref[0]), (other_ref, 1 - meta_ref[0])):
        rows = pl.ds(pl.multiple_of(place * HALF, HALF), HALF)
        out_ref[rows, :] = solve(ref[...], inv_ref)


def ortho_left(meta, mine, other, inverse):
    return pl.pallas_call(
        ortho_kernel,
        out_shape=jax.ShapeDtypeStruct((RANK, RANK), BF16),
        in_specs=[smem_spec()] + [vmem_spec()] * 3,
        out_specs=vmem_spec(),
        compiler_params=params(),
        name="ortho_left",
    )(meta, mine, other, inverse)


def apply_both(b, q, scaled, right):
    feedback = dot(q, right, 1, 1)
    return (b.astype(F32) - 0.05 * feedback).astype(BF16), dot(scaled, right, 1, 1).astype(BF16)


def apply_kernel(meta_ref, b_ref, q_ref, sums_ref, swapped_ref, *refs):
    rights, (m_ref, u_ref, scaled_ref) = refs[:3], refs[3:]
    i, j = pl.program_id(0), pl.program_id(1)

    @pl.when((i == 0) & (j == 0))
    def _():
        sums = sums_ref[0:1, :] + swapped_ref[0:1, :]
        scale = lax.rsqrt(sums + 1e-6) * math.sqrt(D * F / RANK)
        scaled_ref[...] = (q_ref[...].astype(F32) * scale).astype(BF16)

    tile = m_ref.shape[0]
    rows = pl.ds(pl.multiple_of(j * tile, tile), tile)
    for k in range(3):

        @pl.when(i == k)
        def _():
            m_ref[...], u_ref[...] = apply_both(
                b_ref[...], q_ref[rows, :], scaled_ref[rows, :], rights[k][...]
            )


def apply_three(meta, blended, q, sums, rights):
    rows, cols = blended.shape

    tiles = 1

    def place(i, j, meta_ref):
        offset = jnp.where(i == 0, 0, jnp.where(i == 1, 3, 1))
        return (j, (meta_ref[3] + offset) % 4)

    here = pl.BlockSpec((rows // tiles, cols // 4), place)
    whole = lambda a: pl.BlockSpec(a.shape, lambda i, j, meta_ref: (0, 0))
    shape = jax.ShapeDtypeStruct((rows, cols), BF16)
    square = jax.ShapeDtypeStruct((rows, RANK), BF16)
    rest = [q] + sums + rights
    return pl.pallas_call(
        apply_kernel,
        grid_spec=pltpu.PrefetchScalarGridSpec(
            num_scalar_prefetch=1,
            grid=(3, tiles),
            in_specs=[here] + [whole(a) for a in rest],
            out_specs=[here, here, whole(square)],
        ),
        out_shape=[shape, shape, square],
        compiler_params=params(),
        name="apply_three",
    )(meta, blended, *rest)


def last_kernel(meta_ref, b_ref, q_ref, scaled_ref, a_ref, c_ref, m_in, u_in, m_ref, u_ref):
    q, scaled = q_ref[...], scaled_ref[...]
    feedback = dot(q[:, :HALF], a_ref[...], 1, 1) + dot(q[:, HALF:], c_ref[...], 1, 1)
    direction = dot(scaled[:, :HALF], a_ref[...], 1, 1) + dot(scaled[:, HALF:], c_ref[...], 1, 1)
    m_ref[...] = (b_ref[...].astype(F32) - 0.05 * feedback).astype(BF16)
    u_ref[...] = direction.astype(BF16)


def apply_last(meta, blended, q, scaled, rights, outs):
    rows, cols = blended.shape
    tiles = 1
    here = pl.BlockSpec(
        (rows // tiles, cols // 4), lambda i, meta_ref: (i, (meta_ref[3] + 2) % 4)
    )
    part = pl.BlockSpec((rows // tiles, RANK), lambda i, meta_ref: (i, 0))
    whole = pl.BlockSpec((cols // 4, HALF), lambda i, meta_ref: (0, 0))
    kept = pl.BlockSpec(memory_space=pl.ANY)
    shape = jax.ShapeDtypeStruct((rows, cols), BF16)
    return pl.pallas_call(
        last_kernel,
        grid_spec=pltpu.PrefetchScalarGridSpec(
            num_scalar_prefetch=1,
            grid=(tiles,),
            in_specs=[here, part, part, whole, whole, kept, kept],
            out_specs=[here, here],
        ),
        out_shape=[shape, shape],
        input_output_aliases={6: 0, 7: 1},
        compiler_params=params(),
        name="apply_last",
    )(meta, blended, q, scaled, *rights, *outs)


def sums_kernel(r_ref, out_ref):
    r = r_ref[...].astype(F32)
    out_ref[...] = jnp.broadcast_to(jnp.sum(r * r, axis=0, keepdims=True), out_ref.shape)


def block_sums(r):
    return pl.pallas_call(
        sums_kernel,
        out_shape=jax.ShapeDtypeStruct((8, RANK), F32),
        in_specs=[vmem_spec()],
        out_specs=vmem_spec(),
        compiler_params=params(),
        name="block_sums",
    )(r)


def per_device(momentum, gradient, seed_value):
    fsdp, tp = lax.axis_index("fsdp"), lax.axis_index("tp")
    core, x, y = tp % 2, fsdp % 4, fsdp // 4
    first, second = jnp.where(core == 0, x, y), jnp.where(core == 0, y, x)
    meta = jnp.stack([core, tp, seed_value[0], first, second]).astype(jnp.int32)

    blended, keep, send = left_partial(meta, momentum, gradient)
    half = keep + swap_cores(send)
    piece, rounded = sum_piece(exchange(half, "tp", Z_GROUPS))

    def gram_sum(mine, other):
        gram = exchange(gram_share(meta, mine, other), "fsdp")
        return exchange(sum_parts(gram, 16, 16), "fsdp")

    def careful():
        mine = exchange(jnp.tile(piece, (4, 1)), "tp", Z_GROUPS)
        other = swap_cores(mine)
        gram = gram_sum(mine, other)
        inverse, _ = inverse_factor(meta, gram, swap_cores(gram))
        w = right_partial(meta, blended, mine, other, 4)
        w = scatter(scatter(w, FIRST_GROUPS), SECOND_GROUPS)
        return solve_rows(w, inverse), ortho_left(meta, mine, other, inverse)

    mine = exchange(rounded, "tp", Z_GROUPS)
    other = swap_cores(mine)
    w = right_partial(meta, blended, mine, other, 2)
    mine, other, w = lax.optimization_barrier((mine, other, w))
    w = scatter(w, FIRST_GROUPS)
    gram = gram_sum(mine, other)
    w, gram = lax.optimization_barrier((w, gram))
    w = scatter(w, SECOND_GROUPS)
    inverse, loss = inverse_factor(meta, gram, swap_cores(gram))
    q = ortho_left(meta, mine, other, inverse)
    w, inverse, loss, q = lax.optimization_barrier((w, inverse, loss, q))
    block, q = lax.cond(
        loss.reshape(()) <= LOSS_MAX**2, lambda: (solve_rows(w, inverse), q), careful
    )
    right = exchange(jnp.tile(block, (4, 1)), AXES, SECOND_GROUPS)
    right_low = send_first(right, 1)
    right_high = send_first(right, -1)
    sums = block_sums(right)
    sums = sums + sum(shift_z(sums, k) for k in (1, 2, 3))
    parts = [sums] + [send_first(sums, k) for k in (1, 2, 3)]
    right_low, right_high, *parts = lax.optimization_barrier((right_low, right_high, *parts))
    far_a = send_first(right_low[:, :HALF], 1)
    far_b = send_first(right_high[:, HALF:], -1)
    sums = sum(parts)
    sums = [sums, swap_cores(sums)]
    *outs, scaled = apply_three(meta, blended, q, sums, [right, right_low, right_high])
    return tuple(apply_last(meta, blended, q, scaled, [far_a, far_b], outs))


def solution(mesh):
    return jax.shard_map(
        per_device,
        mesh=mesh,
        in_specs=(P("fsdp", "tp"), P("fsdp", "tp"), P()),
        out_specs=(P("fsdp", "tp"), P("fsdp", "tp")),
        check_vma=False,
    )
```

```python
import functools
import math

import jax
import jax.numpy as jnp
from jax import lax
from jax.experimental import pallas as pl
from jax.experimental.pallas import tpu as pltpu
from jax.sharding import PartitionSpec as P

D = 8192
F = 28672
RANK = 512
HALF = RANK // 2
PRIME = 65521
NB = 128
PANEL = 64
STRIP = 16
VMEM_LIMIT = 48 * 1024 * 1024
VMEM_MOST = 57 * 1024 * 1024
VMEM_RIGHT = 52 * 1024 * 1024
F32, BF16 = jnp.float32, jnp.bfloat16
AXES = ("fsdp", "tp")
LOSS_MAX = 2.0


def flat(y, x, z, core):
    return (y * 4 + x) * 8 + z * 2 + core


def everyone():
    return [(y, x, z, c) for y in range(4) for x in range(4) for z in range(4) for c in range(2)]


def shift(along_first, step):
    pairs = []
    for y, x, z, c in everyone():
        if (c == 0) == along_first:
            to = (y, (x + step) % 4, z, c)
        else:
            to = ((y + step) % 4, x, z, c)
        pairs.append((flat(y, x, z, c), flat(*to)))
    return pairs


def send_first(a, step):
    return lax.ppermute(a, AXES, shift(True, step))


def send_second(a, step):
    return lax.ppermute(a, AXES, shift(False, step))


def swap_cores(a):
    return lax.ppermute(a, "tp", [(i, i ^ 1) for i in range(8)])


def shift_z(a, step):
    return lax.ppermute(a, "tp", [(i, (i + 2 * step) % 8) for i in range(8)])


Z_GROUPS = [[c, 2 + c, 4 + c, 6 + c] for c in range(2)]
SECOND_GROUPS = [[flat(y, x, z, 0) for y in range(4)] for x in range(4) for z in range(4)] + [
    [flat(y, x, z, 1) for x in range(4)] for y in range(4) for z in range(4)
]
FIRST_GROUPS = [[flat(y, x, z, 0) for x in range(4)] for y in range(4) for z in range(4)] + [
    [flat(y, x, z, 1) for y in range(4)] for x in range(4) for z in range(4)
]


def exchange(a, axis, groups=None):
    return lax.all_to_all(a, axis, 0, 0, axis_index_groups=groups, tiled=True)


def vmem_spec():
    return pl.BlockSpec(memory_space=pltpu.VMEM)


def smem_spec():
    return pl.BlockSpec(memory_space=pltpu.SMEM)


def params(limit=VMEM_LIMIT):
    return pltpu.CompilerParams(vmem_limit_bytes=limit)


def scatter(a, groups):
    return lax.psum_scatter(
        a, AXES, scatter_dimension=0, axis_index_groups=groups, tiled=True
    )


def sum_kernel(n, copies, a_ref, out_ref):
    rows = a_ref.shape[0] // n
    total = a_ref[:rows, :]
    for k in range(1, n):
        total = total + a_ref[k * rows : (k + 1) * rows, :]
    for k in range(copies):
        out_ref[k * rows : (k + 1) * rows, :] = total


def piece_kernel(a_ref, out_ref, rounded_ref):
    sum_kernel(4, 1, a_ref, out_ref)
    for k in range(4):
        rows = out_ref.shape[0]
        rounded_ref[k * rows : (k + 1) * rows, :] = out_ref[...].astype(BF16)


def sum_piece(a):
    rows, cols = a.shape
    return pl.pallas_call(
        piece_kernel,
        out_shape=(
            jax.ShapeDtypeStruct((rows // 4, cols), F32),
            jax.ShapeDtypeStruct((rows, cols), BF16),
        ),
        in_specs=[vmem_spec()],
        out_specs=(vmem_spec(), vmem_spec()),
        compiler_params=params(),
        name="sum_piece",
    )(a)


def sum_parts(a, n, copies):
    rows, cols = a.shape
    return pl.pallas_call(
        functools.partial(sum_kernel, n, copies),
        out_shape=jax.ShapeDtypeStruct((rows // n * copies, cols), a.dtype),
        in_specs=[vmem_spec()],
        out_specs=vmem_spec(),
        compiler_params=params(),
        name="sum_parts",
    )(a)


def dot(a, b, ca, cb, precision=None):
    return lax.dot_general(
        a, b, (((ca,), (cb,)), ((), ())), precision=precision, preferred_element_type=F32
    )


def exact(a, b, ca, cb):
    return dot(a, b, ca, cb, lax.Precision.HIGHEST)


def two_terms(a):
    top = a.astype(BF16)
    return top, (a.astype(F32) - top.astype(F32)).astype(BF16)


def product(a, b, ca, cb):
    return dot(a, b, ca, cb) if a.dtype == BF16 else exact(a, b, ca, cb)


def fold(v):
    return v - (v >> 16) * PRIME


def wrap(v):
    return jnp.where(v >= PRIME, v - PRIME, v)


def start_value(a):
    low = a & 32767
    low = wrap(fold(fold(low * low + 7))) & 32767
    third = fold(low * low + a).astype(F32)
    third = third - jnp.floor(third * (1.0 / PRIME) + 0.5 / PRIME) * PRIME
    scale = math.sqrt(12.0 / F)
    return third * (scale / PRIME) - 0.5 * scale


INVERSE = pow(9973, -1, PRIME)
ROW = INVERSE * 40503 % PRIME
TABLE = 520
UNROLL = 8
TILE = 1792


def build_table(table):
    rows = lax.broadcasted_iota(jnp.int32, (8, 128), 0)
    cols = lax.broadcasted_iota(jnp.int32, (8, 128), 1)
    base = wrap(fold(fold(cols * 9973 + rows * 40503)))

    def step(i, offset):
        for k in range(UNROLL):
            table[i * UNROLL + k] = start_value(wrap(base + offset))
            offset = wrap(offset + 9973 * 128 % PRIME)
        return offset

    lax.fori_loop(0, TABLE // UNROLL, step, jnp.int32(0))


def left_kernel(meta_ref, m_ref, g_ref, b_ref, keep_ref, send_ref, acc, table, start):
    t = pl.program_id(0)
    core, tp, seed = meta_ref[0], meta_ref[1], lax.rem(meta_ref[2], PRIME)

    @pl.when(t == 0)
    def _():
        build_table(table)

    window = lax.rem(lax.rem(INVERSE * (seed >> 8), PRIME) * 256 + INVERSE * (seed & 255), PRIME)
    window += lax.rem(tp * (ROW * 3584 % PRIME), PRIME) + lax.rem(t * (ROW * TILE % PRIME), PRIME)
    window = lax.rem(window, PRIME)
    lanes = lax.broadcasted_iota(jnp.int32, (8, 128), 1)
    for i in range(0, TILE, 16):
        groups = []
        for _ in range(2):
            part, whole = window & 127, window >> 7
            turned = [pltpu.roll(table[whole + k], (128 - part) & 127, 1) for k in range(5)]
            first = lanes < 128 - part
            groups.append([jnp.where(first, turned[k], turned[k + 1]) for k in range(4)])
            window = wrap(window + ROW * 8 % PRIME)
        for k in range(4):
            rows = jnp.concatenate([groups[0][k], groups[1][k]], axis=0)
            start[i : i + 16, k * 128 : (k + 1) * 128] = rows.astype(BF16)
    b = (m_ref[...].astype(F32) + g_ref[...].astype(F32)).astype(BF16)
    b_ref[...] = b
    part = dot(b, start[...], 1, 0)

    @pl.when(t == 0)
    def _():
        acc[...] = part

    @pl.when(t == pl.num_programs(0) - 1)
    def _():
        acc[...] += part
        keep_ref[...] = acc[pl.ds(pl.multiple_of(core * HALF, HALF), HALF), :]
        send_ref[...] = acc[pl.ds(pl.multiple_of((1 - core) * HALF, HALF), HALF), :]


def left_partial(meta, momentum, gradient):
    rows, cols = momentum.shape
    half = jax.ShapeDtypeStruct((HALF, RANK), F32)
    whole = pl.BlockSpec((HALF, RANK), lambda t: (0, 0))
    tile = pl.BlockSpec((rows, TILE), lambda t: (0, t))
    return pl.pallas_call(
        left_kernel,
        grid=(2,),
        out_shape=(jax.ShapeDtypeStruct((rows, cols), BF16), half, half),
        in_specs=[smem_spec(), tile, tile],
        out_specs=(tile, whole, whole),
        scratch_shapes=[
            pltpu.VMEM((rows, RANK), F32),
            pltpu.VMEM((TABLE, 8, 128), F32),
            pltpu.VMEM((TILE, RANK), BF16),
        ],
        compiler_params=params(VMEM_MOST),
        name="left_partial",
    )(meta, momentum, gradient)


GRAM_SHARE = (((0, 512, 0, 128), (128, 256, 128, 256)), ((256, 512, 128, 384), (384, 512, 384, 512)))


def gram_blocks(core):
    return [
        (i, j)
        for r0, r1, c0, c1 in GRAM_SHARE[core]
        for i in range(r0, r1, NB)
        for j in range(c0, c1, NB)
    ]


def gram_kernel(meta_ref, mine_ref, other_ref, out_ref):
    for core in range(2):

        @pl.when(meta_ref[0] == core)
        def _():
            k = 0
            for r0, r1, c0, c1 in GRAM_SHARE[core]:
                g = product(mine_ref[:, r0:r1], mine_ref[:, c0:c1], 0, 0) + product(
                    other_ref[:, r0:r1], other_ref[:, c0:c1], 0, 0
                )
                for i in range(0, r1 - r0, NB):
                    for j in range(0, c1 - c0, NB):
                        out_ref[k * NB : (k + 1) * NB, :] = g[i : i + NB, j : j + NB]
                        k += 1


def gram_share(meta, mine, other):
    return pl.pallas_call(
        gram_kernel,
        out_shape=jax.ShapeDtypeStruct((5 * NB, NB), F32),
        in_specs=[smem_spec(), vmem_spec(), vmem_spec()],
        out_specs=vmem_spec(),
        compiler_params=params(),
        name="gram_share",
    )(meta, mine, other)


def right_kernel(meta_ref, b_ref, mine_ref, other_ref, out_ref, split):
    terms = split.shape[1] // RANK

    @pl.when(pl.program_id(0) == 0)
    def _():
        core = meta_ref[0]
        for ref, place in ((mine_ref, core), (other_ref, 1 - core)):
            rows = pl.ds(pl.multiple_of(place * HALF, HALF), HALF)
            for k, term in enumerate(two_terms(ref[...])[:terms]):
                split[rows, k * RANK : (k + 1) * RANK] = term

    w = dot(b_ref[...], split[...], 0, 0)
    out_ref[...] = sum(w[:, k * RANK : (k + 1) * RANK] for k in range(terms)).astype(out_ref.dtype)


def right_partial(meta, blended, mine, other, steps):
    rows, cols = blended.shape
    block = cols // steps
    whole = pl.BlockSpec((HALF, RANK), lambda r: (0, 0))
    terms = 1 if mine.dtype == BF16 else 2
    return pl.pallas_call(
        right_kernel,
        grid=(steps,),
        in_specs=[smem_spec(), pl.BlockSpec((rows, block), lambda r: (0, r)), whole, whole],
        out_specs=pl.BlockSpec((block, RANK), lambda r: (r, 0)),
        scratch_shapes=[pltpu.VMEM((RANK, terms * RANK), BF16)],
        out_shape=jax.ShapeDtypeStruct((cols, RANK), mine.dtype),
        compiler_params=params(VMEM_RIGHT),
        name="right_partial",
    )(meta, blended, mine, other)


def invert_block(ae):
    for top in range(0, NB, PANEL):
        end = top + PANEL
        for k0 in range(top, end, STRIP):
            n = end - k0
            rows = lax.broadcasted_iota(jnp.int32, (n, NB), 0)
            left, right = ae[k0:end, :NB], ae[k0:end, NB:]
            columns = [jnp.broadcast_to(left[:, k0 + c : k0 + c + 1], (n, NB)) for c in range(STRIP)]
            scales = []
            for k in range(STRIP):
                pivot = columns[k][k : k + 1, :]
                scales.append(lax.rsqrt(pivot))
                factor = jnp.where(rows > k, columns[k] * (1.0 / pivot), 0.0)
                for c in range(k + 1, STRIP):
                    columns[c] = columns[c] - factor * columns[c][k : k + 1, :]
                left = left - factor * left[k : k + 1, :]
                right = right - factor * right[k : k + 1, :]
            scale = jnp.concatenate(scales, axis=0)
            ae[k0 : k0 + STRIP, :NB] = left[:STRIP] * scale
            ae[k0 : k0 + STRIP, NB:] = right[:STRIP] * scale
            if n > STRIP:
                ae[k0 + STRIP : end, :NB] = left[STRIP:]
                ae[k0 + STRIP : end, NB:] = right[STRIP:]
        if end < NB:
            done = ae[top:end, :]
            ae[end:, :] = ae[end:, :] - exact(done[:, :NB], done, 0, 0)[end:]


def inverse_kernel(meta_ref, mine_ref, other_ref, out_ref, loss_ref, a, ae, diagonal):
    for core in range(2):
        for share, ref in ((core, mine_ref), (1 - core, other_ref)):

            @pl.when(meta_ref[0] == core)
            def _():
                for k, (i, j) in enumerate(gram_blocks(share)):
                    a[i : i + NB, j : j + NB] = ref[k * NB : (k + 1) * NB, :]

    big = lambda d: lax.broadcasted_iota(jnp.int32, (RANK, RANK), d)
    small = lambda d: lax.broadcasted_iota(jnp.int32, (NB, NB), d)
    out_ref[...] = jnp.where(big(0) == big(1), 1.0, 0.0)
    for lo in range(0, RANK, NB):
        hi = lo + NB
        on = jnp.where(small(0) == small(1), a[lo:hi, lo:hi], 0.0)
        diagonal[:, lo:hi] = jnp.sum(on, axis=0, keepdims=True)

    def block(b, carry):
        diag = pl.ds(pl.multiple_of(b * NB, NB), NB)
        ae[:, :NB] = a[diag, diag]
        ae[:, NB:] = jnp.where(small(0) == small(1), 1.0, 0.0)
        invert_block(ae)
        for k in range(RANK // NB):

            @pl.when(b == k)
            def _():
                lo, hi = k * NB, (k + 1) * NB
                inverse = jnp.where(small(0) >= small(1), ae[:, NB:], 0.0)
                done = exact(inverse, out_ref[lo:hi, :hi], 1, 0)
                out_ref[lo:hi, :hi] = done
                if hi < RANK:
                    below = exact(a[hi:, lo:hi], inverse, 1, 1)
                    a[hi:, hi:] = a[hi:, hi:] - exact(below, below, 1, 1)
                    out_ref[hi:, :hi] = out_ref[hi:, :hi] - exact(below, done, 1, 0)

        return carry

    lax.fori_loop(0, RANK // NB, block, 0)
    out = out_ref[...]
    loss_ref[0, 0] = jnp.max(jnp.sum(out * out * diagonal[...], axis=1, keepdims=True))


def inverse_factor(meta, mine, other):
    return pl.pallas_call(
        inverse_kernel,
        out_shape=(
            jax.ShapeDtypeStruct((RANK, RANK), F32),
            jax.ShapeDtypeStruct((1, 1), F32),
        ),
        in_specs=[smem_spec(), vmem_spec(), vmem_spec()],
        out_specs=(vmem_spec(), smem_spec()),
        scratch_shapes=[
            pltpu.VMEM((RANK, RANK), F32),
            pltpu.VMEM((NB, 2 * NB), F32),
            pltpu.VMEM((1, RANK), F32),
        ],
        compiler_params=params(),
        cost_estimate=pl.CostEstimate(flops=0, bytes_accessed=70_000_000, transcendentals=0),
        name="inverse_factor",
    )(meta, mine, other)


def solve(a, inv_ref):
    if a.dtype == BF16:
        top, rest = two_terms(inv_ref[...])
        return (dot(a, top, 1, 1) + dot(a, rest, 1, 1)).astype(BF16)
    return exact(a, inv_ref[...], 1, 1).astype(BF16)


def solve_kernel(w_ref, inv_ref, out_ref):
    out_ref[...] = solve(w_ref[...], inv_ref)


def solve_rows(w, inverse):
    return pl.pallas_call(
        solve_kernel,
        out_shape=jax.ShapeDtypeStruct(w.shape, BF16),
        in_specs=[vmem_spec()] * 2,
        out_specs=vmem_spec(),
        compiler_params=params(),
        name="solve_rows",
    )(w, inverse)


def ortho_kernel(meta_ref, mine_ref, other_ref, inv_ref, out_ref):
    for ref, place in ((mine_ref, meta_ref[0]), (other_ref, 1 - meta_ref[0])):
        rows = pl.ds(pl.multiple_of(place * HALF, HALF), HALF)
        out_ref[rows, :] = solve(ref[...], inv_ref)


def ortho_left(meta, mine, other, inverse):
    return pl.pallas_call(
        ortho_kernel,
        out_shape=jax.ShapeDtypeStruct((RANK, RANK), BF16),
        in_specs=[smem_spec()] + [vmem_spec()] * 3,
        out_specs=vmem_spec(),
        compiler_params=params(),
        name="ortho_left",
    )(meta, mine, other, inverse)


def apply_both(b, q, scaled, right):
    feedback = dot(q, right, 1, 1)
    return (b.astype(F32) - 0.05 * feedback).astype(BF16), dot(scaled, right, 1, 1).astype(BF16)


def apply_kernel(meta_ref, b_ref, q_ref, sums_ref, swapped_ref, *refs):
    rights, (m_ref, u_ref, scaled_ref) = refs[:3], refs[3:]
    i, j = pl.program_id(0), pl.program_id(1)

    @pl.when((i == 0) & (j == 0))
    def _():
        sums = sums_ref[0:1, :] + swapped_ref[0:1, :]
        scale = lax.rsqrt(sums + 1e-6) * math.sqrt(D * F / RANK)
        scaled_ref[...] = (q_ref[...].astype(F32) * scale).astype(BF16)

    tile = m_ref.shape[0]
    rows = pl.ds(pl.multiple_of(j * tile, tile), tile)
    for k in range(3):

        @pl.when(i == k)
        def _():
            m_ref[...], u_ref[...] = apply_both(
                b_ref[...], q_ref[rows, :], scaled_ref[rows, :], rights[k][...]
            )


def apply_three(meta, blended, q, sums, rights):
    rows, cols = blended.shape

    tiles = 1

    def place(i, j, meta_ref):
        offset = jnp.where(i == 0, 0, jnp.where(i == 1, 3, 1))
        return (j, (meta_ref[3] + offset) % 4)

    here = pl.BlockSpec((rows // tiles, cols // 4), place)
    whole = lambda a: pl.BlockSpec(a.shape, lambda i, j, meta_ref: (0, 0))
    shape = jax.ShapeDtypeStruct((rows, cols), BF16)
    square = jax.ShapeDtypeStruct((rows, RANK), BF16)
    rest = [q] + sums + rights
    return pl.pallas_call(
        apply_kernel,
        grid_spec=pltpu.PrefetchScalarGridSpec(
            num_scalar_prefetch=1,
            grid=(3, tiles),
            in_specs=[here] + [whole(a) for a in rest],
            out_specs=[here, here, whole(square)],
        ),
        out_shape=[shape, shape, square],
        compiler_params=params(),
        name="apply_three",
    )(meta, blended, *rest)


def last_kernel(meta_ref, b_ref, q_ref, scaled_ref, a_ref, c_ref, m_in, u_in, m_ref, u_ref):
    q, scaled = q_ref[...], scaled_ref[...]
    feedback = dot(q[:, :HALF], a_ref[...], 1, 1) + dot(q[:, HALF:], c_ref[...], 1, 1)
    direction = dot(scaled[:, :HALF], a_ref[...], 1, 1) + dot(scaled[:, HALF:], c_ref[...], 1, 1)
    m_ref[...] = (b_ref[...].astype(F32) - 0.05 * feedback).astype(BF16)
    u_ref[...] = direction.astype(BF16)


def apply_last(meta, blended, q, scaled, rights, outs):
    rows, cols = blended.shape
    tiles = 1
    here = pl.BlockSpec(
        (rows // tiles, cols // 4), lambda i, meta_ref: (i, (meta_ref[3] + 2) % 4)
    )
    part = pl.BlockSpec((rows // tiles, RANK), lambda i, meta_ref: (i, 0))
    whole = pl.BlockSpec((cols // 4, HALF), lambda i, meta_ref: (0, 0))
    kept = pl.BlockSpec(memory_space=pl.ANY)
    shape = jax.ShapeDtypeStruct((rows, cols), BF16)
    return pl.pallas_call(
        last_kernel,
        grid_spec=pltpu.PrefetchScalarGridSpec(
            num_scalar_prefetch=1,
            grid=(tiles,),
            in_specs=[here, part, part, whole, whole, kept, kept],
            out_specs=[here, here],
        ),
        out_shape=[shape, shape],
        input_output_aliases={6: 0, 7: 1},
        compiler_params=params(),
        name="apply_last",
    )(meta, blended, q, scaled, *rights, *outs)


def sums_kernel(r_ref, out_ref):
    r = r_ref[...].astype(F32)
    out_ref[...] = jnp.broadcast_to(jnp.sum(r * r, axis=0, keepdims=True), out_ref.shape)


def block_sums(r):
    return pl.pallas_call(
        sums_kernel,
        out_shape=jax.ShapeDtypeStruct((8, RANK), F32),
        in_specs=[vmem_spec()],
        out_specs=vmem_spec(),
        compiler_params=params(),
        name="block_sums",
    )(r)


def per_device(momentum, gradient, seed_value):
    fsdp, tp = lax.axis_index("fsdp"), lax.axis_index("tp")
    core, x, y = tp % 2, fsdp % 4, fsdp // 4
    first, second = jnp.where(core == 0, x, y), jnp.where(core == 0, y, x)
    meta = jnp.stack([core, tp, seed_value[0], first, second]).astype(jnp.int32)

    blended, keep, send = left_partial(meta, momentum, gradient)
    half = keep + swap_cores(send)
    piece, rounded = sum_piece(exchange(half, "tp", Z_GROUPS))

    def gram_sum(mine, other):
        gram = exchange(gram_share(meta, mine, other), "fsdp")
        return exchange(sum_parts(gram, 16, 16), "fsdp")

    def careful():
        mine = exchange(jnp.tile(piece, (4, 1)), "tp", Z_GROUPS)
        other = swap_cores(mine)
        gram = gram_sum(mine, other)
        inverse, _ = inverse_factor(meta, gram, swap_cores(gram))
        w = right_partial(meta, blended, mine, other, 4)
        w = scatter(scatter(w, FIRST_GROUPS), SECOND_GROUPS)
        return solve_rows(w, inverse), ortho_left(meta, mine, other, inverse)

    mine = exchange(rounded, "tp", Z_GROUPS)
    other = swap_cores(mine)
    w = right_partial(meta, blended, mine, other, 4)
    mine, other, w = lax.optimization_barrier((mine, other, w))
    w = scatter(w, FIRST_GROUPS)
    gram = gram_sum(mine, other)
    w, gram = lax.optimization_barrier((w, gram))
    w = scatter(w, SECOND_GROUPS)
    inverse, loss = inverse_factor(meta, gram, swap_cores(gram))
    q = ortho_left(meta, mine, other, inverse)
    w, inverse, loss, q = lax.optimization_barrier((w, inverse, loss, q))
    block, q = lax.cond(
        loss.reshape(()) <= LOSS_MAX**2, lambda: (solve_rows(w, inverse), q), careful
    )
    right = exchange(jnp.tile(block, (4, 1)), AXES, SECOND_GROUPS)
    right_low = send_first(right, 1)
    right_high = send_first(right, -1)
    sums = block_sums(right)
    sums = sums + sum(shift_z(sums, k) for k in (1, 2, 3))
    parts = [sums] + [send_first(sums, k) for k in (1, 2, 3)]
    right_low, right_high, *parts = lax.optimization_barrier((right_low, right_high, *parts))
    far_a = send_first(right_low[:, :HALF], 1)
    far_b = send_first(right_high[:, HALF:], -1)
    sums = sum(parts)
    sums = [sums, swap_cores(sums)]
    *outs, scaled = apply_three(meta, blended, q, sums, [right, right_low, right_high])
    return tuple(apply_last(meta, blended, q, scaled, [far_a, far_b], outs))


def solution(mesh):
    return jax.shard_map(
        per_device,
        mesh=mesh,
        in_specs=(P("fsdp", "tp"), P("fsdp", "tp"), P()),
        out_specs=(P("fsdp", "tp"), P("fsdp", "tp")),
        check_vma=False,
    )
```
